32 devices in a mesh: dp: 8 (over y, x, core), ctx: 4 (over z).
Axes of the slice: x: 2, y: 2, z: 4, core: 2. Of those that a mesh axis runs over, the one named last changes fastest.
Arguments:
- tokens: bfloat16 [8, 512, 2048], P('dp', 'ctx'), may hold values from -6 to 6
- segment_ids: int32 [8, 512], P('dp'), may hold values from 0 to 10, as said below
- out_grad: bfloat16 [8, 512, 2048], P('dp', 'ctx'), may hold values from -6 to 6
- gain_attn: bfloat16 [2048], P(('dp', 'ctx')), may hold values from 0.099609375 to 1.8984375
- w_query: bfloat16 [2048, 2048], P(('dp', 'ctx')), may hold values from -0.125 to 0.125
- key_weight: bfloat16 [2048, 256], P(('dp', 'ctx')), may hold values from -0.125 to 0.125
- value_weight: bfloat16 [2048, 256], P(('dp', 'ctx')), may hold values from -0.125 to 0.125
- w_out: bfloat16 [2048, 2048], P(('dp', 'ctx')), may hold values from -1 to 1
- gain_mlp: bfloat16 [2048], P(('dp', 'ctx')), may hold values from 0.099609375 to 1.8984375
- w_gate: bfloat16 [2048, 5632], P(('dp', 'ctx')), may hold values from -0.125 to 0.125
- w_up: bfloat16 [2048, 5632], P(('dp', 'ctx')), may hold values from -0.125 to 0.125
- w_down: bfloat16 [5632, 2048], P(('dp', 'ctx')), may hold values from -0.15625 to 0.15625
Outputs:
- result: bfloat16 [8, 512, 2048], P('dp', 'ctx')
- grad_input: float32 [8, 512, 2048], P('dp', 'ctx')
- grad_gain_attn: float32 [2048], P(('dp', 'ctx'))
- grad_query: float32 [2048, 2048], P(('dp', 'ctx'))
- grad_key: float32 [2048, 256], P(('dp', 'ctx'))
- grad_value: float32 [2048, 256], P(('dp', 'ctx'))
- grad_out: float32 [2048, 2048], P(('dp', 'ctx'))
- grad_gain_mlp: float32 [2048], P(('dp', 'ctx'))
- grad_gate: float32 [2048, 5632], P(('dp', 'ctx'))
- grad_up: float32 [2048, 5632], P(('dp', 'ctx'))
- grad_down: float32 [5632, 2048], P(('dp', 'ctx'))
The draws below stay inside these ranges and needn't reach their ends.
Inputs may be any that keep to these rules, and one draw needn't show every extreme that they name: `segment_ids`: segment numbers start at 0 and rise by one at the first token of each new document; every document but the last of its sequence holds 50 to 500 tokens.
All inputs are finite; a program needn't handle non-finite values.
Results may differ from the reference program's by a relative error of at most 0.015.
Values may be sent and summed in bfloat16 or wider, within the bound.
No kernel may reach another device: no remote copies, remote signals or barrier semaphores. Data moves between devices by JAX's collectives and lax.ppermute only.
A program may use at most 384 MiB of HBM per device.

```python
import jax
import jax.numpy as jnp
from jax import lax

MODEL_WIDTH = 2048
QUERY_HEADS = 32
KEY_VALUE_HEADS = 4
HEAD_SIZE = 64
FF = 5632
TOK_DEV = 128
SEQ_LEN = 512
SEQS = 8


def draw_segment_ids(key, part):
    key = jax.random.fold_in(key, 11)
    shortest = SEQ_LEN * 200 // 2048
    longest = SEQ_LEN * 2000 // 2048
    number = (SEQ_LEN - 1) // shortest + 1
    index = jnp.arange(SEQ_LEN, dtype=jnp.int32)
    key_pick, key_cut, key_rest = jax.random.split(key, 3)
    chosen = jax.random.randint(key_pick, (), 0, SEQS)

    def regular(seq_key):
        lengths = jax.random.randint(seq_key, (number,), shortest, longest + 1)
        bounds = jnp.cumsum(lengths)
        return jnp.sum((bounds[None, :] <= index[:, None]).astype(jnp.int32), axis=1)
    ids = jax.vmap(regular)(jax.random.split(key_rest, SEQS))
    cut = jax.random.randint(key_cut, (), max(SEQ_LEN - longest, 1), TOK_DEV)
    spanning = (index >= SEQ_LEN - cut).astype(jnp.int32)
    finest = index // shortest
    row_index = jnp.arange(SEQS, dtype=jnp.int32)
    ids = jnp.where((row_index == chosen)[:, None], spanning[None, :], ids)
    ids = jnp.where((row_index == (chosen + 1) % SEQS)[:, None], finest[None, :], ids)
    return ids


def levels(rng, dims, shards, smallest, largest):
    gain, own = 1.0, jax.random.fold_in(rng, 6)
    for dim, shards_of in shards:
        draws = jnp.exp(jax.random.uniform(jax.random.fold_in(own, dim), (shards_of,), jnp.float32, smallest / len(shards), largest / len(shards)))
        gain = gain * jnp.repeat(draws, dims[dim] // shards_of).reshape([-1 if axis == dim else 1 for axis in range(len(dims))])
    return gain


def centred(key, dims, scale, reach, pieces=(), kind=jnp.bfloat16):
    drawn = scale * jax.random.normal(key, dims, jnp.float32)
    if pieces:
        drawn = drawn * levels(key, dims, pieces, -0.22, 0.18)
    return jnp.clip(drawn, -reach, reach).astype(kind)


def setup_inputs(seed: int = 0) -> dict:
    seeds = jax.random.split(jax.random.key(seed), 13)
    return {
        "tokens": centred(seeds[0], (SEQS, SEQ_LEN, MODEL_WIDTH), 1.0, 6.0, ((0, 8), (1, 4))),
        "segment_ids": draw_segment_ids(jax.random.fold_in(seeds[12], 71), 0),
        "out_grad": centred(seeds[2], (SEQS, SEQ_LEN, MODEL_WIDTH), 1.0, 6.0, ((0, 8), (1, 4))),
        "gain_attn": jnp.clip(1.0 + 0.18 * jax.random.normal(seeds[3], (MODEL_WIDTH,), jnp.float32), 0.099609375, 1.8984375).astype(jnp.bfloat16),
        "w_query": centred(seeds[4], (MODEL_WIDTH, QUERY_HEADS * HEAD_SIZE), MODEL_WIDTH ** -0.5, 0.125, ((0, 32),)),
        "key_weight": centred(seeds[5], (MODEL_WIDTH, KEY_VALUE_HEADS * HEAD_SIZE), MODEL_WIDTH ** -0.5, 0.125, ((0, 32),)),
        "value_weight": centred(seeds[6], (MODEL_WIDTH, KEY_VALUE_HEADS * HEAD_SIZE), MODEL_WIDTH ** -0.5, 0.125, ((0, 32),)),
        "w_out": centred(seeds[7], (QUERY_HEADS * HEAD_SIZE, MODEL_WIDTH), (max(QUERY_HEADS * HEAD_SIZE * 8 // SEQ_LEN, 1)) ** -0.5, 1.0, ((0, 32),)),
        "gain_mlp": jnp.clip(1.0 + 0.18 * jax.random.normal(seeds[8], (MODEL_WIDTH,), jnp.float32), 0.099609375, 1.8984375).astype(jnp.bfloat16),
        "w_gate": centred(seeds[9], (MODEL_WIDTH, FF), MODEL_WIDTH ** -0.5, 0.125, ((0, 32),)),
        "w_up": centred(seeds[10], (MODEL_WIDTH, FF), MODEL_WIDTH ** -0.5, 0.125, ((0, 32),)),
        "w_down": centred(seeds[11], (FF, MODEL_WIDTH), (FF // 4) ** -0.5, 0.15625, ((0, 32),)),
    }


@jax.custom_vjp
def reduced_precision(v):
    return lax.optimization_barrier(v.astype(jnp.bfloat16)).astype(jnp.float32)

@jax.custom_vjp
def reduced_backward(v):
    return v

def low_keep(v):
    return (reduced_precision(v), None)

def low_pass(kept, grad):
    return (grad,)

def back_keep(v):
    return (v, None)

def back_low(kept, grad):
    return (reduced_precision(grad),)
reduced_precision.defvjp(low_keep, low_pass)
reduced_backward.defvjp(back_keep, back_low)
EPS = 1e-05
NEG = -1e+30
HIGH = lax.Precision.HIGHEST

def matrix_product(left, right):
    return jnp.dot(left, right, precision=HIGH)

def apply_rotary(value_rows, cosine_table, sine_table):
    half = value_rows.shape[-1] // 2
    first = value_rows[..., :half]
    second = value_rows[..., half:]
    return jnp.concatenate([first * cosine_table - second * sine_table, second * cosine_table + first * sine_table], axis=-1)

def layer(inputs, gain_attn, w_query, key_weight, value_weight, w_out, gain_mlp, w_gate, w_up, w_down, segs):
    span_length = inputs.shape[0]
    head_group = QUERY_HEADS // KEY_VALUE_HEADS
    scale = HEAD_SIZE ** (-0.5)
    index = jnp.arange(span_length, dtype=jnp.int32)
    before = lax.optimization_barrier(jnp.sum((segs[None, :] < segs[:, None]).astype(jnp.int32), axis=1))
    place = (index - before).astype(jnp.float32)
    freq = 10000.0 ** (-jnp.arange(HEAD_SIZE // 2, dtype=jnp.float32) / (HEAD_SIZE // 2))
    angle = place[:, None] * freq[None, :]
    cosine_table = jnp.cos(angle)[:, None, :]
    sine_table = jnp.sin(angle)[:, None, :]
    allowed = (index[None, :] <= index[:, None]) & (segs[None, :] == segs[:, None])
    normed = inputs * lax.rsqrt(lax.optimization_barrier(jnp.mean(inputs * inputs, axis=-1, keepdims=True)) + EPS)
    first_input_rows = reduced_precision(normed * gain_attn)
    query_vector = reduced_backward(matrix_product(first_input_rows, w_query)).reshape(span_length, QUERY_HEADS, HEAD_SIZE)
    key = reduced_backward(matrix_product(first_input_rows, key_weight)).reshape(span_length, KEY_VALUE_HEADS, HEAD_SIZE)
    value_vector = reduced_precision(reduced_backward(matrix_product(first_input_rows, value_weight))).reshape(span_length, KEY_VALUE_HEADS, HEAD_SIZE)
    query_vector = reduced_precision(apply_rotary(query_vector, cosine_table, sine_table))
    key = reduced_precision(apply_rotary(key, cosine_table, sine_table))
    query_rows = query_vector.reshape(span_length, KEY_VALUE_HEADS, head_group, HEAD_SIZE).transpose(1, 2, 0, 3)
    key_rows = key.transpose(1, 0, 2)
    value_rows = value_vector.transpose(1, 0, 2)

    def head(args):
        qg, kg, vg = args
        scores = reduced_backward(jnp.einsum('gsd,jd->gsj', qg, kg, precision=HIGH) * scale)
        scores = jnp.where(allowed[None], scores, NEG)
        top = lax.optimization_barrier(jnp.max(scores, axis=-1, keepdims=True))
        expo = jnp.exp(scores - top)
        probs = expo / lax.optimization_barrier(jnp.sum(expo, axis=-1, keepdims=True))
        return jnp.einsum('gsj,jd->gsd', reduced_precision(probs), vg, precision=HIGH)
    mixed = lax.map(jax.checkpoint(head), (query_rows, key_rows, value_rows))
    attn_in = reduced_precision(reduced_backward(mixed.transpose(2, 0, 1, 3).reshape(span_length, QUERY_HEADS * HEAD_SIZE)))
    resid = inputs + reduced_backward(matrix_product(attn_in, w_out))
    normed2 = resid * lax.rsqrt(lax.optimization_barrier(jnp.mean(resid * resid, axis=-1, keepdims=True)) + EPS)
    second_in = reduced_precision(normed2 * gain_mlp)
    gate = reduced_backward(matrix_product(second_in, w_gate))
    up = reduced_backward(matrix_product(second_in, w_up))
    hidden = reduced_precision(jax.nn.silu(gate) * up)
    return resid + reduced_backward(matrix_product(hidden, w_down))

def reference(tokens, segment_ids, out_grad, gain_attn, w_query, key_weight, value_weight, w_out, gain_mlp, w_gate, w_up, w_down):
    weights = tuple((w.astype(jnp.float32) for w in (gain_attn, w_query, key_weight, value_weight, w_out, gain_mlp, w_gate, w_up, w_down)))

    def one(totals, item):
        inputs, segs, cotangent = item

        def forward(xin, *params):
            return layer(xin, *params, segs)
        output, pull = jax.vjp(forward, inputs.astype(jnp.float32), *weights)
        grads = pull(cotangent.astype(jnp.float32))
        new_totals = tuple((a + b for a, b in zip(totals, grads[1:])))
        return (new_totals, (output.astype(jnp.bfloat16), grads[0]))
    zeros = tuple((jnp.zeros_like(w) for w in weights))
    totals, (outputs, grad_input) = lax.scan(one, zeros, (tokens, segment_ids, out_grad))
    return (outputs, grad_input, totals[0], totals[1], totals[2], totals[3], totals[4], totals[5], totals[6], totals[7], totals[8])
```

```python
import functools

import jax
import jax.numpy as jnp
from jax import lax
from jax.sharding import PartitionSpec as P

QUERY_HEADS = 32
KEY_VALUE_HEADS = 4
HEAD_SIZE = 64
EPS = 1e-05
NEG = -1e30
F32 = jnp.float32
BF16 = jnp.bfloat16


def rotate(values, cosine, sine):
    half = values.shape[-1] // 2
    first, second = values[..., :half], values[..., half:]
    return jnp.concatenate(
        [first * cosine - second * sine, second * cosine + first * sine], axis=-1
    )


def dot(left, right):
    return jnp.dot(left, right, preferred_element_type=F32)


def dot_nt(left, right):
    return lax.dot_general(left, right, (((1,), (1,)), ((), ())), preferred_element_type=F32)


def dot_tn(left, right):
    return lax.dot_general(left, right, (((0,), (0,)), ((), ())), preferred_element_type=F32)


def swap(value, bit, size):
    return lax.ppermute(value, "dp", [(i, i ^ bit) for i in range(size)])


def swap_cores(value, size):
    paired = value.reshape(size // 2, 2, *value.shape[1:])
    return swap(paired[:, ::-1].reshape(value.shape), 1, size)


def row_parts(rows, parts):
    units = rows // 16
    edges = [units * j // parts * 16 for j in range(parts)] + [rows]
    return [(edges[j], edges[j + 1]) for j in range(parts)]


def gather_dp(rows, size):
    bits = [1 << j for j in range(1, size.bit_length() - 1)]
    cuts = row_parts(rows.shape[0], len(bits))
    held = [{0: rows[a:b]} for a, b in cuts]
    for step in range(len(bits)):
        for j, pieces in enumerate(held):
            bit = bits[(j + step) % len(bits)]
            for rel, piece in list(pieces.items()):
                pieces[rel ^ bit] = swap(piece, bit, size)
    for pieces in held:
        for rel, piece in list(pieces.items()):
            pieces[rel ^ 1] = swap(piece, 1, size)
    return [jnp.concatenate([pieces[rel] for pieces in held]) for rel in range(size)]


def scatter_dp(terms, size):
    bits = [1 << j for j in range(1, size.bit_length() - 1)]
    cuts = row_parts(terms.shape[1], len(bits))

    def add(own, came):
        return own.astype(F32) + came.astype(F32)

    summed = []
    for j, (a, b) in enumerate(cuts):
        acc = {
            rel: add(terms[rel, a:b], swap(terms[rel ^ 1, a:b], 1, size))
            for rel in range(0, size, 2)
        }
        for step in reversed(range(len(bits))):
            bit = bits[(j + step) % len(bits)]
            acc = {
                rel: add(acc[rel], swap(acc[rel ^ bit].astype(BF16), bit, size))
                for rel in acc
                if not rel & bit
            }
        summed.append(acc[0])
    return jnp.concatenate(summed)


def norm_back(grad_in, normed, inverse, gain):
    grad_normed = grad_in * gain
    return inverse * (
        grad_normed - normed * jnp.mean(grad_normed * normed, axis=-1, keepdims=True)
    )


def per_device(
    n,
    c,
    tokens,
    segment_ids,
    out_grad,
    gain_attn,
    w_query,
    key_weight,
    value_weight,
    w_out,
    gain_mlp,
    w_gate,
    w_up,
    w_down,
):
    t, width = tokens.shape[1:]
    length = segment_ids.shape[1]
    block = w_query.shape[0]
    ff = w_gate.shape[1]
    heads = QUERY_HEADS // n
    group = QUERY_HEADS // KEY_VALUE_HEADS
    q_cols, f_cols = heads * HEAD_SIZE, ff // n
    scale = HEAD_SIZE**-0.5
    me, place_z = lax.axis_index("dp"), lax.axis_index("ctx")
    core = me % 2

    def to_block_order(v):
        return v.reshape(t, n, c, block).transpose(0, 2, 1, 3).reshape(t, width)

    def from_block_order(v):
        return v.reshape(t, c, n, block).transpose(0, 2, 1, 3).reshape(t, width)

    pieces = []
    for d in range(n):
        g = d * heads // group
        kv = value_weight if d % 2 else key_weight
        pieces.append(
            jnp.concatenate(
                [
                    w_query[:, d * q_cols : (d + 1) * q_cols],
                    kv[:, g * HEAD_SIZE : (g + 1) * HEAD_SIZE],
                ],
                axis=1,
            )
        )
    w_attn = lax.all_to_all(jnp.stack(pieces), "dp", 0, 0).reshape(n * block, -1)
    w_attn = lax.all_gather(w_attn, "ctx", axis=0, tiled=True)
    wo = lax.all_gather(w_out, "ctx", axis=0, tiled=True)
    w_pair = jnp.concatenate(
        [w_gate.reshape(block, n, f_cols), w_up.reshape(block, n, f_cols)], axis=2
    ).transpose(1, 0, 2)
    w_pair = lax.all_to_all(w_pair, "dp", 0, 0).reshape(n * block, 2 * f_cols)
    w_pair = lax.all_gather(w_pair, "ctx", axis=0, tiled=True)
    wd = lax.all_gather(w_down, "ctx", axis=0, tiled=True)
    gains = lax.all_gather(
        jnp.stack([gain_attn, gain_mlp]), ("ctx", "dp"), axis=1, tiled=True
    ).astype(F32)
    gain1, gain2 = gains[0], gains[1]
    gain2_plain = gain2.reshape(c, n, block).transpose(1, 0, 2).reshape(width)

    segs = segment_ids
    for bit in [1 << j for j in range(n.bit_length() - 1)]:
        segs = jnp.concatenate([segs, swap(segs, bit, n)])
    local_idx = place_z * t + jnp.arange(t, dtype=jnp.int32)
    local_seg = lax.dynamic_slice_in_dim(segs, place_z * t, t, axis=1)
    before = jnp.sum((segs[:, None, :] < local_seg[:, :, None]).astype(jnp.int32), axis=2)
    place = (local_idx[None] - before).astype(F32)
    freq = 10000.0 ** (-jnp.arange(HEAD_SIZE // 2, dtype=F32) / (HEAD_SIZE // 2))
    angle = place.reshape(n * t)[:, None] * freq[None, :]
    cosine, sine = jnp.cos(angle), jnp.sin(angle)
    kv_cosine = jnp.where(core == 0, cosine, 1.0)
    kv_sine = jnp.where(core == 0, sine, 0.0)
    key_idx = (place_z * t + jnp.arange(length, dtype=jnp.int32)) % length
    key_seg = lax.dynamic_slice_in_dim(
        jnp.concatenate([segs, segs], axis=1), place_z * t, length, axis=1
    )
    allowed = (key_idx[None, None, :] <= local_idx[None, :, None]) & (
        key_seg[:, None, :] == local_seg[:, :, None]
    )

    rows = jnp.concatenate(gather_dp(to_block_order(tokens[0]), n)).astype(F32)
    inverse1 = lax.rsqrt(jnp.mean(rows * rows, axis=-1, keepdims=True) + EPS)
    first_in = (rows * inverse1 * gain1).astype(BF16)
    projected = dot(first_in, w_attn)
    queries = rotate(
        projected[:, :q_cols].reshape(n * t, heads, HEAD_SIZE), cosine[:, None], sine[:, None]
    ).astype(BF16)
    queries = queries.reshape(n, t, heads, HEAD_SIZE).transpose(0, 2, 1, 3)
    kv_own = rotate(projected[:, q_cols:], kv_cosine, kv_sine).astype(BF16).reshape(n, t, -1)
    kv_all = [kv_own] + [
        lax.ppermute(kv_own, "ctx", [(i, (i - j) % c) for i in range(c)]) for j in range(1, c)
    ]
    kv_all = jnp.concatenate(kv_all, axis=1)
    kv_other = swap_cores(kv_all, n)
    keys = jnp.where(core == 0, kv_all, kv_other)
    values = jnp.where(core == 0, kv_other, kv_all)

    scores = jnp.einsum("nhtd,nld->nhtl", queries, keys, preferred_element_type=F32) * scale
    scores = jnp.where(allowed[:, None], scores, NEG)
    top = jnp.max(scores, axis=-1, keepdims=True)
    expo = jnp.exp(scores - top)
    total = jnp.sum(expo, axis=-1, keepdims=True)
    probs = (expo / total).astype(BF16)
    logsum = top + jnp.log(total)
    mixed = jnp.einsum("nhtl,nld->nhtd", probs, values, preferred_element_type=F32)
    mixed = mixed.transpose(0, 2, 1, 3).reshape(n * t, q_cols).astype(BF16)
    x = tokens[0].astype(F32)
    resid = x + scatter_dp(dot(mixed, wo).astype(BF16).reshape(n, t, width), n)

    inverse2 = lax.rsqrt(jnp.mean(resid * resid, axis=-1, keepdims=True) + EPS)
    normed2 = resid * inverse2
    second_in = (normed2 * gain2_plain).astype(BF16)
    second_in = jnp.concatenate(gather_dp(to_block_order(second_in), n))
    dy_local = out_grad[0]
    dy = jnp.concatenate(gather_dp(dy_local, n))
    both = dot(second_in, w_pair)
    gate, up = both[:, :f_cols], both[:, f_cols:]
    sig = jax.nn.sigmoid(gate)
    swish = gate * sig
    hidden = (swish * up).astype(BF16)
    grad_hidden = dot_nt(dy, wd)
    grad_pair = jnp.concatenate(
        [
            (grad_hidden * up * sig * (1.0 + gate * (1.0 - sig))).astype(BF16),
            (grad_hidden * swish).astype(BF16),
        ],
        axis=1,
    )
    grad_second = from_block_order(
        scatter_dp(dot_nt(grad_pair, w_pair).astype(BF16).reshape(n, t, width), n)
    )
    result = resid + scatter_dp(dot(hidden, wd).astype(BF16).reshape(n, t, width), n)
    grad_down = lax.psum_scatter(
        dot_tn(hidden, dy).astype(BF16), "ctx", scatter_dimension=0, tiled=True
    )
    pair_sum = lax.psum_scatter(
        dot_tn(second_in, grad_pair).astype(BF16), "ctx", scatter_dimension=0, tiled=True
    )
    pair_sum = lax.all_to_all(pair_sum.reshape(n, block, 2 * f_cols), "dp", 0, 0).astype(F32)
    grad_gate = pair_sum[:, :, :f_cols].transpose(1, 0, 2).reshape(block, ff)
    grad_up = pair_sum[:, :, f_cols:].transpose(1, 0, 2).reshape(block, ff)
    grad_gain_mlp = jnp.sum(
        w_gate.astype(F32) * grad_gate + w_up.astype(F32) * grad_up, axis=1
    ) / gain_mlp.astype(F32)

    grad_resid = dy_local.astype(F32) + norm_back(grad_second, normed2, inverse2, gain2_plain)
    grad_branch = jnp.concatenate(gather_dp(grad_resid.astype(BF16), n))
    grad_wout = lax.psum_scatter(
        dot_tn(mixed, grad_branch).astype(BF16), "ctx", scatter_dimension=0, tiled=True
    )
    grad_mixed = dot_nt(grad_branch, wo).astype(BF16)
    grad_mixed = grad_mixed.reshape(n, t, heads, HEAD_SIZE).transpose(0, 2, 1, 3)
    probs = jnp.exp(scores - logsum)
    grad_values = jnp.einsum(
        "nhtl,nhtd->nld", probs.astype(BF16), grad_mixed, preferred_element_type=F32
    )
    grad_probs = jnp.einsum("nhtd,nld->nhtl", grad_mixed, values, preferred_element_type=F32)
    inner = jnp.sum(probs * grad_probs, axis=-1, keepdims=True)
    grad_scores = (probs * (grad_probs - inner)).astype(BF16)
    grad_q = jnp.einsum("nhtl,nld->nthd", grad_scores, keys, preferred_element_type=F32) * scale
    grad_keys = (
        jnp.einsum("nhtl,nhtd->nld", grad_scores, queries, preferred_element_type=F32) * scale
    )
    grad_q = rotate(
        grad_q.reshape(n * t, heads, HEAD_SIZE), cosine[:, None], -sine[:, None]
    ).reshape(n * t, q_cols)
    kept = jnp.where(core == 0, grad_keys, grad_values)
    sent = jnp.where(core == 0, grad_values, grad_keys)
    grad_kv = (kept + swap_cores(sent, n)).reshape(n, c, t, HEAD_SIZE)
    total_kv = grad_kv[:, 0]
    for j in range(1, c):
        total_kv = total_kv + lax.ppermute(
            grad_kv[:, j].astype(BF16), "ctx", [(i, (i + j) % c) for i in range(c)]
        ).astype(F32)
    grad_kv = rotate(total_kv.reshape(n * t, HEAD_SIZE), kv_cosine, -kv_sine)
    grad_attn = jnp.concatenate([grad_q, grad_kv], axis=1).astype(BF16)
    grad_first = scatter_dp(dot_nt(grad_attn, w_attn).astype(BF16).reshape(n, t, width), n)
    attn_sum = lax.psum_scatter(
        dot_tn(first_in, grad_attn).astype(BF16), "ctx", scatter_dimension=0, tiled=True
    )
    attn_sum = lax.all_to_all(attn_sum.reshape(n, block, -1), "dp", 0, 0).astype(F32)
    grad_query = attn_sum[:, :, :q_cols].transpose(1, 0, 2).reshape(block, -1)
    kv_sum = attn_sum[:, :, q_cols:].reshape(KEY_VALUE_HEADS, -1, 2, block, HEAD_SIZE).sum(axis=1)
    grad_key = kv_sum[:, 0].transpose(1, 0, 2).reshape(block, -1)
    grad_value = kv_sum[:, 1].transpose(1, 0, 2).reshape(block, -1)
    grad_gain_attn = (
        jnp.sum(w_query.astype(F32) * grad_query, axis=1)
        + jnp.sum(key_weight.astype(F32) * grad_key, axis=1)
        + jnp.sum(value_weight.astype(F32) * grad_value, axis=1)
    ) / gain_attn.astype(F32)
    grad_input = grad_resid + from_block_order(
        norm_back(grad_first, (rows * inverse1)[:t], inverse1[:t], gain1)
    )
    return (
        result.astype(BF16)[None],
        grad_input[None],
        grad_gain_attn,
        grad_query,
        grad_key,
        grad_value,
        grad_wout.astype(F32),
        grad_gain_mlp,
        grad_gate,
        grad_up,
        grad_down.astype(F32),
    )


def solution(mesh):
    n, c = mesh.shape["dp"], mesh.shape["ctx"]
    rows = P("dp", "ctx", None)
    weight, gain = P(("dp", "ctx"), None), P(("dp", "ctx"))
    return jax.shard_map(
        functools.partial(per_device, n, c),
        mesh=mesh,
        in_specs=(rows, P("dp", None), rows, gain, weight, weight, weight, weight, gain)
        + (weight,) * 3,
        out_specs=(rows, rows, gain, weight, weight, weight, weight, gain) + (weight,) * 3,
        check_vma=False,
    )
```

```python
import functools

import jax
import jax.numpy as jnp
from jax import lax
from jax.experimental import pallas as pl
from jax.experimental.pallas import tpu as pltpu
from jax.sharding import Mesh
from jax.sharding import PartitionSpec as P

QUERY_HEADS = 32
KEY_VALUE_HEADS = 4
HEAD_SIZE = 64
EPS = 1e-05
NEG = -1e30
F32 = jnp.float32
BF16 = jnp.bfloat16


def dot(left, right):
    return jnp.dot(left, right, preferred_element_type=F32)


def dot_nt(left, right):
    return lax.dot_general(left, right, (((1,), (1,)), ((), ())), preferred_element_type=F32)


def dot_tn(left, right):
    return lax.dot_general(left, right, (((0,), (0,)), ((), ())), preferred_element_type=F32)


def swap(value, rel):
    size = lax.axis_size(("plane", "core"))
    return lax.ppermute(value, ("plane", "core"), [(i, i ^ rel) for i in range(size)])


def shift(value, step, size):
    return lax.ppermute(value, "ctx", [(i, (i - step) % size) for i in range(size)])


def shifts(value, size):
    return [shift(value, j, size) for j in range(1, size)]


def together(*values):
    return lax.optimization_barrier(values)


def after(value, *earlier):
    return together(value, *earlier)[0]


def dp_same(rows, size):
    return [swap(rows, rel) for rel in range(2, size, 2)]


def kernel_params(mib=48):
    return pltpu.CompilerParams(vmem_limit_bytes=mib * 2**20)

LIGHT = pl.CostEstimate(flops=1024, bytes_accessed=1024, transcendentals=0)


def transposed_dot(lefts, rights):
    tokens, rows = lefts[0].shape
    columns, count = rights[0].shape[1], len(lefts)
    by_rows = rows % 256 == 0 and rows > columns
    row_tile = 256 if by_rows else rows
    column_tile = columns if by_rows or columns % 512 else 512
    moving = pl.BlockSpec((tokens, row_tile if by_rows else column_tile), lambda i: (0, i))
    resting = pl.BlockSpec((tokens, column_tile if by_rows else row_tile), lambda i: (0, 0))

    def body(*refs):
        total = 0.0
        for left, right in zip(refs[:count], refs[count:-1]):
            total += lax.dot_general(
                left[...], right[...], (((0,), (0,)), ((), ())), preferred_element_type=F32
            )
        refs[-1][...] = total.astype(BF16)

    return pl.pallas_call(
        body,
        grid=(rows // row_tile if by_rows else columns // column_tile,),
        in_specs=[moving if by_rows else resting] * count + [resting if by_rows else moving] * count,
        out_specs=pl.BlockSpec(
            (row_tile, column_tile), (lambda i: (i, 0)) if by_rows else (lambda i: (0, i))
        ),
        out_shape=jax.ShapeDtypeStruct((rows, columns), BF16),
        compiler_params=kernel_params(),
        cost_estimate=LIGHT,
    )(*lefts, *rights)


def turn(values, cosine, sine):
    half = HEAD_SIZE // 2
    width = values.shape[1]
    lane = lax.broadcasted_iota(jnp.int32, values.shape, 1)
    up = jnp.concatenate([values[:, half:], values[:, :half]], axis=1)
    down = jnp.concatenate([values[:, width - half :], values[:, : width - half]], axis=1)
    return values * cosine + jnp.where(lane % HEAD_SIZE < half, up, down) * sine


def widen(table, columns):
    return jnp.concatenate([table] * (columns // table.shape[1]), axis=1)


def pack(rows):
    half = rows.shape[0] // 2
    return jnp.concatenate([rows[:half], rows[half:]], axis=1)


def unpack(rows):
    half = rows.shape[1] // 2
    return jnp.concatenate([rows[:, :half], rows[:, half:]], axis=0)


def project(where, even, odd, gain, weights, cosine, sine, q_cols, part):
    half, width = even.shape
    columns = q_cols + HEAD_SIZE
    tile = 256
    steps = half // tile

    def body(at, e, o, gn, w, cs, sn, first, queries, kv):
        x = jnp.where(pl.program_id(0) < steps, e[...], o[...]).astype(F32)
        normed = x * lax.rsqrt(jnp.mean(x * x, axis=-1, keepdims=True) + EPS)
        rows = (normed * gn[...]).astype(BF16)
        first[...] = rows
        raw = dot(rows, w[...])
        queries[...] = turn(
            raw[:, :q_cols], widen(cs[...], q_cols), widen(sn[...], q_cols)
        ).astype(BF16)
        plain = raw[:, q_cols:columns]
        turned = turn(plain, cs[:, :HEAD_SIZE], sn[:, :HEAD_SIZE])
        chosen = jnp.where(at[1] == 0, turned, plain)
        for p in range(tile // part):
            kv[p] = pack(chosen[p * part : (p + 1) * part]).astype(BF16)

    def rows(size):
        return pl.BlockSpec((tile, size), lambda i: (i, 0))

    return pl.pallas_call(
        body,
        grid=(2 * steps,),
        in_specs=[
            pl.BlockSpec(memory_space=pltpu.SMEM),
            pl.BlockSpec((tile, width), lambda i: (jnp.minimum(i, steps - 1), 0)),
            pl.BlockSpec((tile, width), lambda i: (jnp.maximum(i - steps, 0), 0)),
            pl.BlockSpec((1, width), lambda i: (0, 0)),
            pl.BlockSpec(weights.shape, lambda i: (0, 0)),
            rows(cosine.shape[1]),
            rows(cosine.shape[1]),
        ],
        out_specs=(
            rows(width),
            rows(q_cols),
            pl.BlockSpec((tile // part, part // 2, 2 * HEAD_SIZE), lambda i: (i, 0, 0)),
        ),
        out_shape=(
            jax.ShapeDtypeStruct((2 * half, width), BF16),
            jax.ShapeDtypeStruct((2 * half, q_cols), BF16),
            jax.ShapeDtypeStruct((2 * half // part, part // 2, 2 * HEAD_SIZE), BF16),
        ),
        compiler_params=kernel_params(),
        cost_estimate=LIGHT,
    )(where, even, odd, gain, weights, cosine, sine)


def stacked(values, heads):
    return jnp.concatenate(
        [values[:, h * HEAD_SIZE : (h + 1) * HEAD_SIZE] for h in range(heads)], axis=0
    )


def side_by_side(values, heads):
    rows = values.shape[0] // heads
    return jnp.concatenate([values[h * rows : (h + 1) * rows] for h in range(heads)], axis=1)


def probabilities(queries, keys, mine, theirs, place, parts, heads):
    rows, length = queries.shape[0] // heads, keys.shape[0]
    part = length // parts
    scores = dot_nt(queries, keys) * HEAD_SIZE**-0.5
    query_at = place * part + lax.broadcasted_iota(jnp.int32, (rows, length), 0)
    key_at = place * part + lax.broadcasted_iota(jnp.int32, (rows, length), 1)
    key_at = jnp.where(key_at >= length, key_at - length, key_at)
    allowed = (key_at <= query_at) & (mine == theirs)
    allowed = jnp.concatenate([allowed] * heads, axis=0)
    scores = jnp.where(allowed, scores, NEG)
    expo = jnp.exp(scores - jnp.max(scores, axis=-1, keepdims=True))
    return expo / jnp.sum(expo, axis=-1, keepdims=True)


def sequence_specs(sequences, part, parts):
    half = sequences // 2
    shape = (1, part // 2, 2 * HEAD_SIZE)
    own = pl.BlockSpec(shape, lambda i: (i, 0, 0))
    came = pl.BlockSpec(shape, lambda i: (lax.rem(i + half, sequences), 0, 0))
    return [own] * parts + [came] * parts


def keys_values(first, refs):
    parts = len(refs) // 2
    own, came = (
        jnp.concatenate([unpack(ref[0]) for ref in half], axis=0) for half in (refs[:parts], refs[parts:])
    )
    return jnp.where(first, own, came), jnp.where(first, came, own)


def attend(where, queries, own, came, mine, theirs):
    parts = len(own)
    sequences, part = own[0].shape[0], 2 * own[0].shape[1]
    rows, columns = queries.shape[0] // sequences, queries.shape[1]
    heads = columns // HEAD_SIZE

    def body(at, q, m, th, *refs):
        keys, values = keys_values(at[1] == 0, refs[:-1])
        probs = probabilities(stacked(q[...], heads), keys, m[0], th[0], at[0], parts, heads)
        refs[-1][...] = side_by_side(dot(probs.astype(BF16), values), heads).astype(BF16)

    return pl.pallas_call(
        body,
        grid=(sequences,),
        in_specs=[
            pl.BlockSpec(memory_space=pltpu.SMEM),
            pl.BlockSpec((rows, columns), lambda i: (i, 0)),
            pl.BlockSpec((1, rows, 1), lambda i: (i, 0, 0)),
            pl.BlockSpec((1, 1, parts * part), lambda i: (i, 0, 0)),
            *sequence_specs(sequences, part, parts),
        ],
        out_specs=pl.BlockSpec((rows, columns), lambda i: (i, 0)),
        out_shape=jax.ShapeDtypeStruct(queries.shape, BF16),
        compiler_params=kernel_params(),
        cost_estimate=LIGHT,
    )(where, queries, mine, theirs, *own, *came)


def attend_back(where, same, other, w_out, queries, own, came, mine, theirs, cosine, sine):
    parts = len(own)
    sequences, part = own[0].shape[0], 2 * own[0].shape[1]
    length = parts * part
    rows, columns = queries.shape[0] // sequences, queries.shape[1]
    heads, half, width = columns // HEAD_SIZE, sequences // 2, same.shape[1]
    packed = parts, part // 2, 2 * HEAD_SIZE
    scale = HEAD_SIZE**-0.5

    def body(at, s, o, w, q, m, th, cs, sn, *refs):
        dq, down, dcame = refs[-3:]
        first = at[1] == 0
        keys, values = keys_values(first, refs[:-3])
        branch = jnp.where(pl.program_id(0) < half, s[...], o[...])
        mixed = stacked(dot_nt(branch, w[...]).astype(BF16), heads)
        stack = stacked(q[...], heads)
        probs = probabilities(stack, keys, m[0], th[0], at[0], parts, heads)
        grad = dot_nt(mixed, values)
        inner = jnp.sum(probs * grad, axis=-1, keepdims=True)
        scores = (probs * (grad - inner)).astype(BF16)
        grad_q = side_by_side(dot(scores, keys) * scale, heads)
        dq[...] = turn(grad_q, widen(cs[...], columns), -widen(sn[...], columns)).astype(BF16)
        grad_k = dot_tn(scores, stack) * scale
        grad_v = dot_tn(probs.astype(BF16), mixed)
        kept, sent = jnp.where(first, grad_k, grad_v), jnp.where(first, grad_v, grad_k)
        for j in range(parts):
            at_rows = slice(j * part, (j + 1) * part)
            down[0, j] = pack(kept[at_rows])
            dcame[0, j] = pack(sent[at_rows]).astype(BF16)

    def strip(size):
        return pl.BlockSpec((rows, size), lambda i: (i, 0))

    return pl.pallas_call(
        body,
        grid=(sequences,),
        in_specs=[
            pl.BlockSpec(memory_space=pltpu.SMEM),
            pl.BlockSpec((rows, width), lambda i: (jnp.minimum(i, half - 1), 0)),
            pl.BlockSpec((rows, width), lambda i: (jnp.maximum(i - half, 0), 0)),
            pl.BlockSpec(w_out.shape, lambda i: (0, 0)),
            strip(columns),
            pl.BlockSpec((1, rows, 1), lambda i: (i, 0, 0)),
            pl.BlockSpec((1, 1, length), lambda i: (i, 0, 0)),
            strip(cosine.shape[1]),
            strip(cosine.shape[1]),
            *sequence_specs(sequences, part, parts),
        ],
        out_specs=(
            strip(columns),
            pl.BlockSpec((1, *packed), lambda i: (i, 0, 0, 0)),
            pl.BlockSpec((1, *packed), lambda i: (lax.rem(i + half, sequences), 0, 0, 0)),
        ),
        out_shape=(
            jax.ShapeDtypeStruct(queries.shape, BF16),
            jax.ShapeDtypeStruct((sequences, *packed), F32),
            jax.ShapeDtypeStruct((sequences, *packed), BF16),
        ),
        compiler_params=kernel_params(),
        cost_estimate=LIGHT,
    )(where, same, other, w_out, queries, mine, theirs, cosine, sine, *own, *came)


def add_parts(kept, came):
    sequences, parts, rows, columns = kept.shape

    def body(a, b, *outs):
        for j, out in enumerate(outs):
            out[...] = (a[:, j] + b[:, j].astype(F32)).astype(out.dtype)

    return pl.pallas_call(
        body,
        out_shape=[
            jax.ShapeDtypeStruct((sequences, rows, columns), BF16 if j else F32)
            for j in range(parts)
        ],
        compiler_params=kernel_params(),
        cost_estimate=LIGHT,
    )(kept, came)


def sum_keys(where, own, came, cosine, sine):
    sequences, rows, _ = own.shape
    count = len(came)

    def body(at, a, cs, sn, *refs):
        total = a[...]
        for ref in refs[:count]:
            total += ref[...].astype(F32)
        out = refs[count]
        for i in range(sequences):
            at_rows = slice(2 * i * rows, 2 * (i + 1) * rows)
            plain = unpack(total[i])
            turned = turn(plain, cs[at_rows, :HEAD_SIZE], -sn[at_rows, :HEAD_SIZE])
            out[at_rows, :] = jnp.where(at[1] == 0, turned, plain).astype(BF16)

    whole = pl.BlockSpec(memory_space=pltpu.VMEM)
    return pl.pallas_call(
        body,
        in_specs=[pl.BlockSpec(memory_space=pltpu.SMEM)] + [whole] * (3 + count),
        out_shape=jax.ShapeDtypeStruct((2 * sequences * rows, HEAD_SIZE), BF16),
        compiler_params=kernel_params(),
        cost_estimate=LIGHT,
    )(where, own, cosine, sine, *came)


def attention_weight_terms(where, first_in, grad_attn, mixed, grad_branch, used, members, parts):
    tokens, width = first_in.shape
    columns, half = mixed.shape[1], mixed.shape[0] // 2
    block, strip = width // (members * parts), width // members
    lanes = used + strip + -(used + strip) % 128

    def body(at, x, g, m, ba, bb, *refs):
        outs, (left, right) = refs[:parts], refs[parts:]
        left[...] = dot_tn(x[...], g[:, : left.shape[1]])
        right[...] = dot_tn(m[:half, :], ba[...]) + dot_tn(m[half:, :], bb[...])
        unused = jnp.zeros((block, lanes - used - strip), F32)
        for j, out in enumerate(outs):
            place = lax.rem(at[0] + j, parts)
            own = right[pl.ds(pl.multiple_of(place * block, block), block), :]
            for d in range(members):
                rows = pl.ds(pl.multiple_of((d * parts + place) * block, block), block)
                out[d * block : (d + 1) * block, :] = jnp.concatenate(
                    [left[rows, :][:, :used], own[:, d * strip : (d + 1) * strip], unused], axis=1
                ).astype(BF16)

    whole = pl.BlockSpec(memory_space=pltpu.VMEM)
    return pl.pallas_call(
        body,
        in_specs=[pl.BlockSpec(memory_space=pltpu.SMEM)] + [whole] * 5,
        out_shape=[jax.ShapeDtypeStruct((members * block, lanes), BF16)] * parts,
        scratch_shapes=[
            pltpu.VMEM((width, grad_attn.shape[1]), F32),
            pltpu.VMEM((columns, width), F32),
        ],
        compiler_params=kernel_params(),
        cost_estimate=LIGHT,
    )(where, first_in, grad_attn, mixed, *grad_branch)


def feed_forward(second_in, grad_hidden, w_pair, w_down):
    tokens, width = second_in.shape
    ff = w_down.shape[0]
    tile = 512

    def body(x, dh, w, wd, hidden, grads, back, forth):
        both = dot(x[...], w[...])
        gate, up = both[:, :ff], both[:, ff:]
        sig = jax.nn.sigmoid(gate)
        swish = gate * sig
        inner = (swish * up).astype(BF16)
        hidden[...] = inner
        forth[...] = dot(inner, wd[...]).astype(BF16)
        dh_sig = dh[...] * sig
        grad = jnp.concatenate(
            [dh_sig * up * (1.0 + gate * (1.0 - sig)), dh_sig * gate], axis=1
        ).astype(BF16)
        grads[...] = grad
        back[...] = dot_nt(grad, w[...]).astype(BF16)

    def rows(columns):
        return pl.BlockSpec((tile, columns), lambda i: (i, 0))

    def whole(array):
        return pl.BlockSpec(array.shape, lambda i: (0, 0))

    return pl.pallas_call(
        body,
        grid=(tokens // tile,),
        in_specs=[rows(width), rows(ff), whole(w_pair), whole(w_down)],
        out_specs=(rows(ff), rows(2 * ff), rows(width), rows(width)),
        out_shape=(
            jax.ShapeDtypeStruct((tokens, ff), BF16),
            jax.ShapeDtypeStruct((tokens, 2 * ff), BF16),
            jax.ShapeDtypeStruct((tokens, width), BF16),
            jax.ShapeDtypeStruct((tokens, width), BF16),
        ),
        compiler_params=kernel_params(),
        cost_estimate=LIGHT,
    )(second_in, grad_hidden, w_pair, w_down)


def add_blocks(own, came, blocks):
    tokens, columns = own.shape[0] // blocks, own.shape[1]

    def body(a, b, *outs):
        for j, out in enumerate(outs):
            rows = pl.ds(j * tokens, tokens)
            out[...] = (a[rows, :].astype(F32) + b[rows, :].astype(F32)).astype(out.dtype)

    return pl.pallas_call(
        body,
        out_shape=[
            jax.ShapeDtypeStruct((tokens, columns), BF16 if j else F32) for j in range(blocks)
        ],
        compiler_params=kernel_params(),
        cost_estimate=LIGHT,
    )(own, came)


def regroup(values, outer, inner):
    part = values.shape[1] // (outer * inner)
    return jnp.concatenate(
        [
            values[:, (o * inner + i) * part : (o * inner + i + 1) * part]
            for i in range(inner)
            for o in range(outer)
        ],
        axis=1,
    )


def second_norm(x, own, sent, gain, outer, inner):
    count = len(sent)

    def body(x, own, gain, *refs):
        resid = x[...].astype(F32) + own[...]
        for ref in refs[:count]:
            resid += ref[...].astype(F32)
        refs[count][...] = resid
        normed = resid * lax.rsqrt(jnp.mean(resid * resid, axis=-1, keepdims=True) + EPS)
        refs[count + 1][...] = regroup((normed * gain[...]).astype(BF16), outer, inner)

    return pl.pallas_call(
        body,
        out_shape=(
            jax.ShapeDtypeStruct(x.shape, F32),
            jax.ShapeDtypeStruct(x.shape, BF16),
        ),
        compiler_params=kernel_params(),
        cost_estimate=LIGHT,
    )(x, own, gain, *sent)


def second_norm_back(resid, own, sent, gain, grad_out, outer, inner):
    count = len(sent)

    def body(resid, own, gain, grad_out, *refs):
        grad = own[...]
        for ref in refs[:count]:
            grad += ref[...].astype(F32)
        grad = regroup(grad, inner, outer)
        rows = resid[...]
        inverse = lax.rsqrt(jnp.mean(rows * rows, axis=-1, keepdims=True) + EPS)
        total = grad_out[...].astype(F32) + norm_back(grad, rows * inverse, inverse, gain[...])
        refs[count][...] = total
        refs[count + 1][...] = total.astype(BF16)

    return pl.pallas_call(
        body,
        out_shape=(
            jax.ShapeDtypeStruct(resid.shape, F32),
            jax.ShapeDtypeStruct(resid.shape, BF16),
        ),
        compiler_params=kernel_params(),
        cost_estimate=LIGHT,
    )(resid, own, gain, grad_out, *sent)


def dot_blocks(left, right, came, blocks, product):
    tokens, columns = came.shape[0] // blocks, came.shape[1]

    def body(a, b, c, *outs):
        for j, out in enumerate(outs):
            rows = pl.ds(j * tokens, tokens)
            out[...] = (product(a[rows, :], b[...]) + c[rows, :].astype(F32)).astype(out.dtype)

    return pl.pallas_call(
        body,
        out_shape=[
            jax.ShapeDtypeStruct((tokens, columns), BF16 if j else F32) for j in range(blocks)
        ],
        compiler_params=kernel_params(),
        cost_estimate=LIGHT,
    )(left, right, came)


def columns_out(gate, up, planes, members):
    rows, ff = gate.shape
    part = ff // (planes * members)

    def body(g, u, o):
        both = g[...], u[...]
        for s in range(members):
            o[s] = jnp.concatenate(
                [
                    v[:, (p * members + s) * part : (p * members + s + 1) * part]
                    for v in both
                    for p in range(planes)
                ],
                axis=1,
            )

    return pl.pallas_call(
        body,
        out_shape=jax.ShapeDtypeStruct((members, rows, 2 * planes * part), gate.dtype),
        compiler_params=kernel_params(),
        cost_estimate=LIGHT,
    )(gate, up)


def columns_back(blocks, gate, up, gain, planes):
    members, rows, both = blocks.shape
    part = both // (2 * planes)
    ff = planes * members * part

    def body(x, g, u, gn, og, ou, ogn):
        total = 0.0
        for m, (w, o) in enumerate(((g, og), (u, ou))):
            grad = jnp.concatenate(
                [
                    x[s, :, (m * planes + p) * part : (m * planes + p + 1) * part]
                    for p in range(planes)
                    for s in range(members)
                ],
                axis=1,
            ).astype(F32)
            o[...] = grad
            total += jnp.sum(w[...].astype(F32) * grad, axis=1, keepdims=True)
        ogn[...] = total / gn[...].astype(F32)

    shape = jax.ShapeDtypeStruct((rows, ff), F32)
    out = pl.pallas_call(
        body,
        out_shape=(shape, shape, jax.ShapeDtypeStruct((rows, 1), F32)),
        compiler_params=kernel_params(),
        cost_estimate=LIGHT,
    )(blocks, gate, up, gain[:, None])
    return out[0], out[1], out[2][:, 0]


def scatter_dp(left, right, size, product):
    came = swap(product(left[left.shape[0] // 2 :], right).astype(BF16), 1)
    return dot_blocks(left, right, came, size // 2, product)


def attention_weights(parts, place, at_gains):
    size = len(parts)
    a, b, m = parts[0].shape
    lanes = at_gains // 128 * 128

    def body(at, *refs):
        out, gains = refs[-2:]
        for j in range(size):
            out[:, pl.ds(lax.rem(at[0] + j, size), 1)] = refs[j][...][:, None]
        strip = out[:, :, :, lanes : lanes + 128].reshape(a * size * b, 128).astype(F32)
        gains[...] = strip.T[at_gains - lanes : at_gains - lanes + 2]

    return pl.pallas_call(
        body,
        in_specs=[pl.BlockSpec(memory_space=pltpu.SMEM)]
        + [pl.BlockSpec(memory_space=pltpu.VMEM)] * size,
        out_shape=(
            jax.ShapeDtypeStruct((a, size, b, m), parts[0].dtype),
            jax.ShapeDtypeStruct((2, a * size * b), F32),
        ),
        compiler_params=kernel_params(),
        cost_estimate=LIGHT,
    )(jnp.full((1,), place, jnp.int32), *parts)


def norm_back(grad_in, normed, inverse, gain):
    grad_normed = grad_in * gain
    return inverse * (
        grad_normed - normed * jnp.mean(grad_normed * normed, axis=-1, keepdims=True)
    )


def per_device(
    n,
    c,
    tokens,
    segment_ids,
    out_grad,
    gain_attn,
    w_query,
    key_weight,
    value_weight,
    w_out,
    gain_mlp,
    w_gate,
    w_up,
    w_down,
):
    t, width = tokens.shape[1:]
    length = segment_ids.shape[1]
    block = w_query.shape[0]
    ff = w_gate.shape[1]
    heads = QUERY_HEADS // n
    group = QUERY_HEADS // KEY_VALUE_HEADS
    q_cols, f_cols = heads * HEAD_SIZE, ff // n
    every_dp = ("plane", "core")
    plane, core, place_z = (lax.axis_index(axis) for axis in ("plane", "core", "ctx"))
    me = 2 * plane + core

    pieces = []
    used = q_cols + HEAD_SIZE
    extras = jnp.concatenate(
        [gain_attn[:, None], gain_mlp[:, None], segment_ids.astype(BF16).reshape(block, -1)], axis=1
    )
    extras = jnp.pad(extras, ((0, 0), (0, -(used + extras.shape[1]) % 128)))
    for d in range(n):
        g = d * heads // group
        kv = value_weight if d % 2 else key_weight
        pieces += [
            w_query[:, d * q_cols : (d + 1) * q_cols],
            kv[:, g * HEAD_SIZE : (g + 1) * HEAD_SIZE],
            extras,
        ]
    w_attn = jnp.concatenate(pieces, axis=1).reshape(block, n, -1).transpose(1, 0, 2)
    w_attn = lax.all_to_all(w_attn, every_dp, 0, 0)
    x16, dy_local = tokens[0], out_grad[0]
    wd = lax.all_gather(w_down, "ctx", axis=0, tiled=True)
    wo = lax.all_gather(w_out, "ctx", axis=0, tiled=True)
    seg_rows = w_attn[:, :, used + 2 : used + 2 + length // block].reshape(n, length)

    order = me ^ jnp.array([*range(0, n, 2), *range(1, n, 2)], jnp.int32)
    pick = (order[:, None] == jnp.arange(n, dtype=jnp.int32)[None]).astype(BF16)
    segs = dot(pick, seg_rows)
    local_idx = place_z * t + jnp.arange(t, dtype=jnp.int32)
    local_seg = lax.dynamic_slice_in_dim(segs, place_z * t, t, axis=1)
    before = jnp.sum((segs[:, None, :] < local_seg[:, :, None]).astype(jnp.int32), axis=2)
    place = (local_idx[None] - before).astype(F32)
    freq = 10000.0 ** (-jnp.arange(HEAD_SIZE // 2, dtype=F32) / (HEAD_SIZE // 2))
    angle = place.reshape(n * t)[:, None] * freq[None, :]
    cosine, sine = jnp.cos(angle), jnp.sin(angle)
    cosine = jnp.concatenate([cosine] * 4, axis=1)
    sine = jnp.concatenate([-sine, sine] * 2, axis=1)
    w_pair = columns_out(*after((w_gate, w_up), w_attn), 1, n)
    w_pair = lax.all_to_all(w_pair, every_dp, 0, 0).reshape(n * block, 2 * f_cols)
    w_pair = lax.all_gather(w_pair, "ctx", axis=0, tiled=True)
    w_parts, same, cosine, sine = together(
        shifts(w_attn, c), dp_same(after(x16, w_attn), n), cosine, sine
    )
    even = jnp.concatenate([x16, *same])
    odd = swap(even, 1)

    w_attn, gains = attention_weights([w_attn, *w_parts], place_z, used)
    w_attn = w_attn.reshape(width, -1)
    gain1, gain2 = gains[:1], gains[1:]
    where = jnp.stack([place_z, core]).astype(jnp.int32)
    key_seg = lax.dynamic_slice_in_dim(
        jnp.concatenate([segs, segs], axis=1), place_z * t, length, axis=1
    )
    sides = local_seg[:, :, None], key_seg[:, None, :]

    first_in, queries, kv_own = project(where, even, odd, gain1, w_attn, cosine, sine, q_cols, t)

    kv_parts, dy_same = together(shifts(kv_own, c), dp_same(after(dy_local, first_in), n))
    dy_same = jnp.concatenate([dy_local, *dy_same])
    dy = dy_same, swap(dy_same, 1)
    kv_all = [kv_own, *kv_parts]
    kv_other = [swap(v, 1) for v in kv_all]
    mixed = attend(where, queries, kv_all, kv_other, *sides)
    attn_own, *sends = scatter_dp(mixed, wo, n, dot)
    sent = together(*[swap(v, 2 * j) for j, v in enumerate(sends, 1)])
    resid, second_in = second_norm(x16, attn_own, sent, gain2, n, c)

    in_parts, grad_hidden = together(
        dp_same(second_in, n), [dot_nt(half, wd).astype(BF16) for half in dy]
    )
    second_in = jnp.concatenate([second_in, *in_parts])
    second_in = second_in, swap(second_in, 1)
    same = feed_forward(second_in[0], grad_hidden[0], w_pair, wd)
    other = feed_forward(second_in[1], after(grad_hidden[1], same[2]), w_pair, wd)
    hidden, grad_pair = (same[0], other[0]), (same[1], other[1])
    back_came = swap(other[2], 1)
    down_term = transposed_dot(hidden, dy)
    grad_down = lax.psum_scatter(down_term, "ctx", scatter_dimension=0, tiled=True)
    back, *sends = add_blocks(same[2], after(back_came, down_term), n // 2)
    forth = swap(after(other[3], sends), 1)
    pair_term = transposed_dot(after(second_in, forth, down_term), grad_pair)
    forth, *forth_sends = add_blocks(same[3], forth, n // 2)
    sent, pair_term, forth_sends = together(
        [swap(v, 2 * j) for j, v in enumerate(sends, 1)], pair_term, forth_sends
    )
    grad_resid, branch = second_norm_back(resid, back, sent, gain2, dy_local, n, c)

    same, grad_down, pair_term = together(dp_same(branch, n), grad_down, pair_term)
    pair_sum = lax.psum_scatter(pair_term, "ctx", scatter_dimension=0, tiled=True)
    same = jnp.concatenate([branch, *same])
    grad_branch = same, swap(same, 1)
    grad_q, kept, sent = attend_back(
        where, *grad_branch, wo, queries, kv_all, kv_other, *sides, cosine, sine
    )
    result_parts = [swap(v, 2 * j) for j, v in enumerate(forth_sends, 1)]
    kept, sent, result_parts = together(kept, sent, result_parts)
    own_kv, *kv_sends = add_parts(kept, swap(sent, 1))
    kv_parts = together(*[shift(v, -j, c) for j, v in enumerate(kv_sends, 1)])
    result = resid + forth + sum(v.astype(F32) for v in result_parts)
    grad_kv = sum_keys(where, own_kv, kv_parts, cosine, sine)
    unused = jnp.zeros((n * t, w_attn.shape[1] - used), BF16)
    grad_attn = jnp.concatenate([grad_q, grad_kv, unused], axis=1)
    first_own, *sends = scatter_dp(grad_attn, w_attn, n, dot_nt)
    own_terms, *terms = attention_weight_terms(
        where, first_in, grad_attn, mixed, grad_branch, used, n, c
    )
    sent, terms = together(
        [swap(v, 2 * j) for j, v in enumerate(sends, 1)],
        [shift(v, -j, c) for j, v in enumerate(terms, 1)],
    )
    pair_sum = after(pair_sum, terms).reshape(n, block, 2 * f_cols)
    pair_sum = lax.all_to_all(pair_sum, every_dp, 0, 0)
    terms = (own_terms.astype(F32) + sum(v.astype(F32) for v in terms)).reshape(n, block, -1)
    grad_wout = terms[:, :, used : used + width // n].transpose(1, 0, 2).reshape(block, width)
    attn_sum = lax.all_to_all(terms[:, :, :used].astype(BF16), every_dp, 0, 0).astype(F32)
    grad_first = first_own + sum(v.astype(F32) for v in sent)
    grad_down = after(grad_down, attn_sum).astype(F32)

    grad_gate, grad_up, grad_gain_mlp = columns_back(pair_sum, w_gate, w_up, gain_mlp, 1)
    grad_query = attn_sum[:, :, :q_cols].transpose(1, 0, 2).reshape(block, -1)
    kv_sum = attn_sum[:, :, q_cols:].reshape(KEY_VALUE_HEADS, -1, 2, block, HEAD_SIZE).sum(axis=1)
    grad_key = kv_sum[:, 0].transpose(1, 0, 2).reshape(block, -1)
    grad_value = kv_sum[:, 1].transpose(1, 0, 2).reshape(block, -1)
    grad_gain_attn = (
        jnp.sum(w_query.astype(F32) * grad_query, axis=1)
        + jnp.sum(key_weight.astype(F32) * grad_key, axis=1)
        + jnp.sum(value_weight.astype(F32) * grad_value, axis=1)
    ) / gain_attn.astype(F32)
    x = x16.astype(F32)
    inverse1 = lax.rsqrt(jnp.mean(x * x, axis=-1, keepdims=True) + EPS)
    grad_input = grad_resid + norm_back(grad_first, x * inverse1, inverse1, gain1)
    return (
        result.astype(BF16)[None],
        grad_input[None],
        grad_gain_attn,
        grad_query,
        grad_key,
        grad_value,
        grad_wout,
        grad_gain_mlp,
        grad_gate,
        grad_up,
        grad_down,
    )


def solution(mesh):
    n, c = mesh.shape["dp"], mesh.shape["ctx"]
    split = Mesh(mesh.devices.reshape(n // 2, 2, c), ("plane", "core", "ctx"))
    dp, every = ("plane", "core"), ("plane", "core", "ctx")
    rows = P(dp, "ctx", None)
    weight, gain = P(every, None), P(every)
    return jax.shard_map(
        functools.partial(per_device, n, c),
        mesh=split,
        in_specs=(rows, P(dp, None), rows, gain, weight, weight, weight, weight, gain)
        + (weight,) * 3,
        out_specs=(rows, rows, gain, weight, weight, weight, weight, gain) + (weight,) * 3,
        check_vma=False,
    )
```

```python
import functools

import jax
import jax.numpy as jnp
from jax import lax
from jax.experimental import pallas as pl
from jax.experimental.pallas import tpu as pltpu
from jax.sharding import Mesh
from jax.sharding import PartitionSpec as P

QUERY_HEADS = 32
KEY_VALUE_HEADS = 4
HEAD_SIZE = 64
EPS = 1e-05
NEG = -1e30
F32 = jnp.float32
BF16 = jnp.bfloat16


def dot(left, right):
    return jnp.dot(left, right, preferred_element_type=F32)


def dot_nt(left, right):
    return lax.dot_general(left, right, (((1,), (1,)), ((), ())), preferred_element_type=F32)


def dot_tn(left, right):
    return lax.dot_general(left, right, (((0,), (0,)), ((), ())), preferred_element_type=F32)


def swap(value, rel):
    size = lax.axis_size(("plane", "core"))
    return lax.ppermute(value, ("plane", "core"), [(i, i ^ rel) for i in range(size)])


def shift(value, step, size):
    return lax.ppermute(value, "ctx", [(i, (i - step) % size) for i in range(size)])


def shifts(value, size):
    return [shift(value, j, size) for j in range(1, size)]


def together(*values):
    return lax.optimization_barrier(values)


def after(value, *earlier):
    return together(value, *earlier)[0]


def dp_same(rows, size):
    return [swap(rows, rel) for rel in range(2, size, 2)]


def kernel_params(mib=32):
    return pltpu.CompilerParams(vmem_limit_bytes=mib * 2**20)

LIGHT = pl.CostEstimate(flops=1024, bytes_accessed=1024, transcendentals=0)


def transposed_dot(lefts, rights):
    tokens, rows = lefts[0].shape
    columns, count = rights[0].shape[1], len(lefts)
    by_rows = rows % 256 == 0 and rows > columns
    row_tile = 256 if by_rows else rows
    column_tile = columns if by_rows or columns % 512 else 512
    moving = pl.BlockSpec((tokens, row_tile if by_rows else column_tile), lambda i: (0, i))
    resting = pl.BlockSpec((tokens, column_tile if by_rows else row_tile), lambda i: (0, 0))

    def body(*refs):
        total = 0.0
        for left, right in zip(refs[:count], refs[count:-1]):
            total += lax.dot_general(
                left[...], right[...], (((0,), (0,)), ((), ())), preferred_element_type=F32
            )
        refs[-1][...] = total.astype(BF16)

    return pl.pallas_call(
        body,
        grid=(rows // row_tile if by_rows else columns // column_tile,),
        in_specs=[moving if by_rows else resting] * count + [resting if by_rows else moving] * count,
        out_specs=pl.BlockSpec(
            (row_tile, column_tile), (lambda i: (i, 0)) if by_rows else (lambda i: (0, i))
        ),
        out_shape=jax.ShapeDtypeStruct((rows, columns), BF16),
        compiler_params=kernel_params(),
        cost_estimate=LIGHT,
    )(*lefts, *rights)


def turn(values, cosine, sine):
    half = HEAD_SIZE // 2
    width = values.shape[1]
    lane = lax.broadcasted_iota(jnp.int32, values.shape, 1)
    up = jnp.concatenate([values[:, half:], values[:, :half]], axis=1)
    down = jnp.concatenate([values[:, width - half :], values[:, : width - half]], axis=1)
    return values * cosine + jnp.where(lane % HEAD_SIZE < half, up, down) * sine


def widen(table, columns):
    return jnp.concatenate([table] * (columns // table.shape[1]), axis=1)


def pack(rows):
    half = rows.shape[0] // 2
    return jnp.concatenate([rows[:half], rows[half:]], axis=1)


def unpack(rows):
    half = rows.shape[1] // 2
    return jnp.concatenate([rows[:, :half], rows[:, half:]], axis=0)


def project(where, even, odd, gain, weights, cosine, sine, q_cols, part):
    half, width = even.shape
    columns = q_cols + HEAD_SIZE
    tile = 256
    steps = half // tile

    def body(at, e, o, gn, w, cs, sn, first, queries, kv):
        x = jnp.where(pl.program_id(0) < steps, e[...], o[...]).astype(F32)
        normed = x * lax.rsqrt(jnp.mean(x * x, axis=-1, keepdims=True) + EPS)
        rows = (normed * gn[...]).astype(BF16)
        first[...] = rows
        raw = dot(rows, w[...])
        queries[...] = turn(
            raw[:, :q_cols], widen(cs[...], q_cols), widen(sn[...], q_cols)
        ).astype(BF16)
        plain = raw[:, q_cols:columns]
        turned = turn(plain, cs[:, :HEAD_SIZE], sn[:, :HEAD_SIZE])
        chosen = jnp.where(at[1] == 0, turned, plain)
        for p in range(tile // part):
            kv[p] = pack(chosen[p * part : (p + 1) * part]).astype(BF16)

    def rows(size):
        return pl.BlockSpec((tile, size), lambda i: (i, 0))

    return pl.pallas_call(
        body,
        grid=(2 * steps,),
        in_specs=[
            pl.BlockSpec(memory_space=pltpu.SMEM),
            pl.BlockSpec((tile, width), lambda i: (jnp.minimum(i, steps - 1), 0)),
            pl.BlockSpec((tile, width), lambda i: (jnp.maximum(i - steps, 0), 0)),
            pl.BlockSpec((1, width), lambda i: (0, 0)),
            pl.BlockSpec(weights.shape, lambda i: (0, 0)),
            rows(cosine.shape[1]),
            rows(cosine.shape[1]),
        ],
        out_specs=(
            rows(width),
            rows(q_cols),
            pl.BlockSpec((tile // part, part // 2, 2 * HEAD_SIZE), lambda i: (i, 0, 0)),
        ),
        out_shape=(
            jax.ShapeDtypeStruct((2 * half, width), BF16),
            jax.ShapeDtypeStruct((2 * half, q_cols), BF16),
            jax.ShapeDtypeStruct((2 * half // part, part // 2, 2 * HEAD_SIZE), BF16),
        ),
        compiler_params=kernel_params(),
        cost_estimate=LIGHT,
    )(where, even, odd, gain, weights, cosine, sine)


def stacked(values, heads):
    return jnp.concatenate(
        [values[:, h * HEAD_SIZE : (h + 1) * HEAD_SIZE] for h in range(heads)], axis=0
    )


def side_by_side(values, heads):
    rows = values.shape[0] // heads
    return jnp.concatenate([values[h * rows : (h + 1) * rows] for h in range(heads)], axis=1)


def probabilities(queries, keys, mine, theirs, place, parts, heads):
    rows, length = queries.shape[0] // heads, keys.shape[0]
    part = length // parts
    scores = dot_nt(queries, keys) * HEAD_SIZE**-0.5
    query_at = place * part + lax.broadcasted_iota(jnp.int32, (rows, length), 0)
    key_at = place * part + lax.broadcasted_iota(jnp.int32, (rows, length), 1)
    key_at = jnp.where(key_at >= length, key_at - length, key_at)
    allowed = (key_at <= query_at) & (mine == theirs)
    allowed = jnp.concatenate([allowed] * heads, axis=0)
    scores = jnp.where(allowed, scores, NEG)
    expo = jnp.exp(scores - jnp.max(scores, axis=-1, keepdims=True))
    return expo / jnp.sum(expo, axis=-1, keepdims=True)


def sequence_specs(sequences, part, parts):
    half = sequences // 2
    shape = (1, part // 2, 2 * HEAD_SIZE)
    own = pl.BlockSpec(shape, lambda i: (i, 0, 0))
    came = pl.BlockSpec(shape, lambda i: (lax.rem(i + half, sequences), 0, 0))
    return [own] * parts + [came] * parts


def keys_values(first, refs):
    parts = len(refs) // 2
    own, came = (
        jnp.concatenate([unpack(ref[0]) for ref in half], axis=0) for half in (refs[:parts], refs[parts:])
    )
    return jnp.where(first, own, came), jnp.where(first, came, own)


def attend(where, queries, own, came, mine, theirs):
    parts = len(own)
    sequences, part = own[0].shape[0], 2 * own[0].shape[1]
    rows, columns = queries.shape[0] // sequences, queries.shape[1]
    heads = columns // HEAD_SIZE

    def body(at, q, m, th, *refs):
        keys, values = keys_values(at[1] == 0, refs[:-1])
        probs = probabilities(stacked(q[...], heads), keys, m[0], th[0], at[0], parts, heads)
        refs[-1][...] = side_by_side(dot(probs.astype(BF16), values), heads).astype(BF16)

    return pl.pallas_call(
        body,
        grid=(sequences,),
        in_specs=[
            pl.BlockSpec(memory_space=pltpu.SMEM),
            pl.BlockSpec((rows, columns), lambda i: (i, 0)),
            pl.BlockSpec((1, rows, 1), lambda i: (i, 0, 0)),
            pl.BlockSpec((1, 1, parts * part), lambda i: (i, 0, 0)),
            *sequence_specs(sequences, part, parts),
        ],
        out_specs=pl.BlockSpec((rows, columns), lambda i: (i, 0)),
        out_shape=jax.ShapeDtypeStruct(queries.shape, BF16),
        compiler_params=kernel_params(),
        cost_estimate=LIGHT,
    )(where, queries, mine, theirs, *own, *came)


def attend_back(where, same, other, w_out, queries, own, came, mine, theirs, cosine, sine):
    parts = len(own)
    sequences, part = own[0].shape[0], 2 * own[0].shape[1]
    length = parts * part
    rows, columns = queries.shape[0] // sequences, queries.shape[1]
    heads, half, width = columns // HEAD_SIZE, sequences // 2, same.shape[1]
    packed = parts, part // 2, 2 * HEAD_SIZE
    scale = HEAD_SIZE**-0.5

    def body(at, s, o, w, q, m, th, cs, sn, *refs):
        dq, down, dcame = refs[-3:]
        first = at[1] == 0
        keys, values = keys_values(first, refs[:-3])
        branch = jnp.where(pl.program_id(0) < half, s[...], o[...])
        mixed = stacked(dot_nt(branch, w[...]).astype(BF16), heads)
        stack = stacked(q[...], heads)
        probs = probabilities(stack, keys, m[0], th[0], at[0], parts, heads)
        grad = dot_nt(mixed, values)
        inner = jnp.sum(probs * grad, axis=-1, keepdims=True)
        scores = (probs * (grad - inner)).astype(BF16)
        grad_q = side_by_side(dot(scores, keys) * scale, heads)
        dq[...] = turn(grad_q, widen(cs[...], columns), -widen(sn[...], columns)).astype(BF16)
        grad_k = dot_tn(scores, stack) * scale
        grad_v = dot_tn(probs.astype(BF16), mixed)
        kept, sent = jnp.where(first, grad_k, grad_v), jnp.where(first, grad_v, grad_k)
        for j in range(parts):
            at_rows = slice(j * part, (j + 1) * part)
            down[0, j] = pack(kept[at_rows])
            dcame[0, j] = pack(sent[at_rows]).astype(BF16)

    def strip(size):
        return pl.BlockSpec((rows, size), lambda i: (i, 0))

    return pl.pallas_call(
        body,
        grid=(sequences,),
        in_specs=[
            pl.BlockSpec(memory_space=pltpu.SMEM),
            pl.BlockSpec((rows, width), lambda i: (jnp.minimum(i, half - 1), 0)),
            pl.BlockSpec((rows, width), lambda i: (jnp.maximum(i - half, 0), 0)),
            pl.BlockSpec(w_out.shape, lambda i: (0, 0)),
            strip(columns),
            pl.BlockSpec((1, rows, 1), lambda i: (i, 0, 0)),
            pl.BlockSpec((1, 1, length), lambda i: (i, 0, 0)),
            strip(cosine.shape[1]),
            strip(cosine.shape[1]),
            *sequence_specs(sequences, part, parts),
        ],
        out_specs=(
            strip(columns),
            pl.BlockSpec((1, *packed), lambda i: (i, 0, 0, 0)),
            pl.BlockSpec((1, *packed), lambda i: (lax.rem(i + half, sequences), 0, 0, 0)),
        ),
        out_shape=(
            jax.ShapeDtypeStruct(queries.shape, BF16),
            jax.ShapeDtypeStruct((sequences, *packed), F32),
            jax.ShapeDtypeStruct((sequences, *packed), BF16),
        ),
        compiler_params=kernel_params(),
        cost_estimate=LIGHT,
    )(where, same, other, w_out, queries, mine, theirs, cosine, sine, *own, *came)


def add_parts(kept, came):
    sequences, parts, rows, columns = kept.shape

    def body(a, b, *outs):
        for j, out in enumerate(outs):
            out[...] = (a[:, j] + b[:, j].astype(F32)).astype(out.dtype)

    return pl.pallas_call(
        body,
        out_shape=[
            jax.ShapeDtypeStruct((sequences, rows, columns), BF16 if j else F32)
            for j in range(parts)
        ],
        compiler_params=kernel_params(),
        cost_estimate=LIGHT,
    )(kept, came)


def sum_keys(where, own, came, cosine, sine):
    sequences, rows, _ = own.shape
    count = len(came)

    def body(at, a, cs, sn, *refs):
        total = a[...]
        for ref in refs[:count]:
            total += ref[...].astype(F32)
        out = refs[count]
        for i in range(sequences):
            at_rows = slice(2 * i * rows, 2 * (i + 1) * rows)
            plain = unpack(total[i])
            turned = turn(plain, cs[at_rows, :HEAD_SIZE], -sn[at_rows, :HEAD_SIZE])
            out[at_rows, :] = jnp.where(at[1] == 0, turned, plain).astype(BF16)

    whole = pl.BlockSpec(memory_space=pltpu.VMEM)
    return pl.pallas_call(
        body,
        in_specs=[pl.BlockSpec(memory_space=pltpu.SMEM)] + [whole] * (3 + count),
        out_shape=jax.ShapeDtypeStruct((2 * sequences * rows, HEAD_SIZE), BF16),
        compiler_params=kernel_params(),
        cost_estimate=LIGHT,
    )(where, own, cosine, sine, *came)


def attention_weight_terms(where, first_in, grad_attn, mixed, grad_branch, used, members, parts):
    tokens, width = first_in.shape
    columns, half = mixed.shape[1], mixed.shape[0] // 2
    block, strip = width // (members * parts), width // members
    upper = members // 2

    def body(at, x, g, m, ba, bb, *refs):
        outs, (left, right) = refs[:parts], refs[parts:]
        left[...] = dot_tn(x[...], g[:, : left.shape[1]])
        right[...] = dot_tn(m[:half, :], ba[...]) + dot_tn(m[half:, :], bb[...])
        for j, out in enumerate(outs):
            place = lax.rem(at[0] + j, parts)
            own = right[pl.ds(pl.multiple_of(place * block, block), block), :]

            def both(d):
                rows = pl.ds(pl.multiple_of((d * parts + place) * block, block), block)
                return [left[rows, :][:, :used], own[:, d * strip : (d + 1) * strip]]

            for d in range(upper):
                out[d * block : (d + 1) * block, :] = jnp.concatenate(
                    both(d) + both(d + upper), axis=1
                ).astype(BF16)

    whole = pl.BlockSpec(memory_space=pltpu.VMEM)
    return pl.pallas_call(
        body,
        in_specs=[pl.BlockSpec(memory_space=pltpu.SMEM)] + [whole] * 5,
        out_shape=[jax.ShapeDtypeStruct((upper * block, 2 * (used + strip)), BF16)] * parts,
        scratch_shapes=[
            pltpu.VMEM((width, grad_attn.shape[1]), F32),
            pltpu.VMEM((columns, width), F32),
        ],
        compiler_params=kernel_params(),
        cost_estimate=LIGHT,
    )(where, first_in, grad_attn, mixed, *grad_branch)


def hidden_units(second_in, w_pair):
    tokens, width = second_in.shape
    ff = w_pair.shape[1] // 2
    tile = 256

    def body(x, w, both, hidden):
        product = dot(x[...], w[...])
        gate, up = product[:, :ff], product[:, ff:]
        both[...] = product
        hidden[...] = (gate * jax.nn.sigmoid(gate) * up).astype(BF16)

    def rows(columns):
        return pl.BlockSpec((tile, columns), lambda i: (i, 0))

    return pl.pallas_call(
        body,
        grid=(tokens // tile,),
        in_specs=[rows(width), pl.BlockSpec(w_pair.shape, lambda i: (0, 0), pipeline_mode=pl.Buffered(1))],
        out_specs=(rows(2 * ff), rows(ff)),
        out_shape=(
            jax.ShapeDtypeStruct((tokens, 2 * ff), F32),
            jax.ShapeDtypeStruct((tokens, ff), BF16),
        ),
        compiler_params=kernel_params(),
        cost_estimate=LIGHT,
    )(second_in, w_pair)


def feed_forward_back(both, hidden, grad_out, w_pair, w_down):
    tokens, width = grad_out.shape
    ff = hidden.shape[1]
    tile = 256

    def body(both, h, dy, w, wd, grads, back, forth):
        gate, up = both[:, :ff], both[:, ff:]
        sig = jax.nn.sigmoid(gate)
        forth[...] = dot(h[...], wd[...]).astype(BF16)
        dh_sig = dot_nt(dy[...], wd[...]) * sig
        grad = jnp.concatenate(
            [dh_sig * up * (1.0 + gate * (1.0 - sig)), dh_sig * gate], axis=1
        ).astype(BF16)
        grads[...] = grad
        back[...] = dot_nt(grad, w[...]).astype(BF16)

    def rows(columns):
        return pl.BlockSpec((tile, columns), lambda i: (i, 0))

    def whole(array):
        return pl.BlockSpec(array.shape, lambda i: (0, 0), pipeline_mode=pl.Buffered(1))

    return pl.pallas_call(
        body,
        grid=(tokens // tile,),
        in_specs=[rows(2 * ff), rows(ff), rows(width), whole(w_pair), whole(w_down)],
        out_specs=(rows(2 * ff), rows(width), rows(width)),
        out_shape=(
            jax.ShapeDtypeStruct((tokens, 2 * ff), BF16),
            jax.ShapeDtypeStruct((tokens, width), BF16),
            jax.ShapeDtypeStruct((tokens, width), BF16),
        ),
        compiler_params=kernel_params(),
        cost_estimate=LIGHT,
    )(both, hidden, grad_out, w_pair, w_down)


def add_blocks(own, came, blocks):
    tokens, columns = own.shape[0] // blocks, own.shape[1]

    def body(a, b, *outs):
        for j, out in enumerate(outs):
            rows = pl.ds(j * tokens, tokens)
            out[...] = (a[rows, :].astype(F32) + b[rows, :].astype(F32)).astype(out.dtype)

    return pl.pallas_call(
        body,
        out_shape=[
            jax.ShapeDtypeStruct((tokens, columns), BF16 if j else F32) for j in range(blocks)
        ],
        compiler_params=kernel_params(),
        cost_estimate=LIGHT,
    )(own, came)


def regroup(values, outer, inner):
    part = values.shape[1] // (outer * inner)
    return jnp.concatenate(
        [
            values[:, (o * inner + i) * part : (o * inner + i + 1) * part]
            for i in range(inner)
            for o in range(outer)
        ],
        axis=1,
    )


def second_norm(x, own, sent, gain, outer, inner):
    count = len(sent)

    def body(x, own, gain, *refs):
        resid = x[...].astype(F32) + own[...]
        for ref in refs[:count]:
            resid += ref[...].astype(F32)
        refs[count][...] = resid
        normed = resid * lax.rsqrt(jnp.mean(resid * resid, axis=-1, keepdims=True) + EPS)
        refs[count + 1][...] = regroup((normed * gain[...]).astype(BF16), outer, inner)

    return pl.pallas_call(
        body,
        out_shape=(
            jax.ShapeDtypeStruct(x.shape, F32),
            jax.ShapeDtypeStruct(x.shape, BF16),
        ),
        compiler_params=kernel_params(),
        cost_estimate=LIGHT,
    )(x, own, gain, *sent)


def second_norm_back(resid, own, sent, gain, grad_out, outer, inner):
    count = len(sent)

    def body(resid, own, gain, grad_out, *refs):
        grad = own[...]
        for ref in refs[:count]:
            grad += ref[...].astype(F32)
        grad = regroup(grad, inner, outer)
        rows = resid[...]
        inverse = lax.rsqrt(jnp.mean(rows * rows, axis=-1, keepdims=True) + EPS)
        total = grad_out[...].astype(F32) + norm_back(grad, rows * inverse, inverse, gain[...])
        refs[count][...] = total
        refs[count + 1][...] = total.astype(BF16)

    return pl.pallas_call(
        body,
        out_shape=(
            jax.ShapeDtypeStruct(resid.shape, F32),
            jax.ShapeDtypeStruct(resid.shape, BF16),
        ),
        compiler_params=kernel_params(),
        cost_estimate=LIGHT,
    )(resid, own, gain, grad_out, *sent)


def dot_blocks(left, right, came, blocks, product):
    tokens, columns = came.shape[0] // blocks, came.shape[1]

    def body(a, b, c, *outs):
        for j, out in enumerate(outs):
            rows = pl.ds(j * tokens, tokens)
            out[...] = (product(a[rows, :], b[...]) + c[rows, :].astype(F32)).astype(out.dtype)

    return pl.pallas_call(
        body,
        out_shape=[
            jax.ShapeDtypeStruct((tokens, columns), BF16 if j else F32) for j in range(blocks)
        ],
        compiler_params=kernel_params(),
        cost_estimate=LIGHT,
    )(left, right, came)


def columns_out(gate, up, planes, members):
    rows, ff = gate.shape
    part = ff // (planes * members)

    def body(g, u, o):
        both = g[...], u[...]
        for s in range(members):
            o[s] = jnp.concatenate(
                [
                    v[:, (p * members + s) * part : (p * members + s + 1) * part]
                    for v in both
                    for p in range(planes)
                ],
                axis=1,
            )

    return pl.pallas_call(
        body,
        out_shape=jax.ShapeDtypeStruct((members, rows, 2 * planes * part), gate.dtype),
        compiler_params=kernel_params(),
        cost_estimate=LIGHT,
    )(gate, up)


def gather_terms(own, sums, members, used, width):
    block, count, strip = 2 * own.shape[0] // members, len(sums), width // members

    def body(a, *refs):
        total = a[...].astype(F32)
        for ref in refs[:count]:
            total += ref[...].astype(F32)
        out, payload = refs[count:]
        strips = []
        for d in range(members):
            side, row = divmod(d, members // 2)
            start = side * (used + strip)
            rows = total[row * block : (row + 1) * block]
            payload[d] = rows[:, start : start + used].astype(BF16)
            strips.append(rows[:, start + used : start + used + strip])
        out[...] = jnp.concatenate(strips, axis=1)

    return pl.pallas_call(
        body,
        out_shape=(
            jax.ShapeDtypeStruct((block, width), F32),
            jax.ShapeDtypeStruct((members, block, used), BF16),
        ),
        compiler_params=kernel_params(),
        cost_estimate=LIGHT,
    )(own, *sums)


def weight_gradients(pairs, blocks, weights, gains, q_cols):
    members, rows, _ = blocks.shape
    part, shared = pairs.shape[2] // 2, members // (2 * KEY_VALUE_HEADS)

    def body(pair, x, g, u, q, k, v, gains, og, ou, oq, ok, ov, ogain):
        def side(start, size, chosen, x=x):
            return [x[d, :, start : start + size].astype(F32) for d in chosen]

        def heads(core):
            found = side(q_cols, HEAD_SIZE, range(core, members, 2))
            return jnp.concatenate(
                [sum(found[h * shared : (h + 1) * shared]) for h in range(KEY_VALUE_HEADS)], axis=1
            )

        og[...] = jnp.concatenate(side(0, part, range(members), pair), axis=1)
        ou[...] = jnp.concatenate(side(part, part, range(members), pair), axis=1)
        oq[...] = jnp.concatenate(side(0, q_cols, range(members)), axis=1)
        ok[...] = heads(0)
        ov[...] = heads(1)

        def gain(both):
            return sum(jnp.sum(w[...].astype(F32) * o[...], axis=1, keepdims=True) for w, o in both)

        total = jnp.concatenate([gain(((q, oq), (k, ok), (v, ov))), gain(((g, og), (u, ou)))], axis=1)
        ogain[...] = total / gains[...].astype(F32)

    return pl.pallas_call(
        body,
        out_shape=[jax.ShapeDtypeStruct(w.shape, F32) for w in weights]
        + [jax.ShapeDtypeStruct((rows, 2), F32)],
        compiler_params=kernel_params(),
        cost_estimate=LIGHT,
    )(pairs, blocks, *weights, gains)


def scatter_dp(left, right, size, product):
    came = swap(product(left[left.shape[0] // 2 :], right).astype(BF16), 1)
    return dot_blocks(left, right, came, size // 2, product)


def in_order(parts, place):
    size = len(parts)
    rows, columns = parts[0].shape

    def body(at, *refs):
        for j in range(size):
            refs[-1][pl.ds(lax.rem(at[0] + j, size), 1)] = refs[j][...][None]

    out = pl.pallas_call(
        body,
        in_specs=[pl.BlockSpec(memory_space=pltpu.SMEM)]
        + [pl.BlockSpec(memory_space=pltpu.VMEM)] * size,
        out_shape=jax.ShapeDtypeStruct((size, rows, columns), parts[0].dtype),
        compiler_params=kernel_params(),
        cost_estimate=LIGHT,
    )(jnp.full((1,), place, jnp.int32), *parts)
    return out.reshape(size * rows, columns)


def attention_weights(parts, place, at_gains):
    size = len(parts)
    a, b, m = parts[0].shape
    lanes = at_gains // 128 * 128

    def body(at, *refs):
        out, gains = refs[-2:]
        for j in range(size):
            out[:, pl.ds(lax.rem(at[0] + j, size), 1)] = refs[j][...][:, None]
        strip = out[:, :, :, lanes : lanes + 128].reshape(a * size * b, 128).astype(F32)
        gains[...] = strip.T[at_gains - lanes : at_gains - lanes + 2]

    return pl.pallas_call(
        body,
        in_specs=[pl.BlockSpec(memory_space=pltpu.SMEM)]
        + [pl.BlockSpec(memory_space=pltpu.VMEM)] * size,
        out_shape=(
            jax.ShapeDtypeStruct((a, size, b, m), parts[0].dtype),
            jax.ShapeDtypeStruct((2, a * size * b), F32),
        ),
        compiler_params=kernel_params(),
        cost_estimate=LIGHT,
    )(jnp.full((1,), place, jnp.int32), *parts)


def norm_back(grad_in, normed, inverse, gain):
    grad_normed = grad_in * gain
    return inverse * (
        grad_normed - normed * jnp.mean(grad_normed * normed, axis=-1, keepdims=True)
    )


def per_device(
    n,
    c,
    tokens,
    segment_ids,
    out_grad,
    gain_attn,
    w_query,
    key_weight,
    value_weight,
    w_out,
    gain_mlp,
    w_gate,
    w_up,
    w_down,
):
    t, width = tokens.shape[1:]
    length = segment_ids.shape[1]
    block = w_query.shape[0]
    ff = w_gate.shape[1]
    heads = QUERY_HEADS // n
    group = QUERY_HEADS // KEY_VALUE_HEADS
    q_cols, f_cols = heads * HEAD_SIZE, ff // n
    every_dp = ("plane", "core")
    plane, core, place_z = (lax.axis_index(axis) for axis in ("plane", "core", "ctx"))
    me = 2 * plane + core

    pieces = []
    used = q_cols + HEAD_SIZE
    extras = jnp.concatenate(
        [gain_attn[:, None], gain_mlp[:, None], segment_ids.astype(BF16).reshape(block, -1)], axis=1
    )
    extras = jnp.pad(extras, ((0, 0), (0, -(used + extras.shape[1]) % 128)))
    for d in range(n):
        g = d * heads // group
        kv = value_weight if d % 2 else key_weight
        pieces += [
            w_query[:, d * q_cols : (d + 1) * q_cols],
            kv[:, g * HEAD_SIZE : (g + 1) * HEAD_SIZE],
            extras,
        ]
    w_attn = jnp.concatenate(pieces, axis=1).reshape(block, n, -1).transpose(1, 0, 2)
    w_attn = lax.all_to_all(w_attn, every_dp, 0, 0)
    x16, dy_local = tokens[0], out_grad[0]
    w_attn, wo_parts = together(w_attn, shifts(w_out, c))
    seg_rows = w_attn[:, :, used + 2 : used + 2 + length // block].reshape(n, length)

    order = me ^ jnp.array([*range(0, n, 2), *range(1, n, 2)], jnp.int32)
    pick = (order[:, None] == jnp.arange(n, dtype=jnp.int32)[None]).astype(BF16)
    segs = dot(pick, seg_rows)
    local_idx = place_z * t + jnp.arange(t, dtype=jnp.int32)
    local_seg = lax.dynamic_slice_in_dim(segs, place_z * t, t, axis=1)
    before = jnp.sum((segs[:, None, :] < local_seg[:, :, None]).astype(jnp.int32), axis=2)
    place = (local_idx[None] - before).astype(F32)
    freq = 10000.0 ** (-jnp.arange(HEAD_SIZE // 2, dtype=F32) / (HEAD_SIZE // 2))
    angle = place.reshape(n * t)[:, None] * freq[None, :]
    cosine, sine = jnp.cos(angle), jnp.sin(angle)
    cosine = jnp.concatenate([cosine] * 4, axis=1)
    sine = jnp.concatenate([-sine, sine] * 2, axis=1)
    w_pair = columns_out(*after((w_gate, w_up), w_attn), 1, n)
    w_pair = lax.all_to_all(w_pair, every_dp, 0, 0).reshape(n * block, 2 * f_cols)
    w_parts, same, cosine, sine, w_pair = together(
        shifts(w_attn, c), dp_same(after(x16, w_attn), n), cosine, sine, w_pair
    )
    w_pair = lax.all_gather(w_pair, "ctx", axis=0, tiled=True)
    even = jnp.concatenate([x16, *same])
    odd = swap(even, 1)

    w_attn, gains = attention_weights([w_attn, *w_parts], place_z, used)
    w_attn = w_attn.reshape(width, -1)
    gain1, gain2 = gains[:1], gains[1:]
    wo = in_order([w_out, *wo_parts], place_z)
    where = jnp.stack([place_z, core]).astype(jnp.int32)
    key_seg = lax.dynamic_slice_in_dim(
        jnp.concatenate([segs, segs], axis=1), place_z * t, length, axis=1
    )
    sides = local_seg[:, :, None], key_seg[:, None, :]

    first_in, queries, kv_own = project(where, even, odd, gain1, w_attn, cosine, sine, q_cols, t)

    kv_parts, dy_same = together(shifts(kv_own, c), dp_same(after(dy_local, first_in), n))
    dy_same = jnp.concatenate([dy_local, *dy_same])
    dy = dy_same, swap(dy_same, 1)
    kv_all = [kv_own, *kv_parts]
    kv_other = [swap(v, 1) for v in kv_all]
    mixed = attend(where, queries, kv_all, kv_other, *sides)
    attn_own, *sends = scatter_dp(mixed, wo, n, dot)
    sent, w_pair = together([swap(v, 2 * j) for j, v in enumerate(sends, 1)], w_pair)
    wd = lax.all_gather(after(w_down, w_pair), "ctx", axis=0, tiled=True)
    resid, second_in = second_norm(x16, attn_own, sent, gain2, n, c)

    second_in = jnp.concatenate([second_in, *together(*dp_same(second_in, n))])
    second_in = second_in, swap(second_in, 1)
    units = hidden_units(second_in[0], w_pair)
    units = units, hidden_units(after(second_in[1], units), w_pair)
    hidden = [half[1] for half in units]
    down_term = transposed_dot(hidden, dy)
    grad_down = lax.psum_scatter(after(down_term, wd), "ctx", scatter_dimension=0, tiled=True)
    other = feed_forward_back(*units[1], dy[1], w_pair, after(wd, down_term))
    same = feed_forward_back(*units[0], after(dy[0], other[0]), w_pair, wd)
    grad_pair = same[0], other[0]
    back, *sends = add_blocks(same[1], swap(other[1], 1), n // 2)
    forth = swap(after(other[2], sends), 1)
    pair_term = transposed_dot(after(second_in, forth), grad_pair)
    forth, *forth_sends = add_blocks(same[2], forth, n // 2)
    sent, pair_term, forth_sends, grad_down = together(
        [swap(v, 2 * j) for j, v in enumerate(sends, 1)], pair_term, forth_sends, grad_down
    )
    pair_sum = lax.psum_scatter(pair_term, "ctx", scatter_dimension=0, tiled=True)
    grad_resid, branch = second_norm_back(resid, back, sent, gain2, dy_local, n, c)

    same = together(*dp_same(branch, n))
    same = jnp.concatenate([branch, *same])
    grad_branch = same, swap(same, 1)
    grad_q, kept, sent = attend_back(
        where, *grad_branch, wo, queries, kv_all, kv_other, *sides, cosine, sine
    )
    result_parts = [swap(v, 2 * j) for j, v in enumerate(forth_sends, 1)]
    kept, sent, result_parts = together(kept, sent, result_parts)
    own_kv, *kv_sends = add_parts(kept, swap(sent, 1))
    kv_parts = together(*[shift(v, -j, c) for j, v in enumerate(kv_sends, 1)])
    result = resid + forth + sum(v.astype(F32) for v in result_parts)
    grad_kv = sum_keys(where, own_kv, kv_parts, cosine, sine)
    unused = jnp.zeros((n * t, w_attn.shape[1] - used), BF16)
    grad_attn = jnp.concatenate([grad_q, grad_kv, unused], axis=1)
    own_terms, *terms = attention_weight_terms(
        where, first_in, grad_attn, mixed, grad_branch, used, n, c
    )
    first_own, *sends = scatter_dp(after(grad_attn, terms), w_attn, n, dot_nt)
    pair_sum = after(pair_sum, sends).reshape(n, block, 2 * f_cols)
    sent, terms, pair_sum = together(
        [swap(v, 2 * j) for j, v in enumerate(sends, 1)],
        [shift(v, -j, c) for j, v in enumerate(terms, 1)],
        lax.all_to_all(pair_sum, every_dp, 0, 0),
    )
    grad_wout, payload = gather_terms(own_terms, terms, n, used, width)
    payload = lax.all_to_all(payload, every_dp, 0, 0)
    grad_gate, grad_up, grad_query, grad_key, grad_value, grad_gains = weight_gradients(
        pair_sum,
        payload,
        (w_gate, w_up, w_query, key_weight, value_weight),
        jnp.stack([gain_attn, gain_mlp], axis=1),
        q_cols,
    )
    grad_first = first_own + sum(v.astype(F32) for v in sent)
    grad_down = after(grad_down, terms).astype(F32)
    x = x16.astype(F32)
    inverse1 = lax.rsqrt(jnp.mean(x * x, axis=-1, keepdims=True) + EPS)
    grad_input = grad_resid + norm_back(grad_first, x * inverse1, inverse1, gain1)
    return (
        result.astype(BF16)[None],
        grad_input[None],
        grad_gains[:, 0],
        grad_query,
        grad_key,
        grad_value,
        grad_wout,
        grad_gains[:, 1],
        grad_gate,
        grad_up,
        grad_down,
    )


def solution(mesh):
    n, c = mesh.shape["dp"], mesh.shape["ctx"]
    split = Mesh(mesh.devices.reshape(n // 2, 2, c), ("plane", "core", "ctx"))
    dp, every = ("plane", "core"), ("plane", "core", "ctx")
    rows = P(dp, "ctx", None)
    weight, gain = P(every, None), P(every)
    return jax.shard_map(
        functools.partial(per_device, n, c),
        mesh=split,
        in_specs=(rows, P(dp, None), rows, gain, weight, weight, weight, weight, gain)
        + (weight,) * 3,
        out_specs=(rows, rows, gain, weight, weight, weight, weight, gain) + (weight,) * 3,
        check_vma=False,
    )
```

```python
import functools

import jax
import jax.numpy as jnp
from jax import lax
from jax.experimental import pallas as pl
from jax.experimental.pallas import tpu as pltpu
from jax.sharding import Mesh
from jax.sharding import PartitionSpec as P

QUERY_HEADS = 32
KEY_VALUE_HEADS = 4
HEAD_SIZE = 64
EPS = 1e-05
NEG = -1e30
F32 = jnp.float32
BF16 = jnp.bfloat16


def dot(left, right):
    return jnp.dot(left, right, preferred_element_type=F32)


def dot_nt(left, right):
    return lax.dot_general(left, right, (((1,), (1,)), ((), ())), preferred_element_type=F32)


def dot_tn(left, right):
    return lax.dot_general(left, right, (((0,), (0,)), ((), ())), preferred_element_type=F32)


def swap(value, rel):
    size = lax.axis_size(("plane", "core"))
    return lax.ppermute(value, ("plane", "core"), [(i, i ^ rel) for i in range(size)])


def shift(value, step, size):
    return lax.ppermute(value, "ctx", [(i, (i - step) % size) for i in range(size)])


def shifts(value, size):
    return [shift(value, j, size) for j in range(1, size)]


def together(*values):
    return lax.optimization_barrier(values)


def after(value, *earlier):
    return together(value, *earlier)[0]


def dp_same(rows, size):
    return [swap(rows, rel) for rel in range(2, size, 2)]


def kernel_params(mib=32):
    return pltpu.CompilerParams(vmem_limit_bytes=mib * 2**20)

LIGHT = pl.CostEstimate(flops=1024, bytes_accessed=1024, transcendentals=0)


def transposed_dot(lefts, rights):
    tokens, rows = lefts[0].shape
    columns, count = rights[0].shape[1], len(lefts)
    by_rows = rows % 256 == 0 and rows > columns
    row_tile = 256 if by_rows else rows
    column_tile = columns if by_rows or columns % 512 else 512
    moving = pl.BlockSpec((tokens, row_tile if by_rows else column_tile), lambda i: (0, i))
    resting = pl.BlockSpec((tokens, column_tile if by_rows else row_tile), lambda i: (0, 0))

    def body(*refs):
        total = 0.0
        for left, right in zip(refs[:count], refs[count:-1]):
            total += lax.dot_general(
                left[...], right[...], (((0,), (0,)), ((), ())), preferred_element_type=F32
            )
        refs[-1][...] = total.astype(BF16)

    return pl.pallas_call(
        body,
        grid=(rows // row_tile if by_rows else columns // column_tile,),
        in_specs=[moving if by_rows else resting] * count + [resting if by_rows else moving] * count,
        out_specs=pl.BlockSpec(
            (row_tile, column_tile), (lambda i: (i, 0)) if by_rows else (lambda i: (0, i))
        ),
        out_shape=jax.ShapeDtypeStruct((rows, columns), BF16),
        compiler_params=kernel_params(),
        cost_estimate=LIGHT,
    )(*lefts, *rights)


def turn(values, cosine, sine):
    half = HEAD_SIZE // 2
    width = values.shape[1]
    lane = lax.broadcasted_iota(jnp.int32, values.shape, 1)
    up = jnp.concatenate([values[:, half:], values[:, :half]], axis=1)
    down = jnp.concatenate([values[:, width - half :], values[:, : width - half]], axis=1)
    return values * cosine + jnp.where(lane % HEAD_SIZE < half, up, down) * sine


def widen(table, columns):
    return jnp.concatenate([table] * (columns // table.shape[1]), axis=1)


def pack(rows):
    half = rows.shape[0] // 2
    return jnp.concatenate([rows[:half], rows[half:]], axis=1)


def unpack(rows):
    half = rows.shape[1] // 2
    return jnp.concatenate([rows[:, :half], rows[:, half:]], axis=0)


def project(where, even, odd, gain, weights, cosine, sine, q_cols, part):
    half, width = even.shape
    columns = q_cols + HEAD_SIZE
    tile = 256
    steps = half // tile

    def body(at, e, o, gn, w, cs, sn, first, queries, kv):
        x = jnp.where(pl.program_id(0) < steps, e[...], o[...]).astype(F32)
        normed = x * lax.rsqrt(jnp.mean(x * x, axis=-1, keepdims=True) + EPS)
        rows = (normed * gn[...]).astype(BF16)
        first[...] = rows
        raw = dot(rows, w[...])
        queries[...] = turn(
            raw[:, :q_cols], widen(cs[...], q_cols), widen(sn[...], q_cols)
        ).astype(BF16)
        plain = raw[:, q_cols:columns]
        turned = turn(plain, cs[:, :HEAD_SIZE], sn[:, :HEAD_SIZE])
        chosen = jnp.where(at[1] == 0, turned, plain)
        for p in range(tile // part):
            kv[p] = pack(chosen[p * part : (p + 1) * part]).astype(BF16)

    def rows(size):
        return pl.BlockSpec((tile, size), lambda i: (i, 0))

    return pl.pallas_call(
        body,
        grid=(2 * steps,),
        in_specs=[
            pl.BlockSpec(memory_space=pltpu.SMEM),
            pl.BlockSpec((tile, width), lambda i: (jnp.minimum(i, steps - 1), 0)),
            pl.BlockSpec((tile, width), lambda i: (jnp.maximum(i - steps, 0), 0)),
            pl.BlockSpec((1, width), lambda i: (0, 0)),
            pl.BlockSpec(weights.shape, lambda i: (0, 0)),
            rows(cosine.shape[1]),
            rows(cosine.shape[1]),
        ],
        out_specs=(
            rows(width),
            rows(q_cols),
            pl.BlockSpec((tile // part, part // 2, 2 * HEAD_SIZE), lambda i: (i, 0, 0)),
        ),
        out_shape=(
            jax.ShapeDtypeStruct((2 * half, width), BF16),
            jax.ShapeDtypeStruct((2 * half, q_cols), BF16),
            jax.ShapeDtypeStruct((2 * half // part, part // 2, 2 * HEAD_SIZE), BF16),
        ),
        compiler_params=kernel_params(),
        cost_estimate=LIGHT,
    )(where, even, odd, gain, weights, cosine, sine)


def stacked(values, heads):
    return jnp.concatenate(
        [values[:, h * HEAD_SIZE : (h + 1) * HEAD_SIZE] for h in range(heads)], axis=0
    )


def side_by_side(values, heads):
    rows = values.shape[0] // heads
    return jnp.concatenate([values[h * rows : (h + 1) * rows] for h in range(heads)], axis=1)


def probabilities(queries, keys, mine, theirs, place, parts, heads):
    rows, length = queries.shape[0] // heads, keys.shape[0]
    part = length // parts
    scores = dot_nt(queries, keys) * HEAD_SIZE**-0.5
    query_at = place * part + lax.broadcasted_iota(jnp.int32, (rows, length), 0)
    key_at = place * part + lax.broadcasted_iota(jnp.int32, (rows, length), 1)
    key_at = jnp.where(key_at >= length, key_at - length, key_at)
    allowed = (key_at <= query_at) & (mine == theirs)
    allowed = jnp.concatenate([allowed] * heads, axis=0)
    scores = jnp.where(allowed, scores, NEG)
    expo = jnp.exp(scores - jnp.max(scores, axis=-1, keepdims=True))
    return expo / jnp.sum(expo, axis=-1, keepdims=True)


def sequence_specs(sequences, part, parts):
    half = sequences // 2
    shape = (1, part // 2, 2 * HEAD_SIZE)
    own = pl.BlockSpec(shape, lambda i: (i, 0, 0))
    came = pl.BlockSpec(shape, lambda i: (lax.rem(i + half, sequences), 0, 0))
    return [own] * parts + [came] * parts


def keys_values(first, refs):
    parts = len(refs) // 2
    own, came = (
        jnp.concatenate([unpack(ref[0]) for ref in half], axis=0) for half in (refs[:parts], refs[parts:])
    )
    return jnp.where(first, own, came), jnp.where(first, came, own)


def attend(where, queries, own, came, mine, theirs):
    parts = len(own)
    sequences, part = own[0].shape[0], 2 * own[0].shape[1]
    rows, columns = queries.shape[0] // sequences, queries.shape[1]
    heads = columns // HEAD_SIZE

    def body(at, q, m, th, *refs):
        keys, values = keys_values(at[1] == 0, refs[:-1])
        probs = probabilities(stacked(q[...], heads), keys, m[0], th[0], at[0], parts, heads)
        refs[-1][...] = side_by_side(dot(probs.astype(BF16), values), heads).astype(BF16)

    return pl.pallas_call(
        body,
        grid=(sequences,),
        in_specs=[
            pl.BlockSpec(memory_space=pltpu.SMEM),
            pl.BlockSpec((rows, columns), lambda i: (i, 0)),
            pl.BlockSpec((1, rows, 1), lambda i: (i, 0, 0)),
            pl.BlockSpec((1, 1, parts * part), lambda i: (i, 0, 0)),
            *sequence_specs(sequences, part, parts),
        ],
        out_specs=pl.BlockSpec((rows, columns), lambda i: (i, 0)),
        out_shape=jax.ShapeDtypeStruct(queries.shape, BF16),
        compiler_params=kernel_params(),
        cost_estimate=LIGHT,
    )(where, queries, mine, theirs, *own, *came)


def attend_back(where, same, other, w_out, queries, own, came, mine, theirs, cosine, sine):
    parts = len(own)
    sequences, part = own[0].shape[0], 2 * own[0].shape[1]
    length = parts * part
    rows, columns = queries.shape[0] // sequences, queries.shape[1]
    heads, half, width = columns // HEAD_SIZE, sequences // 2, same.shape[1]
    packed = parts, part // 2, 2 * HEAD_SIZE
    scale = HEAD_SIZE**-0.5

    def body(at, s, o, w, q, m, th, cs, sn, *refs):
        dq, down, dcame = refs[-3:]
        first = at[1] == 0
        keys, values = keys_values(first, refs[:-3])
        branch = jnp.where(pl.program_id(0) < half, s[...], o[...])
        mixed = stacked(dot_nt(branch, w[...]).astype(BF16), heads)
        stack = stacked(q[...], heads)
        probs = probabilities(stack, keys, m[0], th[0], at[0], parts, heads)
        grad = dot_nt(mixed, values)
        inner = jnp.sum(probs * grad, axis=-1, keepdims=True)
        scores = (probs * (grad - inner)).astype(BF16)
        grad_q = side_by_side(dot(scores, keys) * scale, heads)
        dq[...] = turn(grad_q, widen(cs[...], columns), -widen(sn[...], columns)).astype(BF16)
        grad_k = dot_tn(scores, stack) * scale
        grad_v = dot_tn(probs.astype(BF16), mixed)
        kept, sent = jnp.where(first, grad_k, grad_v), jnp.where(first, grad_v, grad_k)
        for j in range(parts):
            at_rows = slice(j * part, (j + 1) * part)
            down[0, j] = pack(kept[at_rows])
            dcame[0, j] = pack(sent[at_rows]).astype(BF16)

    def strip(size):
        return pl.BlockSpec((rows, size), lambda i: (i, 0))

    return pl.pallas_call(
        body,
        grid=(sequences,),
        in_specs=[
            pl.BlockSpec(memory_space=pltpu.SMEM),
            pl.BlockSpec((rows, width), lambda i: (jnp.minimum(i, half - 1), 0)),
            pl.BlockSpec((rows, width), lambda i: (jnp.maximum(i - half, 0), 0)),
            pl.BlockSpec(w_out.shape, lambda i: (0, 0)),
            strip(columns),
            pl.BlockSpec((1, rows, 1), lambda i: (i, 0, 0)),
            pl.BlockSpec((1, 1, length), lambda i: (i, 0, 0)),
            strip(cosine.shape[1]),
            strip(cosine.shape[1]),
            *sequence_specs(sequences, part, parts),
        ],
        out_specs=(
            strip(columns),
            pl.BlockSpec((1, *packed), lambda i: (i, 0, 0, 0)),
            pl.BlockSpec((1, *packed), lambda i: (lax.rem(i + half, sequences), 0, 0, 0)),
        ),
        out_shape=(
            jax.ShapeDtypeStruct(queries.shape, BF16),
            jax.ShapeDtypeStruct((sequences, *packed), F32),
            jax.ShapeDtypeStruct((sequences, *packed), BF16),
        ),
        compiler_params=kernel_params(),
        cost_estimate=LIGHT,
    )(where, same, other, w_out, queries, mine, theirs, cosine, sine, *own, *came)


def add_parts(kept, came):
    sequences, parts, rows, columns = kept.shape

    def body(a, b, *outs):
        for j, out in enumerate(outs):
            out[...] = (a[:, j] + b[:, j].astype(F32)).astype(out.dtype)

    return pl.pallas_call(
        body,
        out_shape=[
            jax.ShapeDtypeStruct((sequences, rows, columns), BF16 if j else F32)
            for j in range(parts)
        ],
        compiler_params=kernel_params(),
        cost_estimate=LIGHT,
    )(kept, came)


def sum_keys(where, own, came, cosine, sine):
    sequences, rows, _ = own.shape
    count = len(came)

    def body(at, a, cs, sn, *refs):
        total = a[...]
        for ref in refs[:count]:
            total += ref[...].astype(F32)
        out = refs[count]
        for i in range(sequences):
            at_rows = slice(2 * i * rows, 2 * (i + 1) * rows)
            plain = unpack(total[i])
            turned = turn(plain, cs[at_rows, :HEAD_SIZE], -sn[at_rows, :HEAD_SIZE])
            out[at_rows, :] = jnp.where(at[1] == 0, turned, plain).astype(BF16)

    whole = pl.BlockSpec(memory_space=pltpu.VMEM)
    return pl.pallas_call(
        body,
        in_specs=[pl.BlockSpec(memory_space=pltpu.SMEM)] + [whole] * (3 + count),
        out_shape=jax.ShapeDtypeStruct((2 * sequences * rows, HEAD_SIZE), BF16),
        compiler_params=kernel_params(),
        cost_estimate=LIGHT,
    )(where, own, cosine, sine, *came)


def attention_weight_terms(where, first_in, grad_attn, mixed, grad_branch, used, members, parts):
    tokens, width = first_in.shape
    columns, half = mixed.shape[1], mixed.shape[0] // 2
    block, strip = width // (members * parts), width // members
    upper = members // 2

    def body(at, x, g, m, ba, bb, *refs):
        outs, (left, right) = refs[:parts], refs[parts:]
        left[...] = dot_tn(x[...], g[:, : left.shape[1]])
        right[...] = dot_tn(m[:half, :], ba[...]) + dot_tn(m[half:, :], bb[...])
        for j, out in enumerate(outs):
            place = lax.rem(at[0] + j, parts)
            own = right[pl.ds(pl.multiple_of(place * block, block), block), :]

            def both(d):
                rows = pl.ds(pl.multiple_of((d * parts + place) * block, block), block)
                return [left[rows, :][:, :used], own[:, d * strip : (d + 1) * strip]]

            for d in range(upper):
                out[d * block : (d + 1) * block, :] = jnp.concatenate(
                    both(d) + both(d + upper), axis=1
                ).astype(BF16)

    whole = pl.BlockSpec(memory_space=pltpu.VMEM)
    return pl.pallas_call(
        body,
        in_specs=[pl.BlockSpec(memory_space=pltpu.SMEM)] + [whole] * 5,
        out_shape=[jax.ShapeDtypeStruct((upper * block, 2 * (used + strip)), BF16)] * parts,
        scratch_shapes=[
            pltpu.VMEM((width, grad_attn.shape[1]), F32),
            pltpu.VMEM((columns, width), F32),
        ],
        compiler_params=kernel_params(),
        cost_estimate=LIGHT,
    )(where, first_in, grad_attn, mixed, *grad_branch)


def hidden_units(second_in, w_pair):
    tokens, width = second_in.shape
    ff = w_pair.shape[1] // 2
    tile = 256

    def body(x, w, both, hidden):
        product = dot(x[...], w[...])
        gate, up = product[:, :ff], product[:, ff:]
        both[...] = product
        hidden[...] = (gate * jax.nn.sigmoid(gate) * up).astype(BF16)

    def rows(columns):
        return pl.BlockSpec((tile, columns), lambda i: (i, 0))

    return pl.pallas_call(
        body,
        grid=(tokens // tile,),
        in_specs=[rows(width), pl.BlockSpec(w_pair.shape, lambda i: (0, 0), pipeline_mode=pl.Buffered(1))],
        out_specs=(rows(2 * ff), rows(ff)),
        out_shape=(
            jax.ShapeDtypeStruct((tokens, 2 * ff), F32),
            jax.ShapeDtypeStruct((tokens, ff), BF16),
        ),
        compiler_params=kernel_params(),
        cost_estimate=LIGHT,
    )(second_in, w_pair)


def feed_forward_back(both, hidden, grad_out, w_pair, w_down):
    tokens, width = grad_out.shape
    ff = hidden.shape[1]
    tile = 256

    def body(both, h, dy, w, wd, grads, back, forth):
        gate, up = both[:, :ff], both[:, ff:]
        sig = jax.nn.sigmoid(gate)
        forth[...] = dot(h[...], wd[...]).astype(BF16)
        dh_sig = dot_nt(dy[...], wd[...]) * sig
        grad = jnp.concatenate(
            [dh_sig * up * (1.0 + gate * (1.0 - sig)), dh_sig * gate], axis=1
        ).astype(BF16)
        grads[...] = grad
        back[...] = dot_nt(grad, w[...]).astype(BF16)

    def rows(columns):
        return pl.BlockSpec((tile, columns), lambda i: (i, 0))

    def whole(array):
        return pl.BlockSpec(array.shape, lambda i: (0, 0), pipeline_mode=pl.Buffered(1))

    return pl.pallas_call(
        body,
        grid=(tokens // tile,),
        in_specs=[rows(2 * ff), rows(ff), rows(width), whole(w_pair), whole(w_down)],
        out_specs=(rows(2 * ff), rows(width), rows(width)),
        out_shape=(
            jax.ShapeDtypeStruct((tokens, 2 * ff), BF16),
            jax.ShapeDtypeStruct((tokens, width), BF16),
            jax.ShapeDtypeStruct((tokens, width), BF16),
        ),
        compiler_params=kernel_params(),
        cost_estimate=LIGHT,
    )(both, hidden, grad_out, w_pair, w_down)


def add_blocks(own, came, blocks):
    tokens, columns = own.shape[0] // blocks, own.shape[1]

    def body(a, b, *outs):
        for j, out in enumerate(outs):
            rows = pl.ds(j * tokens, tokens)
            out[...] = (a[rows, :].astype(F32) + b[rows, :].astype(F32)).astype(out.dtype)

    return pl.pallas_call(
        body,
        out_shape=[
            jax.ShapeDtypeStruct((tokens, columns), BF16 if j else F32) for j in range(blocks)
        ],
        compiler_params=kernel_params(),
        cost_estimate=LIGHT,
    )(own, came)


def regroup(values, outer, inner):
    part = values.shape[1] // (outer * inner)
    return jnp.concatenate(
        [
            values[:, (o * inner + i) * part : (o * inner + i + 1) * part]
            for i in range(inner)
            for o in range(outer)
        ],
        axis=1,
    )


def second_norm(x, own, sent, gain, outer, inner):
    count = len(sent)

    def body(x, own, gain, *refs):
        resid = x[...].astype(F32) + own[...]
        for ref in refs[:count]:
            resid += ref[...].astype(F32)
        refs[count][...] = resid
        normed = resid * lax.rsqrt(jnp.mean(resid * resid, axis=-1, keepdims=True) + EPS)
        refs[count + 1][...] = regroup((normed * gain[...]).astype(BF16), outer, inner)

    return pl.pallas_call(
        body,
        out_shape=(
            jax.ShapeDtypeStruct(x.shape, F32),
            jax.ShapeDtypeStruct(x.shape, BF16),
        ),
        compiler_params=kernel_params(),
        cost_estimate=LIGHT,
    )(x, own, gain, *sent)


def second_norm_back(resid, own, sent, gain, grad_out, outer, inner):
    count = len(sent)

    def body(resid, own, gain, grad_out, *refs):
        grad = own[...]
        for ref in refs[:count]:
            grad += ref[...].astype(F32)
        grad = regroup(grad, inner, outer)
        rows = resid[...]
        inverse = lax.rsqrt(jnp.mean(rows * rows, axis=-1, keepdims=True) + EPS)
        total = grad_out[...].astype(F32) + norm_back(grad, rows * inverse, inverse, gain[...])
        refs[count][...] = total
        refs[count + 1][...] = total.astype(BF16)

    return pl.pallas_call(
        body,
        out_shape=(
            jax.ShapeDtypeStruct(resid.shape, F32),
            jax.ShapeDtypeStruct(resid.shape, BF16),
        ),
        compiler_params=kernel_params(),
        cost_estimate=LIGHT,
    )(resid, own, gain, grad_out, *sent)


def dot_blocks(left, right, came, blocks, product):
    tokens, columns = came.shape[0] // blocks, came.shape[1]

    def body(a, b, c, *outs):
        for j, out in enumerate(outs):
            rows = pl.ds(j * tokens, tokens)
            out[...] = (product(a[rows, :], b[...]) + c[rows, :].astype(F32)).astype(out.dtype)

    return pl.pallas_call(
        body,
        out_shape=[
            jax.ShapeDtypeStruct((tokens, columns), BF16 if j else F32) for j in range(blocks)
        ],
        compiler_params=kernel_params(),
        cost_estimate=LIGHT,
    )(left, right, came)


def columns_out(gate, up, planes, members):
    rows, ff = gate.shape
    part = ff // (planes * members)

    def body(g, u, o):
        both = g[...], u[...]
        for s in range(members):
            o[s] = jnp.concatenate(
                [
                    v[:, (p * members + s) * part : (p * members + s + 1) * part]
                    for v in both
                    for p in range(planes)
                ],
                axis=1,
            )

    return pl.pallas_call(
        body,
        out_shape=jax.ShapeDtypeStruct((members, rows, 2 * planes * part), gate.dtype),
        compiler_params=kernel_params(),
        cost_estimate=LIGHT,
    )(gate, up)


def gather_terms(own, sums, members, used, width):
    block, count, strip = 2 * own.shape[0] // members, len(sums), width // members

    def body(a, *refs):
        total = a[...].astype(F32)
        for ref in refs[:count]:
            total += ref[...].astype(F32)
        out, payload = refs[count:]
        strips = []
        for d in range(members):
            side, row = divmod(d, members // 2)
            start = side * (used + strip)
            rows = total[row * block : (row + 1) * block]
            payload[d] = rows[:, start : start + used].astype(BF16)
            strips.append(rows[:, start + used : start + used + strip])
        out[...] = jnp.concatenate(strips, axis=1)

    return pl.pallas_call(
        body,
        out_shape=(
            jax.ShapeDtypeStruct((block, width), F32),
            jax.ShapeDtypeStruct((members, block, used), BF16),
        ),
        compiler_params=kernel_params(),
        cost_estimate=LIGHT,
    )(own, *sums)


def weight_gradients(pairs, blocks, weights, gains, q_cols):
    members, rows, _ = blocks.shape
    part, shared = pairs.shape[2] // 2, members // (2 * KEY_VALUE_HEADS)

    def body(pair, x, g, u, q, k, v, gains, og, ou, oq, ok, ov, ogain):
        def side(start, size, chosen, x=x):
            return [x[d, :, start : start + size].astype(F32) for d in chosen]

        def heads(core):
            found = side(q_cols, HEAD_SIZE, range(core, members, 2))
            return jnp.concatenate(
                [sum(found[h * shared : (h + 1) * shared]) for h in range(KEY_VALUE_HEADS)], axis=1
            )

        og[...] = jnp.concatenate(side(0, part, range(members), pair), axis=1)
        ou[...] = jnp.concatenate(side(part, part, range(members), pair), axis=1)
        oq[...] = jnp.concatenate(side(0, q_cols, range(members)), axis=1)
        ok[...] = heads(0)
        ov[...] = heads(1)

        def gain(both):
            return sum(jnp.sum(w[...].astype(F32) * o[...], axis=1, keepdims=True) for w, o in both)

        total = jnp.concatenate([gain(((q, oq), (k, ok), (v, ov))), gain(((g, og), (u, ou)))], axis=1)
        ogain[...] = total / gains[...].astype(F32)

    return pl.pallas_call(
        body,
        out_shape=[jax.ShapeDtypeStruct(w.shape, F32) for w in weights]
        + [jax.ShapeDtypeStruct((rows, 2), F32)],
        compiler_params=kernel_params(),
        cost_estimate=LIGHT,
    )(pairs, blocks, *weights, gains)


def scatter_dp(left, right, size, product):
    came = swap(product(left[left.shape[0] // 2 :], right).astype(BF16), 1)
    return dot_blocks(left, right, came, size // 2, product)


def in_order(parts, place):
    size = len(parts)
    rows, columns = parts[0].shape

    def body(at, *refs):
        for j in range(size):
            refs[-1][pl.ds(lax.rem(at[0] + j, size), 1)] = refs[j][...][None]

    out = pl.pallas_call(
        body,
        in_specs=[pl.BlockSpec(memory_space=pltpu.SMEM)]
        + [pl.BlockSpec(memory_space=pltpu.VMEM)] * size,
        out_shape=jax.ShapeDtypeStruct((size, rows, columns), parts[0].dtype),
        compiler_params=kernel_params(),
        cost_estimate=LIGHT,
    )(jnp.full((1,), place, jnp.int32), *parts)
    return out.reshape(size * rows, columns)


def attention_weights(parts, place, at_gains):
    size = len(parts)
    a, b, m = parts[0].shape
    lanes = at_gains // 128 * 128

    def body(at, *refs):
        out, gains = refs[-2:]
        for j in range(size):
            out[:, pl.ds(lax.rem(at[0] + j, size), 1)] = refs[j][...][:, None]
        strip = out[:, :, :, lanes : lanes + 128].reshape(a * size * b, 128).astype(F32)
        gains[...] = strip.T[at_gains - lanes : at_gains - lanes + 2]

    return pl.pallas_call(
        body,
        in_specs=[pl.BlockSpec(memory_space=pltpu.SMEM)]
        + [pl.BlockSpec(memory_space=pltpu.VMEM)] * size,
        out_shape=(
            jax.ShapeDtypeStruct((a, size, b, m), parts[0].dtype),
            jax.ShapeDtypeStruct((2, a * size * b), F32),
        ),
        compiler_params=kernel_params(),
        cost_estimate=LIGHT,
    )(jnp.full((1,), place, jnp.int32), *parts)


def norm_back(grad_in, normed, inverse, gain):
    grad_normed = grad_in * gain
    return inverse * (
        grad_normed - normed * jnp.mean(grad_normed * normed, axis=-1, keepdims=True)
    )


def per_device(
    n,
    c,
    tokens,
    segment_ids,
    out_grad,
    gain_attn,
    w_query,
    key_weight,
    value_weight,
    w_out,
    gain_mlp,
    w_gate,
    w_up,
    w_down,
):
    t, width = tokens.shape[1:]
    length = segment_ids.shape[1]
    block = w_query.shape[0]
    ff = w_gate.shape[1]
    heads = QUERY_HEADS // n
    group = QUERY_HEADS // KEY_VALUE_HEADS
    q_cols, f_cols = heads * HEAD_SIZE, ff // n
    every_dp = ("plane", "core")
    plane, core, place_z = (lax.axis_index(axis) for axis in ("plane", "core", "ctx"))
    me = 2 * plane + core

    pieces = []
    used = q_cols + HEAD_SIZE
    extras = jnp.concatenate(
        [gain_attn[:, None], gain_mlp[:, None], segment_ids.astype(BF16).reshape(block, -1)], axis=1
    )
    extras = jnp.pad(extras, ((0, 0), (0, -(used + extras.shape[1]) % 128)))
    for d in range(n):
        g = d * heads // group
        kv = value_weight if d % 2 else key_weight
        pieces += [
            w_query[:, d * q_cols : (d + 1) * q_cols],
            kv[:, g * HEAD_SIZE : (g + 1) * HEAD_SIZE],
            extras,
        ]
    w_attn = jnp.concatenate(pieces, axis=1).reshape(block, n, -1).transpose(1, 0, 2)
    w_attn = lax.all_to_all(w_attn, every_dp, 0, 0)
    x16, dy_local = tokens[0], out_grad[0]
    wd = lax.all_gather(w_down, "ctx", axis=0, tiled=True)
    w_attn, wo_parts, same = together(w_attn, shifts(w_out, c), dp_same(x16, n))
    seg_rows = w_attn[:, :, used + 2 : used + 2 + length // block].reshape(n, length)

    order = me ^ jnp.array([*range(0, n, 2), *range(1, n, 2)], jnp.int32)
    pick = (order[:, None] == jnp.arange(n, dtype=jnp.int32)[None]).astype(BF16)
    segs = dot(pick, seg_rows)
    local_idx = place_z * t + jnp.arange(t, dtype=jnp.int32)
    local_seg = lax.dynamic_slice_in_dim(segs, place_z * t, t, axis=1)
    before = jnp.sum((segs[:, None, :] < local_seg[:, :, None]).astype(jnp.int32), axis=2)
    place = (local_idx[None] - before).astype(F32)
    freq = 10000.0 ** (-jnp.arange(HEAD_SIZE // 2, dtype=F32) / (HEAD_SIZE // 2))
    angle = place.reshape(n * t)[:, None] * freq[None, :]
    cosine, sine = jnp.cos(angle), jnp.sin(angle)
    cosine = jnp.concatenate([cosine] * 4, axis=1)
    sine = jnp.concatenate([-sine, sine] * 2, axis=1)
    w_pair = columns_out(*after((w_gate, w_up), w_attn), 1, n)
    w_pair = lax.all_to_all(w_pair, every_dp, 0, 0).reshape(n * block, 2 * f_cols)
    even = jnp.concatenate([x16, *same])
    odd = swap(even, 1)
    w_parts, cosine, sine, w_pair, wd = together(
        shifts(w_attn, c), cosine, sine, w_pair, wd
    )
    w_pair = lax.all_gather(w_pair, "ctx", axis=0, tiled=True)

    w_attn, gains = attention_weights([w_attn, *w_parts], place_z, used)
    w_attn = w_attn.reshape(width, -1)
    gain1, gain2 = gains[:1], gains[1:]
    wo = in_order([w_out, *wo_parts], place_z)
    where = jnp.stack([place_z, core]).astype(jnp.int32)
    key_seg = lax.dynamic_slice_in_dim(
        jnp.concatenate([segs, segs], axis=1), place_z * t, length, axis=1
    )
    sides = local_seg[:, :, None], key_seg[:, None, :]

    first_in, queries, kv_own = project(where, even, odd, gain1, w_attn, cosine, sine, q_cols, t)

    kv_parts, dy_same = together(shifts(kv_own, c), dp_same(after(dy_local, first_in), n))
    dy_same = jnp.concatenate([dy_local, *dy_same])
    dy = dy_same, swap(dy_same, 1)
    kv_all = [kv_own, *kv_parts]
    kv_other = [swap(v, 1) for v in kv_all]
    mixed = attend(where, queries, kv_all, kv_other, *sides)
    attn_own, *sends = scatter_dp(mixed, wo, n, dot)
    sent = together(*[swap(v, 2 * j) for j, v in enumerate(sends, 1)])
    resid, second_in = second_norm(x16, attn_own, sent, gain2, n, c)

    second_in = jnp.concatenate([second_in, *together(*dp_same(second_in, n))])
    second_in = second_in, swap(second_in, 1)
    units = hidden_units(second_in[0], w_pair)
    units = units, hidden_units(after(second_in[1], units), w_pair)
    hidden = [half[1] for half in units]
    down_term = transposed_dot(hidden, dy)
    grad_down = lax.psum_scatter(after(down_term, wd), "ctx", scatter_dimension=0, tiled=True)
    other = feed_forward_back(*units[1], dy[1], w_pair, after(wd, down_term))
    same = feed_forward_back(*units[0], after(dy[0], other[0]), w_pair, wd)
    grad_pair = same[0], other[0]
    back, *sends = add_blocks(same[1], swap(other[1], 1), n // 2)
    forth = swap(after(other[2], sends), 1)
    pair_term = transposed_dot(after(second_in, forth), grad_pair)
    forth, *forth_sends = add_blocks(same[2], forth, n // 2)
    sent, pair_term, forth_sends, grad_down = together(
        [swap(v, 2 * j) for j, v in enumerate(sends, 1)], pair_term, forth_sends, grad_down
    )
    pair_sum = lax.psum_scatter(pair_term, "ctx", scatter_dimension=0, tiled=True)
    grad_resid, branch = second_norm_back(resid, back, sent, gain2, dy_local, n, c)

    same = together(*dp_same(branch, n))
    same = jnp.concatenate([branch, *same])
    grad_branch = same, swap(same, 1)
    grad_q, kept, sent = attend_back(
        where, *grad_branch, wo, queries, kv_all, kv_other, *sides, cosine, sine
    )
    result_parts = [swap(v, 2 * j) for j, v in enumerate(forth_sends, 1)]
    kept, sent, result_parts = together(kept, sent, result_parts)
    own_kv, *kv_sends = add_parts(kept, swap(sent, 1))
    kv_parts = together(*[shift(v, -j, c) for j, v in enumerate(kv_sends, 1)])
    result = resid + forth + sum(v.astype(F32) for v in result_parts)
    grad_kv = sum_keys(where, own_kv, kv_parts, cosine, sine)
    unused = jnp.zeros((n * t, w_attn.shape[1] - used), BF16)
    grad_attn = jnp.concatenate([grad_q, grad_kv, unused], axis=1)
    own_terms, *terms = attention_weight_terms(
        where, first_in, grad_attn, mixed, grad_branch, used, n, c
    )
    first_own, *sends = scatter_dp(after(grad_attn, terms), w_attn, n, dot_nt)
    pair_sum = after(pair_sum, sends).reshape(n, block, 2 * f_cols)
    sent, terms, pair_sum = together(
        [swap(v, 2 * j) for j, v in enumerate(sends, 1)],
        [shift(v, -j, c) for j, v in enumerate(terms, 1)],
        lax.all_to_all(pair_sum, every_dp, 0, 0),
    )
    grad_wout, payload = gather_terms(own_terms, terms, n, used, width)
    payload = lax.all_to_all(payload, every_dp, 0, 0)
    grad_gate, grad_up, grad_query, grad_key, grad_value, grad_gains = weight_gradients(
        pair_sum,
        payload,
        (w_gate, w_up, w_query, key_weight, value_weight),
        jnp.stack([gain_attn, gain_mlp], axis=1),
        q_cols,
    )
    grad_first = first_own + sum(v.astype(F32) for v in sent)
    grad_down = after(grad_down, terms).astype(F32)
    x = x16.astype(F32)
    inverse1 = lax.rsqrt(jnp.mean(x * x, axis=-1, keepdims=True) + EPS)
    grad_input = grad_resid + norm_back(grad_first, x * inverse1, inverse1, gain1)
    return (
        result.astype(BF16)[None],
        grad_input[None],
        grad_gains[:, 0],
        grad_query,
        grad_key,
        grad_value,
        grad_wout,
        grad_gains[:, 1],
        grad_gate,
        grad_up,
        grad_down,
    )


def solution(mesh):
    n, c = mesh.shape["dp"], mesh.shape["ctx"]
    split = Mesh(mesh.devices.reshape(n // 2, 2, c), ("plane", "core", "ctx"))
    dp, every = ("plane", "core"), ("plane", "core", "ctx")
    rows = P(dp, "ctx", None)
    weight, gain = P(every, None), P(every)
    return jax.shard_map(
        functools.partial(per_device, n, c),
        mesh=split,
        in_specs=(rows, P(dp, None), rows, gain, weight, weight, weight, weight, gain)
        + (weight,) * 3,
        out_specs=(rows, rows, gain, weight, weight, weight, weight, gain) + (weight,) * 3,
        check_vma=False,
    )
```

```python
import functools

import jax
import jax.numpy as jnp
from jax import lax
from jax.experimental import pallas as pl
from jax.experimental.pallas import tpu as pltpu
from jax.sharding import Mesh
from jax.sharding import PartitionSpec as P

QUERY_HEADS = 32
KEY_VALUE_HEADS = 4
HEAD_SIZE = 64
EPS = 1e-05
NEG = -1e30
F32 = jnp.float32
BF16 = jnp.bfloat16


def dot(left, right):
    return jnp.dot(left, right, preferred_element_type=F32)


def dot_nt(left, right):
    return lax.dot_general(left, right, (((1,), (1,)), ((), ())), preferred_element_type=F32)


def dot_tn(left, right):
    return lax.dot_general(left, right, (((0,), (0,)), ((), ())), preferred_element_type=F32)


def swap(value, rel):
    size = lax.axis_size(("plane", "core"))
    return lax.ppermute(value, ("plane", "core"), [(i, i ^ rel) for i in range(size)])


def shift(value, step, size):
    return lax.ppermute(value, "ctx", [(i, (i - step) % size) for i in range(size)])


def shifts(value, size):
    return [shift(value, j, size) for j in range(1, size)]


def together(*values):
    return lax.optimization_barrier(values)


def after(value, *earlier):
    return together(value, *earlier)[0]


def dp_same(rows, size):
    return [swap(rows, rel) for rel in range(2, size, 2)]


def kernel_params(mib=32):
    return pltpu.CompilerParams(vmem_limit_bytes=mib * 2**20)

LIGHT = pl.CostEstimate(flops=1024, bytes_accessed=1024, transcendentals=0)


def transposed_dot(lefts, rights):
    tokens, rows = lefts[0].shape
    columns, count = rights[0].shape[1], len(lefts)
    by_rows = rows % 256 == 0 and rows > columns
    row_tile = 256 if by_rows else rows
    column_tile = columns if by_rows or columns % 512 else 512
    moving = pl.BlockSpec((tokens, row_tile if by_rows else column_tile), lambda i: (0, i))
    resting = pl.BlockSpec((tokens, column_tile if by_rows else row_tile), lambda i: (0, 0))

    def body(*refs):
        total = 0.0
        for left, right in zip(refs[:count], refs[count:-1]):
            total += lax.dot_general(
                left[...], right[...], (((0,), (0,)), ((), ())), preferred_element_type=F32
            )
        refs[-1][...] = total.astype(BF16)

    return pl.pallas_call(
        body,
        grid=(rows // row_tile if by_rows else columns // column_tile,),
        in_specs=[moving if by_rows else resting] * count + [resting if by_rows else moving] * count,
        out_specs=pl.BlockSpec(
            (row_tile, column_tile), (lambda i: (i, 0)) if by_rows else (lambda i: (0, i))
        ),
        out_shape=jax.ShapeDtypeStruct((rows, columns), BF16),
        compiler_params=kernel_params(),
        cost_estimate=LIGHT,
    )(*lefts, *rights)


def turn(values, cosine, sine):
    half = HEAD_SIZE // 2
    width = values.shape[1]
    lane = lax.broadcasted_iota(jnp.int32, values.shape, 1)
    up = jnp.concatenate([values[:, half:], values[:, :half]], axis=1)
    down = jnp.concatenate([values[:, width - half :], values[:, : width - half]], axis=1)
    return values * cosine + jnp.where(lane % HEAD_SIZE < half, up, down) * sine


def widen(table, columns):
    return jnp.concatenate([table] * (columns // table.shape[1]), axis=1)


def pack(rows):
    half = rows.shape[0] // 2
    return jnp.concatenate([rows[:half], rows[half:]], axis=1)


def unpack(rows):
    half = rows.shape[1] // 2
    return jnp.concatenate([rows[:, :half], rows[:, half:]], axis=0)


def project(where, even, odd, gain, weights, cosine, sine, q_cols, part):
    half, width = even.shape
    columns = q_cols + HEAD_SIZE
    tile = 256
    steps = half // tile

    def body(at, e, o, gn, w, cs, sn, first, queries, kv):
        x = jnp.where(pl.program_id(0) < steps, e[...], o[...]).astype(F32)
        normed = x * lax.rsqrt(jnp.mean(x * x, axis=-1, keepdims=True) + EPS)
        rows = (normed * gn[...]).astype(BF16)
        first[...] = rows
        raw = dot(rows, w[...])
        queries[...] = turn(
            raw[:, :q_cols], widen(cs[...], q_cols), widen(sn[...], q_cols)
        ).astype(BF16)
        plain = raw[:, q_cols:columns]
        turned = turn(plain, cs[:, :HEAD_SIZE], sn[:, :HEAD_SIZE])
        chosen = jnp.where(at[1] == 0, turned, plain)
        for p in range(tile // part):
            kv[p] = pack(chosen[p * part : (p + 1) * part]).astype(BF16)

    def rows(size):
        return pl.BlockSpec((tile, size), lambda i: (i, 0))

    return pl.pallas_call(
        body,
        grid=(2 * steps,),
        in_specs=[
            pl.BlockSpec(memory_space=pltpu.SMEM),
            pl.BlockSpec((tile, width), lambda i: (jnp.minimum(i, steps - 1), 0)),
            pl.BlockSpec((tile, width), lambda i: (jnp.maximum(i - steps, 0), 0)),
            pl.BlockSpec((1, width), lambda i: (0, 0)),
            pl.BlockSpec(weights.shape, lambda i: (0, 0)),
            rows(cosine.shape[1]),
            rows(cosine.shape[1]),
        ],
        out_specs=(
            rows(width),
            rows(q_cols),
            pl.BlockSpec((tile // part, part // 2, 2 * HEAD_SIZE), lambda i: (i, 0, 0)),
        ),
        out_shape=(
            jax.ShapeDtypeStruct((2 * half, width), BF16),
            jax.ShapeDtypeStruct((2 * half, q_cols), BF16),
            jax.ShapeDtypeStruct((2 * half // part, part // 2, 2 * HEAD_SIZE), BF16),
        ),
        compiler_params=kernel_params(),
        cost_estimate=LIGHT,
    )(where, even, odd, gain, weights, cosine, sine)


def stacked(values, heads):
    return jnp.concatenate(
        [values[:, h * HEAD_SIZE : (h + 1) * HEAD_SIZE] for h in range(heads)], axis=0
    )


def side_by_side(values, heads):
    rows = values.shape[0] // heads
    return jnp.concatenate([values[h * rows : (h + 1) * rows] for h in range(heads)], axis=1)


def probabilities(queries, keys, mine, theirs, place, parts, heads):
    rows, length = queries.shape[0] // heads, keys.shape[0]
    part = length // parts
    scores = dot_nt(queries, keys) * HEAD_SIZE**-0.5
    query_at = place * part + lax.broadcasted_iota(jnp.int32, (rows, length), 0)
    key_at = place * part + lax.broadcasted_iota(jnp.int32, (rows, length), 1)
    key_at = jnp.where(key_at >= length, key_at - length, key_at)
    allowed = (key_at <= query_at) & (mine == theirs)
    allowed = jnp.concatenate([allowed] * heads, axis=0)
    scores = jnp.where(allowed, scores, NEG)
    expo = jnp.exp(scores - jnp.max(scores, axis=-1, keepdims=True))
    return expo / jnp.sum(expo, axis=-1, keepdims=True)


def sequence_specs(sequences, part, parts):
    half = sequences // 2
    shape = (1, part // 2, 2 * HEAD_SIZE)
    own = pl.BlockSpec(shape, lambda i: (i, 0, 0))
    came = pl.BlockSpec(shape, lambda i: (lax.rem(i + half, sequences), 0, 0))
    return [own] * parts + [came] * parts


def keys_values(first, refs):
    parts = len(refs) // 2
    own, came = (
        jnp.concatenate([unpack(ref[0]) for ref in half], axis=0) for half in (refs[:parts], refs[parts:])
    )
    return jnp.where(first, own, came), jnp.where(first, came, own)


def attend(where, queries, own, came, mine, theirs):
    parts = len(own)
    sequences, part = own[0].shape[0], 2 * own[0].shape[1]
    rows, columns = queries.shape[0] // sequences, queries.shape[1]
    heads = columns // HEAD_SIZE

    def body(at, q, m, th, *refs):
        keys, values = keys_values(at[1] == 0, refs[:-1])
        probs = probabilities(stacked(q[...], heads), keys, m[0], th[0], at[0], parts, heads)
        refs[-1][...] = side_by_side(dot(probs.astype(BF16), values), heads).astype(BF16)

    return pl.pallas_call(
        body,
        grid=(sequences,),
        in_specs=[
            pl.BlockSpec(memory_space=pltpu.SMEM),
            pl.BlockSpec((rows, columns), lambda i: (i, 0)),
            pl.BlockSpec((1, rows, 1), lambda i: (i, 0, 0)),
            pl.BlockSpec((1, 1, parts * part), lambda i: (i, 0, 0)),
            *sequence_specs(sequences, part, parts),
        ],
        out_specs=pl.BlockSpec((rows, columns), lambda i: (i, 0)),
        out_shape=jax.ShapeDtypeStruct(queries.shape, BF16),
        compiler_params=kernel_params(),
        cost_estimate=LIGHT,
    )(where, queries, mine, theirs, *own, *came)


def attend_back(where, same, other, w_out, queries, own, came, mine, theirs, cosine, sine):
    parts = len(own)
    sequences, part = own[0].shape[0], 2 * own[0].shape[1]
    length = parts * part
    rows, columns = queries.shape[0] // sequences, queries.shape[1]
    heads, half, width = columns // HEAD_SIZE, sequences // 2, same.shape[1]
    packed = parts, part // 2, 2 * HEAD_SIZE
    scale = HEAD_SIZE**-0.5

    def body(at, s, o, w, q, m, th, cs, sn, *refs):
        dq, down, dcame = refs[-3:]
        first = at[1] == 0
        keys, values = keys_values(first, refs[:-3])
        branch = jnp.where(pl.program_id(0) < half, s[...], o[...])
        mixed = stacked(dot_nt(branch, w[...]).astype(BF16), heads)
        stack = stacked(q[...], heads)
        probs = probabilities(stack, keys, m[0], th[0], at[0], parts, heads)
        grad = dot_nt(mixed, values)
        inner = jnp.sum(probs * grad, axis=-1, keepdims=True)
        scores = (probs * (grad - inner)).astype(BF16)
        grad_q = side_by_side(dot(scores, keys) * scale, heads)
        dq[...] = turn(grad_q, widen(cs[...], columns), -widen(sn[...], columns)).astype(BF16)
        grad_k = dot_tn(scores, stack) * scale
        grad_v = dot_tn(probs.astype(BF16), mixed)
        kept, sent = jnp.where(first, grad_k, grad_v), jnp.where(first, grad_v, grad_k)
        for j in range(parts):
            at_rows = slice(j * part, (j + 1) * part)
            down[0, j] = pack(kept[at_rows])
            dcame[0, j] = pack(sent[at_rows]).astype(BF16)

    def strip(size):
        return pl.BlockSpec((rows, size), lambda i: (i, 0))

    return pl.pallas_call(
        body,
        grid=(sequences,),
        in_specs=[
            pl.BlockSpec(memory_space=pltpu.SMEM),
            pl.BlockSpec((rows, width), lambda i: (jnp.minimum(i, half - 1), 0)),
            pl.BlockSpec((rows, width), lambda i: (jnp.maximum(i - half, 0), 0)),
            pl.BlockSpec(w_out.shape, lambda i: (0, 0)),
            strip(columns),
            pl.BlockSpec((1, rows, 1), lambda i: (i, 0, 0)),
            pl.BlockSpec((1, 1, length), lambda i: (i, 0, 0)),
            strip(cosine.shape[1]),
            strip(cosine.shape[1]),
            *sequence_specs(sequences, part, parts),
        ],
        out_specs=(
            strip(columns),
            pl.BlockSpec((1, *packed), lambda i: (i, 0, 0, 0)),
            pl.BlockSpec((1, *packed), lambda i: (lax.rem(i + half, sequences), 0, 0, 0)),
        ),
        out_shape=(
            jax.ShapeDtypeStruct(queries.shape, BF16),
            jax.ShapeDtypeStruct((sequences, *packed), F32),
            jax.ShapeDtypeStruct((sequences, *packed), BF16),
        ),
        compiler_params=kernel_params(),
        cost_estimate=LIGHT,
    )(where, same, other, w_out, queries, mine, theirs, cosine, sine, *own, *came)


def add_parts(kept, came):
    sequences, parts, rows, columns = kept.shape

    def body(a, b, *outs):
        for j, out in enumerate(outs):
            out[...] = (a[:, j] + b[:, j].astype(F32)).astype(out.dtype)

    return pl.pallas_call(
        body,
        out_shape=[
            jax.ShapeDtypeStruct((sequences, rows, columns), BF16 if j else F32)
            for j in range(parts)
        ],
        compiler_params=kernel_params(),
        cost_estimate=LIGHT,
    )(kept, came)


def sum_keys(where, own, came, cosine, sine):
    sequences, rows, _ = own.shape
    count = len(came)

    def body(at, a, cs, sn, *refs):
        total = a[...]
        for ref in refs[:count]:
            total += ref[...].astype(F32)
        out = refs[count]
        for i in range(sequences):
            at_rows = slice(2 * i * rows, 2 * (i + 1) * rows)
            plain = unpack(total[i])
            turned = turn(plain, cs[at_rows, :HEAD_SIZE], -sn[at_rows, :HEAD_SIZE])
            out[at_rows, :] = jnp.where(at[1] == 0, turned, plain).astype(BF16)

    whole = pl.BlockSpec(memory_space=pltpu.VMEM)
    return pl.pallas_call(
        body,
        in_specs=[pl.BlockSpec(memory_space=pltpu.SMEM)] + [whole] * (3 + count),
        out_shape=jax.ShapeDtypeStruct((2 * sequences * rows, HEAD_SIZE), BF16),
        compiler_params=kernel_params(),
        cost_estimate=LIGHT,
    )(where, own, cosine, sine, *came)


def attention_weight_terms(where, first_in, grad_attn, mixed, grad_branch, used, members, parts):
    tokens, width = first_in.shape
    columns, half = mixed.shape[1], mixed.shape[0] // 2
    block, strip = width // (members * parts), width // members
    upper = members // 2

    def body(at, x, g, m, ba, bb, *refs):
        outs, (left, right) = refs[:parts], refs[parts:]
        left[...] = dot_tn(x[...], g[:, : left.shape[1]])
        right[...] = dot_tn(m[:half, :], ba[...]) + dot_tn(m[half:, :], bb[...])
        for j, out in enumerate(outs):
            place = lax.rem(at[0] + j, parts)
            own = right[pl.ds(pl.multiple_of(place * block, block), block), :]

            def both(d):
                rows = pl.ds(pl.multiple_of((d * parts + place) * block, block), block)
                return [left[rows, :][:, :used], own[:, d * strip : (d + 1) * strip]]

            for d in range(upper):
                out[d * block : (d + 1) * block, :] = jnp.concatenate(
                    both(d) + both(d + upper), axis=1
                ).astype(BF16)

    whole = pl.BlockSpec(memory_space=pltpu.VMEM)
    return pl.pallas_call(
        body,
        in_specs=[pl.BlockSpec(memory_space=pltpu.SMEM)] + [whole] * 5,
        out_shape=[jax.ShapeDtypeStruct((upper * block, 2 * (used + strip)), BF16)] * parts,
        scratch_shapes=[
            pltpu.VMEM((width, grad_attn.shape[1]), F32),
            pltpu.VMEM((columns, width), F32),
        ],
        compiler_params=kernel_params(),
        cost_estimate=LIGHT,
    )(where, first_in, grad_attn, mixed, *grad_branch)


def hidden_units(second_in, w_pair):
    tokens, width = second_in.shape
    ff = w_pair.shape[1] // 2
    tile = 256

    def body(x, w, both, hidden):
        product = dot(x[...], w[...])
        gate, up = product[:, :ff], product[:, ff:]
        both[...] = product
        hidden[...] = (gate * jax.nn.sigmoid(gate) * up).astype(BF16)

    def rows(columns):
        return pl.BlockSpec((tile, columns), lambda i: (i, 0))

    return pl.pallas_call(
        body,
        grid=(tokens // tile,),
        in_specs=[rows(width), pl.BlockSpec(w_pair.shape, lambda i: (0, 0), pipeline_mode=pl.Buffered(1))],
        out_specs=(rows(2 * ff), rows(ff)),
        out_shape=(
            jax.ShapeDtypeStruct((tokens, 2 * ff), F32),
            jax.ShapeDtypeStruct((tokens, ff), BF16),
        ),
        compiler_params=kernel_params(),
        cost_estimate=LIGHT,
    )(second_in, w_pair)


def feed_forward_back(both, hidden, grad_out, w_pair, w_down):
    tokens, width = grad_out.shape
    ff = hidden.shape[1]
    tile = 256

    def body(both, h, dy, w, wd, grads, back, forth):
        gate, up = both[:, :ff], both[:, ff:]
        sig = jax.nn.sigmoid(gate)
        forth[...] = dot(h[...], wd[...]).astype(BF16)
        dh_sig = dot_nt(dy[...], wd[...]) * sig
        grad = jnp.concatenate(
            [dh_sig * up * (1.0 + gate * (1.0 - sig)), dh_sig * gate], axis=1
        ).astype(BF16)
        grads[...] = grad
        back[...] = dot_nt(grad, w[...]).astype(BF16)

    def rows(columns):
        return pl.BlockSpec((tile, columns), lambda i: (i, 0))

    def whole(array):
        return pl.BlockSpec(array.shape, lambda i: (0, 0), pipeline_mode=pl.Buffered(1))

    return pl.pallas_call(
        body,
        grid=(tokens // tile,),
        in_specs=[rows(2 * ff), rows(ff), rows(width), whole(w_pair), whole(w_down)],
        out_specs=(rows(2 * ff), rows(width), rows(width)),
        out_shape=(
            jax.ShapeDtypeStruct((tokens, 2 * ff), BF16),
            jax.ShapeDtypeStruct((tokens, width), BF16),
            jax.ShapeDtypeStruct((tokens, width), BF16),
        ),
        compiler_params=kernel_params(),
        cost_estimate=LIGHT,
    )(both, hidden, grad_out, w_pair, w_down)


def add_blocks(own, came, blocks):
    tokens, columns = own.shape[0] // blocks, own.shape[1]

    def body(a, b, *outs):
        for j, out in enumerate(outs):
            rows = pl.ds(j * tokens, tokens)
            out[...] = (a[rows, :].astype(F32) + b[rows, :].astype(F32)).astype(out.dtype)

    return pl.pallas_call(
        body,
        out_shape=[
            jax.ShapeDtypeStruct((tokens, columns), BF16 if j else F32) for j in range(blocks)
        ],
        compiler_params=kernel_params(),
        cost_estimate=LIGHT,
    )(own, came)


def regroup(values, outer, inner):
    part = values.shape[1] // (outer * inner)
    return jnp.concatenate(
        [
            values[:, (o * inner + i) * part : (o * inner + i + 1) * part]
            for i in range(inner)
            for o in range(outer)
        ],
        axis=1,
    )


def second_norm(x, own, sent, gain, outer, inner):
    count = len(sent)

    def body(x, own, gain, *refs):
        resid = x[...].astype(F32) + own[...]
        for ref in refs[:count]:
            resid += ref[...].astype(F32)
        refs[count][...] = resid
        normed = resid * lax.rsqrt(jnp.mean(resid * resid, axis=-1, keepdims=True) + EPS)
        refs[count + 1][...] = regroup((normed * gain[...]).astype(BF16), outer, inner)

    return pl.pallas_call(
        body,
        out_shape=(
            jax.ShapeDtypeStruct(x.shape, F32),
            jax.ShapeDtypeStruct(x.shape, BF16),
        ),
        compiler_params=kernel_params(),
        cost_estimate=LIGHT,
    )(x, own, gain, *sent)


def second_norm_back(resid, own, sent, gain, grad_out, outer, inner):
    count = len(sent)

    def body(resid, own, gain, grad_out, *refs):
        grad = own[...]
        for ref in refs[:count]:
            grad += ref[...].astype(F32)
        grad = regroup(grad, inner, outer)
        rows = resid[...]
        inverse = lax.rsqrt(jnp.mean(rows * rows, axis=-1, keepdims=True) + EPS)
        total = grad_out[...].astype(F32) + norm_back(grad, rows * inverse, inverse, gain[...])
        refs[count][...] = total
        refs[count + 1][...] = total.astype(BF16)

    return pl.pallas_call(
        body,
        out_shape=(
            jax.ShapeDtypeStruct(resid.shape, F32),
            jax.ShapeDtypeStruct(resid.shape, BF16),
        ),
        compiler_params=kernel_params(),
        cost_estimate=LIGHT,
    )(resid, own, gain, grad_out, *sent)


def dot_blocks(left, right, came, blocks, product):
    tokens, columns = came.shape[0] // blocks, came.shape[1]

    def body(a, b, c, *outs):
        for j, out in enumerate(outs):
            rows = pl.ds(j * tokens, tokens)
            out[...] = (product(a[rows, :], b[...]) + c[rows, :].astype(F32)).astype(out.dtype)

    return pl.pallas_call(
        body,
        out_shape=[
            jax.ShapeDtypeStruct((tokens, columns), BF16 if j else F32) for j in range(blocks)
        ],
        compiler_params=kernel_params(),
        cost_estimate=LIGHT,
    )(left, right, came)


def columns_out(gate, up, planes, members):
    rows, ff = gate.shape
    part = ff // (planes * members)

    def body(g, u, o):
        both = g[...], u[...]
        for s in range(members):
            o[s] = jnp.concatenate(
                [
                    v[:, (p * members + s) * part : (p * members + s + 1) * part]
                    for v in both
                    for p in range(planes)
                ],
                axis=1,
            )

    return pl.pallas_call(
        body,
        out_shape=jax.ShapeDtypeStruct((members, rows, 2 * planes * part), gate.dtype),
        compiler_params=kernel_params(),
        cost_estimate=LIGHT,
    )(gate, up)


def gather_terms(own, sums, members, used, width):
    block, count, strip = 2 * own.shape[0] // members, len(sums), width // members

    def body(a, *refs):
        total = a[...].astype(F32)
        for ref in refs[:count]:
            total += ref[...].astype(F32)
        out, payload = refs[count:]
        strips = []
        for d in range(members):
            side, row = divmod(d, members // 2)
            start = side * (used + strip)
            rows = total[row * block : (row + 1) * block]
            payload[d] = rows[:, start : start + used].astype(BF16)
            strips.append(rows[:, start + used : start + used + strip])
        out[...] = jnp.concatenate(strips, axis=1)

    return pl.pallas_call(
        body,
        out_shape=(
            jax.ShapeDtypeStruct((block, width), F32),
            jax.ShapeDtypeStruct((members, block, used), BF16),
        ),
        compiler_params=kernel_params(),
        cost_estimate=LIGHT,
    )(own, *sums)


def weight_gradients(pairs, blocks, weights, gains, q_cols):
    members, rows, _ = blocks.shape
    part, shared = pairs.shape[2] // 2, members // (2 * KEY_VALUE_HEADS)

    def body(pair, x, g, u, q, k, v, gains, og, ou, oq, ok, ov, ogain):
        def side(start, size, chosen, x=x):
            return [x[d, :, start : start + size].astype(F32) for d in chosen]

        def heads(core):
            found = side(q_cols, HEAD_SIZE, range(core, members, 2))
            return jnp.concatenate(
                [sum(found[h * shared : (h + 1) * shared]) for h in range(KEY_VALUE_HEADS)], axis=1
            )

        og[...] = jnp.concatenate(side(0, part, range(members), pair), axis=1)
        ou[...] = jnp.concatenate(side(part, part, range(members), pair), axis=1)
        oq[...] = jnp.concatenate(side(0, q_cols, range(members)), axis=1)
        ok[...] = heads(0)
        ov[...] = heads(1)

        def gain(both):
            return sum(jnp.sum(w[...].astype(F32) * o[...], axis=1, keepdims=True) for w, o in both)

        total = jnp.concatenate([gain(((q, oq), (k, ok), (v, ov))), gain(((g, og), (u, ou)))], axis=1)
        ogain[...] = total / gains[...].astype(F32)

    return pl.pallas_call(
        body,
        out_shape=[jax.ShapeDtypeStruct(w.shape, F32) for w in weights]
        + [jax.ShapeDtypeStruct((rows, 2), F32)],
        compiler_params=kernel_params(),
        cost_estimate=LIGHT,
    )(pairs, blocks, *weights, gains)


def stack_rows(parts):
    rows, columns = parts[0].shape

    def body(*refs):
        for j, ref in enumerate(refs[:-1]):
            refs[-1][j * rows : (j + 1) * rows, :] = ref[...]

    return pl.pallas_call(
        body,
        out_shape=jax.ShapeDtypeStruct((len(parts) * rows, columns), parts[0].dtype),
        compiler_params=kernel_params(),
        cost_estimate=LIGHT,
    )(*parts)


def scatter_dp(left, right, size, product):
    came = swap(product(left[left.shape[0] // 2 :], right).astype(BF16), 1)
    return dot_blocks(left, right, came, size // 2, product)


def in_order(parts, place):
    size = len(parts)
    rows, columns = parts[0].shape

    def body(at, *refs):
        for j in range(size):
            refs[-1][pl.ds(lax.rem(at[0] + j, size), 1)] = refs[j][...][None]

    out = pl.pallas_call(
        body,
        in_specs=[pl.BlockSpec(memory_space=pltpu.SMEM)]
        + [pl.BlockSpec(memory_space=pltpu.VMEM)] * size,
        out_shape=jax.ShapeDtypeStruct((size, rows, columns), parts[0].dtype),
        compiler_params=kernel_params(),
        cost_estimate=LIGHT,
    )(jnp.full((1,), place, jnp.int32), *parts)
    return out.reshape(size * rows, columns)


def attention_weights(parts, place, at_gains):
    size = len(parts)
    a, b, m = parts[0].shape
    lanes = at_gains // 128 * 128

    def body(at, *refs):
        out, gains = refs[-2:]
        for j in range(size):
            out[:, pl.ds(lax.rem(at[0] + j, size), 1)] = refs[j][...][:, None]
        strip = out[:, :, :, lanes : lanes + 128].reshape(a * size * b, 128).astype(F32)
        gains[...] = strip.T[at_gains - lanes : at_gains - lanes + 2]

    return pl.pallas_call(
        body,
        in_specs=[pl.BlockSpec(memory_space=pltpu.SMEM)]
        + [pl.BlockSpec(memory_space=pltpu.VMEM)] * size,
        out_shape=(
            jax.ShapeDtypeStruct((a, size, b, m), parts[0].dtype),
            jax.ShapeDtypeStruct((2, a * size * b), F32),
        ),
        compiler_params=kernel_params(),
        cost_estimate=LIGHT,
    )(jnp.full((1,), place, jnp.int32), *parts)


def norm_back(grad_in, normed, inverse, gain):
    grad_normed = grad_in * gain
    return inverse * (
        grad_normed - normed * jnp.mean(grad_normed * normed, axis=-1, keepdims=True)
    )


def per_device(
    n,
    c,
    tokens,
    segment_ids,
    out_grad,
    gain_attn,
    w_query,
    key_weight,
    value_weight,
    w_out,
    gain_mlp,
    w_gate,
    w_up,
    w_down,
):
    t, width = tokens.shape[1:]
    length = segment_ids.shape[1]
    block = w_query.shape[0]
    ff = w_gate.shape[1]
    heads = QUERY_HEADS // n
    group = QUERY_HEADS // KEY_VALUE_HEADS
    q_cols, f_cols = heads * HEAD_SIZE, ff // n
    every_dp = ("plane", "core")
    plane, core, place_z = (lax.axis_index(axis) for axis in ("plane", "core", "ctx"))
    me = 2 * plane + core

    pieces = []
    used = q_cols + HEAD_SIZE
    extras = jnp.concatenate(
        [gain_attn[:, None], gain_mlp[:, None], segment_ids.astype(BF16).reshape(block, -1)], axis=1
    )
    extras = jnp.pad(extras, ((0, 0), (0, -(used + extras.shape[1]) % 128)))
    for d in range(n):
        g = d * heads // group
        kv = value_weight if d % 2 else key_weight
        pieces += [
            w_query[:, d * q_cols : (d + 1) * q_cols],
            kv[:, g * HEAD_SIZE : (g + 1) * HEAD_SIZE],
            extras,
        ]
    w_attn = jnp.concatenate(pieces, axis=1).reshape(block, n, -1).transpose(1, 0, 2)
    w_attn = lax.all_to_all(w_attn, every_dp, 0, 0)
    x16, dy_local = tokens[0], out_grad[0]
    wd = lax.all_gather(w_down, "ctx", axis=0, tiled=True)
    w_attn, wo_parts, same = together(w_attn, shifts(w_out, c), dp_same(x16, n))
    seg_rows = w_attn[:, :, used + 2 : used + 2 + length // block].reshape(n, length)

    order = me ^ jnp.array([*range(0, n, 2), *range(1, n, 2)], jnp.int32)
    pick = (order[:, None] == jnp.arange(n, dtype=jnp.int32)[None]).astype(BF16)
    segs = dot(pick, seg_rows)
    local_idx = place_z * t + jnp.arange(t, dtype=jnp.int32)
    local_seg = lax.dynamic_slice_in_dim(segs, place_z * t, t, axis=1)
    before = jnp.sum((segs[:, None, :] < local_seg[:, :, None]).astype(jnp.int32), axis=2)
    place = (local_idx[None] - before).astype(F32)
    freq = 10000.0 ** (-jnp.arange(HEAD_SIZE // 2, dtype=F32) / (HEAD_SIZE // 2))
    angle = place.reshape(n * t)[:, None] * freq[None, :]
    cosine, sine = jnp.cos(angle), jnp.sin(angle)
    cosine = jnp.concatenate([cosine] * 4, axis=1)
    sine = jnp.concatenate([-sine, sine] * 2, axis=1)
    w_pair = columns_out(*after((w_gate, w_up), w_attn), 1, n)
    w_pair = lax.all_to_all(w_pair, every_dp, 0, 0).reshape(n * block, 2 * f_cols)
    even = jnp.concatenate([x16, *same])
    odd = swap(even, 1)
    wo = in_order([w_out, *wo_parts], place_z)
    w_parts, cosine, sine, w_pair, wd, wo = together(
        shifts(w_attn, c), cosine, sine, w_pair, wd, wo
    )
    w_pair = lax.all_gather(w_pair, "ctx", axis=0, tiled=True)

    w_attn, gains = attention_weights([w_attn, *w_parts], place_z, used)
    w_attn = w_attn.reshape(width, -1)
    gain1, gain2 = gains[:1], gains[1:]
    where = jnp.stack([place_z, core]).astype(jnp.int32)
    key_seg = lax.dynamic_slice_in_dim(
        jnp.concatenate([segs, segs], axis=1), place_z * t, length, axis=1
    )
    sides = local_seg[:, :, None], key_seg[:, None, :]

    first_in, queries, kv_own = project(where, even, odd, gain1, w_attn, cosine, sine, q_cols, t)

    kv_parts, dy_same = together(shifts(kv_own, c), dp_same(after(dy_local, first_in), n))
    dy_same = jnp.concatenate([dy_local, *dy_same])
    dy = dy_same, swap(dy_same, 1)
    kv_all = [kv_own, *kv_parts]
    kv_other = [swap(v, 1) for v in kv_all]
    mixed = attend(where, queries, kv_all, kv_other, *sides)
    attn_own, *sends = scatter_dp(mixed, wo, n, dot)
    sent = together(*[swap(v, 2 * j) for j, v in enumerate(sends, 1)])
    resid, second_in = second_norm(x16, attn_own, sent, gain2, n, c)

    second_in = stack_rows([second_in, *together(*dp_same(second_in, n))])
    second_in = second_in, swap(second_in, 1)
    units = hidden_units(second_in[0], w_pair)
    units = units, hidden_units(after(second_in[1], units), w_pair)
    hidden = [half[1] for half in units]
    down_term = transposed_dot(hidden, dy)
    grad_down = lax.psum_scatter(after(down_term, wd), "ctx", scatter_dimension=0, tiled=True)
    other = feed_forward_back(*units[1], dy[1], w_pair, after(wd, down_term))
    same = feed_forward_back(*units[0], after(dy[0], other[0]), w_pair, wd)
    grad_pair = same[0], other[0]
    back, *sends = add_blocks(same[1], swap(other[1], 1), n // 2)
    forth = swap(after(other[2], sends), 1)
    pair_term = transposed_dot(after(second_in, forth), grad_pair)
    forth, *forth_sends = add_blocks(same[2], forth, n // 2)
    sent, pair_term, forth_sends, grad_down = together(
        [swap(v, 2 * j) for j, v in enumerate(sends, 1)], pair_term, forth_sends, grad_down
    )
    pair_sum = lax.psum_scatter(pair_term, "ctx", scatter_dimension=0, tiled=True)
    grad_resid, branch = second_norm_back(resid, back, sent, gain2, dy_local, n, c)

    same = together(*dp_same(branch, n))
    same = stack_rows([branch, *same])
    grad_branch = same, swap(same, 1)
    grad_q, kept, sent = attend_back(
        where, *grad_branch, wo, queries, kv_all, kv_other, *sides, cosine, sine
    )
    result_parts = [swap(v, 2 * j) for j, v in enumerate(forth_sends, 1)]
    kept, sent, result_parts = together(kept, sent, result_parts)
    own_kv, *kv_sends = add_parts(kept, swap(sent, 1))
    kv_parts = together(*[shift(v, -j, c) for j, v in enumerate(kv_sends, 1)])
    result = resid + forth + sum(v.astype(F32) for v in result_parts)
    grad_kv = sum_keys(where, own_kv, kv_parts, cosine, sine)
    unused = jnp.zeros((n * t, w_attn.shape[1] - used), BF16)
    grad_attn = jnp.concatenate([grad_q, grad_kv, unused], axis=1)
    own_terms, *terms = attention_weight_terms(
        where, first_in, grad_attn, mixed, grad_branch, used, n, c
    )
    first_own, *sends = scatter_dp(after(grad_attn, terms), w_attn, n, dot_nt)
    pair_sum = after(pair_sum, sends).reshape(n, block, 2 * f_cols)
    sent, terms, pair_sum = together(
        [swap(v, 2 * j) for j, v in enumerate(sends, 1)],
        [shift(v, -j, c) for j, v in enumerate(terms, 1)],
        lax.all_to_all(pair_sum, every_dp, 0, 0),
    )
    grad_wout, payload = gather_terms(own_terms, terms, n, used, width)
    payload = lax.all_to_all(payload, every_dp, 0, 0)
    grad_gate, grad_up, grad_query, grad_key, grad_value, grad_gains = weight_gradients(
        pair_sum,
        payload,
        (w_gate, w_up, w_query, key_weight, value_weight),
        jnp.stack([gain_attn, gain_mlp], axis=1),
        q_cols,
    )
    grad_first = first_own + sum(v.astype(F32) for v in sent)
    grad_down = after(grad_down, terms).astype(F32)
    x = x16.astype(F32)
    inverse1 = lax.rsqrt(jnp.mean(x * x, axis=-1, keepdims=True) + EPS)
    grad_input = grad_resid + norm_back(grad_first, x * inverse1, inverse1, gain1)
    return (
        result.astype(BF16)[None],
        grad_input[None],
        grad_gains[:, 0],
        grad_query,
        grad_key,
        grad_value,
        grad_wout,
        grad_gains[:, 1],
        grad_gate,
        grad_up,
        grad_down,
    )


def solution(mesh):
    n, c = mesh.shape["dp"], mesh.shape["ctx"]
    split = Mesh(mesh.devices.reshape(n // 2, 2, c), ("plane", "core", "ctx"))
    dp, every = ("plane", "core"), ("plane", "core", "ctx")
    rows = P(dp, "ctx", None)
    weight, gain = P(every, None), P(every)
    return jax.shard_map(
        functools.partial(per_device, n, c),
        mesh=split,
        in_specs=(rows, P(dp, None), rows, gain, weight, weight, weight, weight, gain)
        + (weight,) * 3,
        out_specs=(rows, rows, gain, weight, weight, weight, weight, gain) + (weight,) * 3,
        check_vma=False,
    )
```

```python
import functools

import jax
import jax.numpy as jnp
from jax import lax
from jax.experimental import pallas as pl
from jax.experimental.pallas import tpu as pltpu
from jax.sharding import Mesh
from jax.sharding import PartitionSpec as P

QUERY_HEADS = 32
KEY_VALUE_HEADS = 4
HEAD_SIZE = 64
EPS = 1e-05
NEG = -1e30
F32 = jnp.float32
BF16 = jnp.bfloat16


def dot(left, right):
    return jnp.dot(left, right, preferred_element_type=F32)


def dot_nt(left, right):
    return lax.dot_general(left, right, (((1,), (1,)), ((), ())), preferred_element_type=F32)


def dot_tn(left, right):
    return lax.dot_general(left, right, (((0,), (0,)), ((), ())), preferred_element_type=F32)


def swap(value, rel):
    size = lax.axis_size(("plane", "core"))
    return lax.ppermute(value, ("plane", "core"), [(i, i ^ rel) for i in range(size)])


def shift(value, step, size):
    return lax.ppermute(value, "ctx", [(i, (i - step) % size) for i in range(size)])


def shifts(value, size):
    return [shift(value, j, size) for j in range(1, size)]


def together(*values):
    return lax.optimization_barrier(values)


def after(value, *earlier):
    return together(value, *earlier)[0]


def dp_same(rows, size):
    return [swap(rows, rel) for rel in range(2, size, 2)]


def kernel_params(mib=32):
    return pltpu.CompilerParams(vmem_limit_bytes=mib * 2**20)

LIGHT = pl.CostEstimate(flops=1024, bytes_accessed=1024, transcendentals=0)


def transposed_dot(lefts, rights):
    tokens, rows = lefts[0].shape
    columns, count = rights[0].shape[1], len(lefts)
    by_rows = rows % 256 == 0 and rows > columns
    row_tile = 256 if by_rows else rows
    column_tile = columns if by_rows or columns % 512 else 512
    moving = pl.BlockSpec((tokens, row_tile if by_rows else column_tile), lambda i: (0, i))
    resting = pl.BlockSpec((tokens, column_tile if by_rows else row_tile), lambda i: (0, 0))

    def body(*refs):
        total = 0.0
        for left, right in zip(refs[:count], refs[count:-1]):
            total += lax.dot_general(
                left[...], right[...], (((0,), (0,)), ((), ())), preferred_element_type=F32
            )
        refs[-1][...] = total.astype(BF16)

    return pl.pallas_call(
        body,
        grid=(rows // row_tile if by_rows else columns // column_tile,),
        in_specs=[moving if by_rows else resting] * count + [resting if by_rows else moving] * count,
        out_specs=pl.BlockSpec(
            (row_tile, column_tile), (lambda i: (i, 0)) if by_rows else (lambda i: (0, i))
        ),
        out_shape=jax.ShapeDtypeStruct((rows, columns), BF16),
        compiler_params=kernel_params(),
        cost_estimate=LIGHT,
    )(*lefts, *rights)


def turn(values, cosine, sine):
    half = HEAD_SIZE // 2
    width = values.shape[1]
    lane = lax.broadcasted_iota(jnp.int32, values.shape, 1)
    up = jnp.concatenate([values[:, half:], values[:, :half]], axis=1)
    down = jnp.concatenate([values[:, width - half :], values[:, : width - half]], axis=1)
    return values * cosine + jnp.where(lane % HEAD_SIZE < half, up, down) * sine


def widen(table, columns):
    return jnp.concatenate([table] * (columns // table.shape[1]), axis=1)


def pack(rows):
    half = rows.shape[0] // 2
    return jnp.concatenate([rows[:half], rows[half:]], axis=1)


def unpack(rows):
    half = rows.shape[1] // 2
    return jnp.concatenate([rows[:, :half], rows[:, half:]], axis=0)


def project(where, even, odd, gain, weights, cosine, sine, q_cols, part):
    half, width = even.shape
    columns = q_cols + HEAD_SIZE
    tile = 256
    steps = half // tile

    def body(at, e, o, gn, w, cs, sn, first, queries, kv):
        x = jnp.where(pl.program_id(0) < steps, e[...], o[...]).astype(F32)
        normed = x * lax.rsqrt(jnp.mean(x * x, axis=-1, keepdims=True) + EPS)
        rows = (normed * gn[...]).astype(BF16)
        first[...] = rows
        raw = dot(rows, w[...])
        queries[...] = turn(
            raw[:, :q_cols], widen(cs[...], q_cols), widen(sn[...], q_cols)
        ).astype(BF16)
        plain = raw[:, q_cols:columns]
        turned = turn(plain, cs[:, :HEAD_SIZE], sn[:, :HEAD_SIZE])
        chosen = jnp.where(at[1] == 0, turned, plain)
        for p in range(tile // part):
            kv[p] = pack(chosen[p * part : (p + 1) * part]).astype(BF16)

    def rows(size):
        return pl.BlockSpec((tile, size), lambda i: (i, 0))

    return pl.pallas_call(
        body,
        grid=(2 * steps,),
        in_specs=[
            pl.BlockSpec(memory_space=pltpu.SMEM),
            pl.BlockSpec((tile, width), lambda i: (jnp.minimum(i, steps - 1), 0)),
            pl.BlockSpec((tile, width), lambda i: (jnp.maximum(i - steps, 0), 0)),
            pl.BlockSpec((1, width), lambda i: (0, 0)),
            pl.BlockSpec(weights.shape, lambda i: (0, 0)),
            rows(cosine.shape[1]),
            rows(cosine.shape[1]),
        ],
        out_specs=(
            rows(width),
            rows(q_cols),
            pl.BlockSpec((tile // part, part // 2, 2 * HEAD_SIZE), lambda i: (i, 0, 0)),
        ),
        out_shape=(
            jax.ShapeDtypeStruct((2 * half, width), BF16),
            jax.ShapeDtypeStruct((2 * half, q_cols), BF16),
            jax.ShapeDtypeStruct((2 * half // part, part // 2, 2 * HEAD_SIZE), BF16),
        ),
        compiler_params=kernel_params(),
        cost_estimate=LIGHT,
    )(where, even, odd, gain, weights, cosine, sine)


def stacked(values, heads):
    return jnp.concatenate(
        [values[:, h * HEAD_SIZE : (h + 1) * HEAD_SIZE] for h in range(heads)], axis=0
    )


def side_by_side(values, heads):
    rows = values.shape[0] // heads
    return jnp.concatenate([values[h * rows : (h + 1) * rows] for h in range(heads)], axis=1)


def probabilities(queries, keys, mine, theirs, place, parts, heads):
    rows, length = queries.shape[0] // heads, keys.shape[0]
    part = length // parts
    scores = dot_nt(queries, keys) * HEAD_SIZE**-0.5
    query_at = place * part + lax.broadcasted_iota(jnp.int32, (rows, length), 0)
    key_at = place * part + lax.broadcasted_iota(jnp.int32, (rows, length), 1)
    key_at = jnp.where(key_at >= length, key_at - length, key_at)
    allowed = (key_at <= query_at) & (mine == theirs)
    allowed = jnp.concatenate([allowed] * heads, axis=0)
    scores = jnp.where(allowed, scores, NEG)
    expo = jnp.exp(scores - jnp.max(scores, axis=-1, keepdims=True))
    return expo / jnp.sum(expo, axis=-1, keepdims=True)


def sequence_specs(sequences, part, parts):
    half = sequences // 2
    shape = (1, part // 2, 2 * HEAD_SIZE)
    own = pl.BlockSpec(shape, lambda i: (i, 0, 0))
    came = pl.BlockSpec(shape, lambda i: (lax.rem(i + half, sequences), 0, 0))
    return [own] * parts + [came] * parts


def keys_values(first, refs):
    parts = len(refs) // 2
    own, came = (
        jnp.concatenate([unpack(ref[0]) for ref in half], axis=0) for half in (refs[:parts], refs[parts:])
    )
    return jnp.where(first, own, came), jnp.where(first, came, own)


def attend(where, queries, own, came, mine, theirs):
    parts = len(own)
    sequences, part = own[0].shape[0], 2 * own[0].shape[1]
    rows, columns = queries.shape[0] // sequences, queries.shape[1]
    heads = columns // HEAD_SIZE

    def body(at, q, m, th, *refs):
        keys, values = keys_values(at[1] == 0, refs[:-1])
        probs = probabilities(stacked(q[...], heads), keys, m[0], th[0], at[0], parts, heads)
        refs[-1][...] = side_by_side(dot(probs.astype(BF16), values), heads).astype(BF16)

    return pl.pallas_call(
        body,
        grid=(sequences,),
        in_specs=[
            pl.BlockSpec(memory_space=pltpu.SMEM),
            pl.BlockSpec((rows, columns), lambda i: (i, 0)),
            pl.BlockSpec((1, rows, 1), lambda i: (i, 0, 0)),
            pl.BlockSpec((1, 1, parts * part), lambda i: (i, 0, 0)),
            *sequence_specs(sequences, part, parts),
        ],
        out_specs=pl.BlockSpec((rows, columns), lambda i: (i, 0)),
        out_shape=jax.ShapeDtypeStruct(queries.shape, BF16),
        compiler_params=kernel_params(),
        cost_estimate=LIGHT,
    )(where, queries, mine, theirs, *own, *came)


def attend_back(where, same, other, w_out, queries, own, came, mine, theirs, cosine, sine):
    parts = len(own)
    sequences, part = own[0].shape[0], 2 * own[0].shape[1]
    length = parts * part
    rows, columns = queries.shape[0] // sequences, queries.shape[1]
    heads, half, width = columns // HEAD_SIZE, sequences // 2, same.shape[1]
    packed = parts, part // 2, 2 * HEAD_SIZE
    scale = HEAD_SIZE**-0.5

    def body(at, s, o, w, q, m, th, cs, sn, *refs):
        dq, down, dcame = refs[-3:]
        first = at[1] == 0
        keys, values = keys_values(first, refs[:-3])
        branch = jnp.where(pl.program_id(0) < half, s[...], o[...])
        mixed = stacked(dot_nt(branch, w[...]).astype(BF16), heads)
        stack = stacked(q[...], heads)
        probs = probabilities(stack, keys, m[0], th[0], at[0], parts, heads)
        grad = dot_nt(mixed, values)
        inner = jnp.sum(probs * grad, axis=-1, keepdims=True)
        scores = (probs * (grad - inner)).astype(BF16)
        grad_q = side_by_side(dot(scores, keys) * scale, heads)
        dq[...] = turn(grad_q, widen(cs[...], columns), -widen(sn[...], columns)).astype(BF16)
        grad_k = dot_tn(scores, stack) * scale
        grad_v = dot_tn(probs.astype(BF16), mixed)
        kept, sent = jnp.where(first, grad_k, grad_v), jnp.where(first, grad_v, grad_k)
        for j in range(parts):
            at_rows = slice(j * part, (j + 1) * part)
            down[0, j] = pack(kept[at_rows])
            dcame[0, j] = pack(sent[at_rows]).astype(BF16)

    def strip(size):
        return pl.BlockSpec((rows, size), lambda i: (i, 0))

    return pl.pallas_call(
        body,
        grid=(sequences,),
        in_specs=[
            pl.BlockSpec(memory_space=pltpu.SMEM),
            pl.BlockSpec((rows, width), lambda i: (jnp.minimum(i, half - 1), 0)),
            pl.BlockSpec((rows, width), lambda i: (jnp.maximum(i - half, 0), 0)),
            pl.BlockSpec(w_out.shape, lambda i: (0, 0)),
            strip(columns),
            pl.BlockSpec((1, rows, 1), lambda i: (i, 0, 0)),
            pl.BlockSpec((1, 1, length), lambda i: (i, 0, 0)),
            strip(cosine.shape[1]),
            strip(cosine.shape[1]),
            *sequence_specs(sequences, part, parts),
        ],
        out_specs=(
            strip(columns),
            pl.BlockSpec((1, *packed), lambda i: (i, 0, 0, 0)),
            pl.BlockSpec((1, *packed), lambda i: (lax.rem(i + half, sequences), 0, 0, 0)),
        ),
        out_shape=(
            jax.ShapeDtypeStruct(queries.shape, BF16),
            jax.ShapeDtypeStruct((sequences, *packed), F32),
            jax.ShapeDtypeStruct((sequences, *packed), BF16),
        ),
        compiler_params=kernel_params(),
        cost_estimate=LIGHT,
    )(where, same, other, w_out, queries, mine, theirs, cosine, sine, *own, *came)


def add_parts(kept, came):
    sequences, parts, rows, columns = kept.shape

    def body(a, b, *outs):
        for j, out in enumerate(outs):
            out[...] = (a[:, j] + b[:, j].astype(F32)).astype(out.dtype)

    return pl.pallas_call(
        body,
        out_shape=[
            jax.ShapeDtypeStruct((sequences, rows, columns), BF16 if j else F32)
            for j in range(parts)
        ],
        compiler_params=kernel_params(),
        cost_estimate=LIGHT,
    )(kept, came)


def sum_keys(where, own, came, cosine, sine):
    sequences, rows, _ = own.shape
    count = len(came)

    def body(at, a, cs, sn, *refs):
        total = a[...]
        for ref in refs[:count]:
            total += ref[...].astype(F32)
        out = refs[count]
        for i in range(sequences):
            at_rows = slice(2 * i * rows, 2 * (i + 1) * rows)
            plain = unpack(total[i])
            turned = turn(plain, cs[at_rows, :HEAD_SIZE], -sn[at_rows, :HEAD_SIZE])
            out[at_rows, :] = jnp.where(at[1] == 0, turned, plain).astype(BF16)

    whole = pl.BlockSpec(memory_space=pltpu.VMEM)
    return pl.pallas_call(
        body,
        in_specs=[pl.BlockSpec(memory_space=pltpu.SMEM)] + [whole] * (3 + count),
        out_shape=jax.ShapeDtypeStruct((2 * sequences * rows, HEAD_SIZE), BF16),
        compiler_params=kernel_params(),
        cost_estimate=LIGHT,
    )(where, own, cosine, sine, *came)


def attention_weight_terms(where, first_in, grad_attn, mixed, grad_branch, used, members, parts):
    tokens, width = first_in.shape
    columns, half = mixed.shape[1], mixed.shape[0] // 2
    block, strip = width // (members * parts), width // members
    upper = members // 2

    def body(at, x, g, m, ba, bb, *refs):
        outs, (left, right) = refs[:parts], refs[parts:]
        left[...] = dot_tn(x[...], g[:, : left.shape[1]])
        right[...] = dot_tn(m[:half, :], ba[...]) + dot_tn(m[half:, :], bb[...])
        for j, out in enumerate(outs):
            place = lax.rem(at[0] + j, parts)
            own = right[pl.ds(pl.multiple_of(place * block, block), block), :]

            def both(d):
                rows = pl.ds(pl.multiple_of((d * parts + place) * block, block), block)
                return [left[rows, :][:, :used], own[:, d * strip : (d + 1) * strip]]

            for d in range(upper):
                out[d * block : (d + 1) * block, :] = jnp.concatenate(
                    both(d) + both(d + upper), axis=1
                ).astype(BF16)

    whole = pl.BlockSpec(memory_space=pltpu.VMEM)
    return pl.pallas_call(
        body,
        in_specs=[pl.BlockSpec(memory_space=pltpu.SMEM)] + [whole] * 5,
        out_shape=[jax.ShapeDtypeStruct((upper * block, 2 * (used + strip)), BF16)] * parts,
        scratch_shapes=[
            pltpu.VMEM((width, grad_attn.shape[1]), F32),
            pltpu.VMEM((columns, width), F32),
        ],
        compiler_params=kernel_params(),
        cost_estimate=LIGHT,
    )(where, first_in, grad_attn, mixed, *grad_branch)


def hidden_units(second_in, w_pair):
    tokens, width = second_in.shape
    ff = w_pair.shape[1] // 2
    tile = 256

    def body(x, w, both, hidden):
        product = dot(x[...], w[...])
        gate, up = product[:, :ff], product[:, ff:]
        both[...] = product.astype(BF16)
        hidden[...] = (gate * jax.nn.sigmoid(gate) * up).astype(BF16)

    def rows(columns):
        return pl.BlockSpec((tile, columns), lambda i: (i, 0))

    return pl.pallas_call(
        body,
        grid=(tokens // tile,),
        in_specs=[rows(width), pl.BlockSpec(w_pair.shape, lambda i: (0, 0), pipeline_mode=pl.Buffered(1))],
        out_specs=(rows(2 * ff), rows(ff)),
        out_shape=(
            jax.ShapeDtypeStruct((tokens, 2 * ff), BF16),
            jax.ShapeDtypeStruct((tokens, ff), BF16),
        ),
        compiler_params=kernel_params(),
        cost_estimate=LIGHT,
    )(second_in, w_pair)


def feed_forward_back(both, hidden, grad_out, w_pair, w_down):
    tokens, width = grad_out.shape
    ff = hidden.shape[1]
    tile = 256

    def body(both, h, dy, w, wd, grads, back, forth):
        gate, up = both[:, :ff].astype(F32), both[:, ff:].astype(F32)
        sig = jax.nn.sigmoid(gate)
        forth[...] = dot(h[...], wd[...]).astype(BF16)
        dh_sig = dot_nt(dy[...], wd[...]) * sig
        grad = jnp.concatenate(
            [dh_sig * up * (1.0 + gate * (1.0 - sig)), dh_sig * gate], axis=1
        ).astype(BF16)
        grads[...] = grad
        back[...] = dot_nt(grad, w[...]).astype(BF16)

    def rows(columns):
        return pl.BlockSpec((tile, columns), lambda i: (i, 0))

    def whole(array):
        return pl.BlockSpec(array.shape, lambda i: (0, 0), pipeline_mode=pl.Buffered(1))

    return pl.pallas_call(
        body,
        grid=(tokens // tile,),
        in_specs=[rows(2 * ff), rows(ff), rows(width), whole(w_pair), whole(w_down)],
        out_specs=(rows(2 * ff), rows(width), rows(width)),
        out_shape=(
            jax.ShapeDtypeStruct((tokens, 2 * ff), BF16),
            jax.ShapeDtypeStruct((tokens, width), BF16),
            jax.ShapeDtypeStruct((tokens, width), BF16),
        ),
        compiler_params=kernel_params(),
        cost_estimate=LIGHT,
    )(both, hidden, grad_out, w_pair, w_down)


def add_blocks(own, came, blocks):
    tokens, columns = own.shape[0] // blocks, own.shape[1]

    def body(a, b, *outs):
        for j, out in enumerate(outs):
            rows = pl.ds(j * tokens, tokens)
            out[...] = (a[rows, :].astype(F32) + b[rows, :].astype(F32)).astype(out.dtype)

    return pl.pallas_call(
        body,
        out_shape=[
            jax.ShapeDtypeStruct((tokens, columns), BF16 if j else F32) for j in range(blocks)
        ],
        compiler_params=kernel_params(),
        cost_estimate=LIGHT,
    )(own, came)


def regroup(values, outer, inner):
    part = values.shape[1] // (outer * inner)
    return jnp.concatenate(
        [
            values[:, (o * inner + i) * part : (o * inner + i + 1) * part]
            for i in range(inner)
            for o in range(outer)
        ],
        axis=1,
    )


def second_norm(x, own, sent, gain, outer, inner):
    count = len(sent)

    def body(x, own, gain, *refs):
        resid = x[...].astype(F32) + own[...]
        for ref in refs[:count]:
            resid += ref[...].astype(F32)
        refs[count][...] = resid
        normed = resid * lax.rsqrt(jnp.mean(resid * resid, axis=-1, keepdims=True) + EPS)
        refs[count + 1][...] = regroup((normed * gain[...]).astype(BF16), outer, inner)

    return pl.pallas_call(
        body,
        out_shape=(
            jax.ShapeDtypeStruct(x.shape, F32),
            jax.ShapeDtypeStruct(x.shape, BF16),
        ),
        compiler_params=kernel_params(),
        cost_estimate=LIGHT,
    )(x, own, gain, *sent)


def second_norm_back(resid, own, sent, gain, grad_out, outer, inner):
    count = len(sent)

    def body(resid, own, gain, grad_out, *refs):
        grad = own[...]
        for ref in refs[:count]:
            grad += ref[...].astype(F32)
        grad = regroup(grad, inner, outer)
        rows = resid[...]
        inverse = lax.rsqrt(jnp.mean(rows * rows, axis=-1, keepdims=True) + EPS)
        total = grad_out[...].astype(F32) + norm_back(grad, rows * inverse, inverse, gain[...])
        refs[count][...] = total
        refs[count + 1][...] = total.astype(BF16)

    return pl.pallas_call(
        body,
        out_shape=(
            jax.ShapeDtypeStruct(resid.shape, F32),
            jax.ShapeDtypeStruct(resid.shape, BF16),
        ),
        compiler_params=kernel_params(),
        cost_estimate=LIGHT,
    )(resid, own, gain, grad_out, *sent)


def dot_blocks(left, right, came, blocks, product):
    tokens, columns = came.shape[0] // blocks, came.shape[1]

    def body(a, b, c, *outs):
        for j, out in enumerate(outs):
            rows = pl.ds(j * tokens, tokens)
            out[...] = (product(a[rows, :], b[...]) + c[rows, :].astype(F32)).astype(out.dtype)

    return pl.pallas_call(
        body,
        out_shape=[
            jax.ShapeDtypeStruct((tokens, columns), BF16 if j else F32) for j in range(blocks)
        ],
        compiler_params=kernel_params(),
        cost_estimate=LIGHT,
    )(left, right, came)


def columns_out(gate, up, planes, members):
    rows, ff = gate.shape
    part = ff // (planes * members)

    def body(g, u, o):
        both = g[...], u[...]
        for s in range(members):
            o[s] = jnp.concatenate(
                [
                    v[:, (p * members + s) * part : (p * members + s + 1) * part]
                    for v in both
                    for p in range(planes)
                ],
                axis=1,
            )

    return pl.pallas_call(
        body,
        out_shape=jax.ShapeDtypeStruct((members, rows, 2 * planes * part), gate.dtype),
        compiler_params=kernel_params(),
        cost_estimate=LIGHT,
    )(gate, up)


def sum_terms(*terms):
    def body(*refs):
        refs[-1][...] = sum(ref[...].astype(F32) for ref in refs[:-1])

    return pl.pallas_call(
        body,
        out_shape=jax.ShapeDtypeStruct(terms[0].shape, F32),
        compiler_params=kernel_params(),
        cost_estimate=LIGHT,
    )(*terms)


def gather_terms(own, sums, members, used, width):
    block, count, strip = 2 * own.shape[0] // members, len(sums), width // members

    def body(a, *refs):
        total = a[...].astype(F32)
        for ref in refs[:count]:
            total += ref[...].astype(F32)
        out, payload = refs[count:]
        strips = []
        for d in range(members):
            side, row = divmod(d, members // 2)
            start = side * (used + strip)
            rows = total[row * block : (row + 1) * block]
            payload[d] = rows[:, start : start + used].astype(BF16)
            strips.append(rows[:, start + used : start + used + strip])
        out[...] = jnp.concatenate(strips, axis=1)

    return pl.pallas_call(
        body,
        out_shape=(
            jax.ShapeDtypeStruct((block, width), F32),
            jax.ShapeDtypeStruct((members, block, used), BF16),
        ),
        compiler_params=kernel_params(),
        cost_estimate=LIGHT,
    )(own, *sums)


def weight_gradients(pairs, blocks, weights, gains, q_cols):
    members, rows, _ = blocks.shape
    part, shared = pairs.shape[2] // 2, members // (2 * KEY_VALUE_HEADS)

    def body(pair, x, g, u, q, k, v, gains, og, ou, oq, ok, ov, ogain):
        def side(start, size, chosen, x=x):
            return [x[d, :, start : start + size].astype(F32) for d in chosen]

        def heads(core):
            found = side(q_cols, HEAD_SIZE, range(core, members, 2))
            return jnp.concatenate(
                [sum(found[h * shared : (h + 1) * shared]) for h in range(KEY_VALUE_HEADS)], axis=1
            )

        og[...] = jnp.concatenate(side(0, part, range(members), pair), axis=1)
        ou[...] = jnp.concatenate(side(part, part, range(members), pair), axis=1)
        oq[...] = jnp.concatenate(side(0, q_cols, range(members)), axis=1)
        ok[...] = heads(0)
        ov[...] = heads(1)

        def gain(both):
            return sum(jnp.sum(w[...].astype(F32) * o[...], axis=1, keepdims=True) for w, o in both)

        total = jnp.concatenate([gain(((q, oq), (k, ok), (v, ov))), gain(((g, og), (u, ou)))], axis=1)
        ogain[...] = total / gains[...].astype(F32)

    return pl.pallas_call(
        body,
        out_shape=[jax.ShapeDtypeStruct(w.shape, F32) for w in weights]
        + [jax.ShapeDtypeStruct((rows, 2), F32)],
        compiler_params=kernel_params(),
        cost_estimate=LIGHT,
    )(pairs, blocks, *weights, gains)


def stack_rows(parts):
    rows, columns = parts[0].shape

    def body(*refs):
        for j, ref in enumerate(refs[:-1]):
            refs[-1][j * rows : (j + 1) * rows, :] = ref[...]

    return pl.pallas_call(
        body,
        out_shape=jax.ShapeDtypeStruct((len(parts) * rows, columns), parts[0].dtype),
        compiler_params=kernel_params(),
        cost_estimate=LIGHT,
    )(*parts)


def scatter_dp(left, right, size, product):
    came = swap(product(left[left.shape[0] // 2 :], right).astype(BF16), 1)
    return dot_blocks(left, right, came, size // 2, product)


def in_order(parts, place):
    size = len(parts)
    rows, columns = parts[0].shape

    def body(at, *refs):
        for j in range(size):
            refs[-1][pl.ds(lax.rem(at[0] + j, size), 1)] = refs[j][...][None]

    out = pl.pallas_call(
        body,
        in_specs=[pl.BlockSpec(memory_space=pltpu.SMEM)]
        + [pl.BlockSpec(memory_space=pltpu.VMEM)] * size,
        out_shape=jax.ShapeDtypeStruct((size, rows, columns), parts[0].dtype),
        compiler_params=kernel_params(),
        cost_estimate=LIGHT,
    )(jnp.full((1,), place, jnp.int32), *parts)
    return out.reshape(size * rows, columns)


def attention_weights(parts, place, at_gains):
    size = len(parts)
    a, b, m = parts[0].shape
    lanes = at_gains // 128 * 128

    def body(at, *refs):
        out, gains = refs[-2:]
        for j in range(size):
            out[:, pl.ds(lax.rem(at[0] + j, size), 1)] = refs[j][...][:, None]
        strip = out[:, :, :, lanes : lanes + 128].reshape(a * size * b, 128).astype(F32)
        gains[...] = strip.T[at_gains - lanes : at_gains - lanes + 2]

    return pl.pallas_call(
        body,
        in_specs=[pl.BlockSpec(memory_space=pltpu.SMEM)]
        + [pl.BlockSpec(memory_space=pltpu.VMEM)] * size,
        out_shape=(
            jax.ShapeDtypeStruct((a, size, b, m), parts[0].dtype),
            jax.ShapeDtypeStruct((2, a * size * b), F32),
        ),
        compiler_params=kernel_params(),
        cost_estimate=LIGHT,
    )(jnp.full((1,), place, jnp.int32), *parts)


def norm_back(grad_in, normed, inverse, gain):
    grad_normed = grad_in * gain
    return inverse * (
        grad_normed - normed * jnp.mean(grad_normed * normed, axis=-1, keepdims=True)
    )


def per_device(
    n,
    c,
    tokens,
    segment_ids,
    out_grad,
    gain_attn,
    w_query,
    key_weight,
    value_weight,
    w_out,
    gain_mlp,
    w_gate,
    w_up,
    w_down,
):
    t, width = tokens.shape[1:]
    length = segment_ids.shape[1]
    block = w_query.shape[0]
    ff = w_gate.shape[1]
    heads = QUERY_HEADS // n
    group = QUERY_HEADS // KEY_VALUE_HEADS
    q_cols, f_cols = heads * HEAD_SIZE, ff // n
    every_dp = ("plane", "core")
    plane, core, place_z = (lax.axis_index(axis) for axis in ("plane", "core", "ctx"))
    me = 2 * plane + core

    pieces = []
    used = q_cols + HEAD_SIZE
    extras = jnp.concatenate(
        [gain_attn[:, None], gain_mlp[:, None], segment_ids.astype(BF16).reshape(block, -1)], axis=1
    )
    extras = jnp.pad(extras, ((0, 0), (0, -(used + extras.shape[1]) % 128)))
    for d in range(n):
        g = d * heads // group
        kv = value_weight if d % 2 else key_weight
        pieces += [
            w_query[:, d * q_cols : (d + 1) * q_cols],
            kv[:, g * HEAD_SIZE : (g + 1) * HEAD_SIZE],
            extras,
        ]
    w_attn = jnp.concatenate(pieces, axis=1).reshape(block, n, -1).transpose(1, 0, 2)
    w_attn = lax.all_to_all(w_attn, every_dp, 0, 0)
    x16, dy_local = tokens[0], out_grad[0]
    wd = lax.all_gather(w_down, "ctx", axis=0, tiled=True)
    w_attn, wo_parts, same = together(w_attn, shifts(w_out, c), dp_same(x16, n))
    seg_rows = w_attn[:, :, used + 2 : used + 2 + length // block].reshape(n, length)

    order = me ^ jnp.array([*range(0, n, 2), *range(1, n, 2)], jnp.int32)
    pick = (order[:, None] == jnp.arange(n, dtype=jnp.int32)[None]).astype(BF16)
    segs = dot(pick, seg_rows)
    local_idx = place_z * t + jnp.arange(t, dtype=jnp.int32)
    local_seg = lax.dynamic_slice_in_dim(segs, place_z * t, t, axis=1)
    before = jnp.sum((segs[:, None, :] < local_seg[:, :, None]).astype(jnp.int32), axis=2)
    place = (local_idx[None] - before).astype(F32)
    freq = 10000.0 ** (-jnp.arange(HEAD_SIZE // 2, dtype=F32) / (HEAD_SIZE // 2))
    angle = place.reshape(n * t)[:, None] * freq[None, :]
    cosine, sine = jnp.cos(angle), jnp.sin(angle)
    cosine = jnp.concatenate([cosine] * 4, axis=1)
    sine = jnp.concatenate([-sine, sine] * 2, axis=1)
    w_pair = columns_out(*after((w_gate, w_up), w_attn), 1, n)
    w_pair = lax.all_to_all(w_pair, every_dp, 0, 0).reshape(n * block, 2 * f_cols)
    even = jnp.concatenate([x16, *same])
    odd = swap(even, 1)
    wo = in_order([w_out, *wo_parts], place_z)
    w_parts, cosine, sine, w_pair, wd, wo = together(
        shifts(w_attn, c), cosine, sine, w_pair, wd, wo
    )
    w_pair = lax.all_gather(w_pair, "ctx", axis=0, tiled=True)

    w_attn, gains = attention_weights([w_attn, *w_parts], place_z, used)
    w_attn = w_attn.reshape(width, -1)
    gain1, gain2 = gains[:1], gains[1:]
    where = jnp.stack([place_z, core]).astype(jnp.int32)
    key_seg = lax.dynamic_slice_in_dim(
        jnp.concatenate([segs, segs], axis=1), place_z * t, length, axis=1
    )
    sides = local_seg[:, :, None], key_seg[:, None, :]

    first_in, queries, kv_own = project(where, even, odd, gain1, w_attn, cosine, sine, q_cols, t)

    kv_parts, dy_same = together(shifts(kv_own, c), dp_same(after(dy_local, first_in), n))
    dy_same = jnp.concatenate([dy_local, *dy_same])
    dy = dy_same, swap(dy_same, 1)
    kv_all = [kv_own, *kv_parts]
    kv_other = [swap(v, 1) for v in kv_all]
    mixed = attend(where, queries, kv_all, kv_other, *sides)
    attn_own, *sends = scatter_dp(mixed, wo, n, dot)
    sent = together(*[swap(v, 2 * j) for j, v in enumerate(sends, 1)])
    resid, second_in = second_norm(x16, attn_own, sent, gain2, n, c)

    second_in = stack_rows([second_in, *together(*dp_same(second_in, n))])
    second_in = second_in, swap(second_in, 1)
    units = hidden_units(second_in[0], w_pair)
    units = units, hidden_units(after(second_in[1], units), w_pair)
    hidden = [half[1] for half in units]
    down_term = transposed_dot(hidden, dy)
    grad_down = lax.psum_scatter(after(down_term, wd), "ctx", scatter_dimension=0, tiled=True)
    other = feed_forward_back(*units[1], dy[1], w_pair, after(wd, down_term))
    same = feed_forward_back(*units[0], after(dy[0], other[0]), w_pair, wd)
    grad_pair = same[0], other[0]
    back, *sends = add_blocks(same[1], swap(other[1], 1), n // 2)
    forth = swap(after(other[2], sends), 1)
    pair_term = transposed_dot(after(second_in, forth), grad_pair)
    forth, *forth_sends = add_blocks(same[2], forth, n // 2)
    sent, pair_term, forth_sends, grad_down = together(
        [swap(v, 2 * j) for j, v in enumerate(sends, 1)], pair_term, forth_sends, grad_down
    )
    pair_sum = lax.psum_scatter(pair_term, "ctx", scatter_dimension=0, tiled=True)
    grad_resid, branch = second_norm_back(resid, back, sent, gain2, dy_local, n, c)

    same = together(*dp_same(branch, n))
    same = stack_rows([branch, *same])
    grad_branch = same, swap(same, 1)
    grad_q, kept, sent = attend_back(
        where, *grad_branch, wo, queries, kv_all, kv_other, *sides, cosine, sine
    )
    result_parts = [swap(v, 2 * j) for j, v in enumerate(forth_sends, 1)]
    kept, sent, result_parts = together(kept, sent, result_parts)
    own_kv, *kv_sends = add_parts(kept, swap(sent, 1))
    kv_parts = together(*[shift(v, -j, c) for j, v in enumerate(kv_sends, 1)])
    result = resid + forth + sum(v.astype(F32) for v in result_parts)
    grad_kv = sum_keys(where, own_kv, kv_parts, cosine, sine)
    unused = jnp.zeros((n * t, w_attn.shape[1] - used), BF16)
    grad_attn = jnp.concatenate([grad_q, grad_kv, unused], axis=1)
    own_terms, *terms = attention_weight_terms(
        where, first_in, grad_attn, mixed, grad_branch, used, n, c
    )
    first_own, *sends = scatter_dp(after(grad_attn, terms), w_attn, n, dot_nt)
    sent, near, last, far = together(
        [swap(v, 2 * j) for j, v in enumerate(sends, 1)],
        shift(terms[0], -1, c),
        shift(terms[-1], 1, c),
        terms[1:-1],
    )
    pair_sum = after(pair_sum, near)
    far, pair_sum = together(
        [shift(v, -j, c) for j, v in enumerate(far, 2)],
        lax.all_to_all(pair_sum.reshape(n, block, 2 * f_cols), every_dp, 0, 0),
    )
    own_terms, terms = sum_terms(own_terms, near, last), far
    grad_wout, payload = gather_terms(own_terms, terms, n, used, width)
    payload = lax.all_to_all(payload, every_dp, 0, 0)
    grad_gate, grad_up, grad_query, grad_key, grad_value, grad_gains = weight_gradients(
        pair_sum,
        payload,
        (w_gate, w_up, w_query, key_weight, value_weight),
        jnp.stack([gain_attn, gain_mlp], axis=1),
        q_cols,
    )
    grad_first = first_own + sum(v.astype(F32) for v in sent)
    grad_down = after(grad_down, terms).astype(F32)
    x = x16.astype(F32)
    inverse1 = lax.rsqrt(jnp.mean(x * x, axis=-1, keepdims=True) + EPS)
    grad_input = grad_resid + norm_back(grad_first, x * inverse1, inverse1, gain1)
    return (
        result.astype(BF16)[None],
        grad_input[None],
        grad_gains[:, 0],
        grad_query,
        grad_key,
        grad_value,
        grad_wout,
        grad_gains[:, 1],
        grad_gate,
        grad_up,
        grad_down,
    )


def solution(mesh):
    n, c = mesh.shape["dp"], mesh.shape["ctx"]
    split = Mesh(mesh.devices.reshape(n // 2, 2, c), ("plane", "core", "ctx"))
    dp, every = ("plane", "core"), ("plane", "core", "ctx")
    rows = P(dp, "ctx", None)
    weight, gain = P(every, None), P(every)
    return jax.shard_map(
        functools.partial(per_device, n, c),
        mesh=split,
        in_specs=(rows, P(dp, None), rows, gain, weight, weight, weight, weight, gain)
        + (weight,) * 3,
        out_specs=(rows, rows, gain, weight, weight, weight, weight, gain) + (weight,) * 3,
        check_vma=False,
    )
```
